128 devices in a mesh: band: 8 (over y, core), tile: 16 (over x, z).
Axes of the slice: x: 4, y: 4, z: 4, core: 2. Of those that a mesh axis runs over, the one named last changes fastest.
Arguments:
- wind_east: float32 [16, 1024, 1024], P(None, 'tile', 'band'), may hold values from -2.5 to 2.5
- wind_north: float32 [16, 1024, 1024], P(None, 'tile', 'band'), may hold values from -2.5 to 2.5
- theta_pert: float32 [16, 1024, 1024], P(None, 'tile', 'band'), may hold values from -6 to 6
- tke_field: float32 [16, 1024, 1024], P(None, 'tile', 'band'), may hold values from 0.1 to 1
- target_east: float32 [16, 1024, 1024], P(None, 'tile', 'band'), may hold values from -2.5 to 2.5
- target_north: float32 [16, 1024, 1024], P(None, 'tile', 'band'), may hold values from -2.5 to 2.5
- target_theta: float32 [16, 1024, 1024], P(None, 'tile', 'band'), may hold values from -6 to 6
- turbine_count: int32 [1024, 1024], P('tile', 'band'), may hold values from 0 to 3
- turbine_type: int32 [1024, 1024], P('tile', 'band'), may hold values from 0 to 7
- drag_coeff: float32 [8, 16], replicated, may hold values from 0.005 to 0.05
- tke_coeff: float32 [8, 16], replicated, may hold values from 0.01 to 0.1
- cutoffs: int32 [2, 16], replicated, may hold values from 1 to 64
Outputs:
- east_out: float32 [16, 1024, 1024], P(None, 'tile', 'band')
- north_out: float32 [16, 1024, 1024], P(None, 'tile', 'band')
- theta_out: float32 [16, 1024, 1024], P(None, 'tile', 'band')
- tke_out: float32 [16, 1024, 1024], P(None, 'tile', 'band')
The draws below stay inside these ranges and needn't reach their ends.
All inputs are finite; a program needn't handle non-finite values.
Results may differ from the reference program's by a relative error of at most 0.000082.
Values sent between devices are 32-bit elements; how exact they have to be, the bound alone decides.
A program may use at most 192 MiB of HBM per device.

```python
import math
import jax
import jax.numpy as jnp
from jax import lax

LEV = 16
KMAX = 64
NTYPE = 8
NX = 1024
NY = 1024


def plant(values, rng, smallest, largest):
    index_at = [jax.random.randint(jax.random.fold_in(rng, axis), (), 0, length) for axis, length in enumerate(values.shape)]
    main_axis = values.shape.index(max(values.shape))
    neighbour = index_at[:main_axis] + [(index_at[main_axis] + 1) % values.shape[main_axis]] + index_at[main_axis + 1:]
    return values.at[tuple(index_at)].set(smallest).at[tuple(neighbour)].set(largest)


def level_of(rng, shape, pieces, smallest, high):
    factor_of = 1.0
    for position, blocks in pieces:
        steps = jax.random.uniform(jax.random.fold_in(jax.random.fold_in(rng, 6), position), (blocks,), jnp.float32, smallest / len(pieces), high / len(pieces))
        factor_of = factor_of * jnp.repeat(jnp.exp(steps), shape[position] // blocks).reshape((-1,) + (1,) * (len(shape) - 1 - position))
    return factor_of


def gaussian(own_key, shape, width, bound, pieces=(), held_as=jnp.bfloat16):
    drawn = width * jax.random.normal(own_key, shape, jnp.float32)
    if pieces:
        drawn = drawn * level_of(own_key, shape, pieces, -0.22, 0.18)
    return jnp.clip(drawn, -bound, bound).astype(held_as)


def setup_inputs(seed: int = 0) -> dict:
    key_list = jax.random.split(jax.random.key(seed), 13)
    return {
        "wind_east": gaussian(key_list[0], (LEV, NX, NY), 0.35, 2.5, ((1, 16), (2, 8)), jnp.float32),
        "wind_north": gaussian(key_list[1], (LEV, NX, NY), 0.35, 2.5, ((1, 16), (2, 8)), jnp.float32),
        "theta_pert": gaussian(key_list[2], (LEV, NX, NY), 1.0, 6.0, ((1, 16), (2, 8)), jnp.float32),
        "tke_field": jnp.clip(0.1 + 0.9 * jax.random.uniform(key_list[3], (LEV, NX, NY), jnp.float32) ** level_of(key_list[3], (LEV, NX, NY), ((1, 16), (2, 8)), -0.2, 0.2), 0.1, 1.0),
        "target_east": gaussian(key_list[4], (LEV, NX, NY), 0.35, 2.5, ((1, 16), (2, 8)), jnp.float32),
        "target_north": gaussian(key_list[5], (LEV, NX, NY), 0.35, 2.5, ((1, 16), (2, 8)), jnp.float32),
        "target_theta": gaussian(key_list[6], (LEV, NX, NY), 1.0, 6.0, ((1, 16), (2, 8)), jnp.float32),
        "turbine_count": plant(jax.random.randint(key_list[7], (NX, NY), 0, 4), jax.random.fold_in(key_list[7], 1), 0, 3).astype(jnp.int32),
        "turbine_type": plant(jax.random.randint(key_list[8], (NX, NY), 0, NTYPE), jax.random.fold_in(key_list[8], 1), 0, NTYPE - 1).astype(jnp.int32),
        "drag_coeff": jnp.clip(jnp.exp(jax.random.uniform(key_list[9], (NTYPE, LEV), jnp.float32, math.log(0.005), math.log(0.05))), 0.005, 0.05),
        "tke_coeff": jnp.clip(jnp.exp(jax.random.uniform(key_list[10], (NTYPE, LEV), jnp.float32, math.log(0.01), math.log(0.1))), 0.01, 0.1),
        "cutoffs": plant(jax.random.randint(key_list[11], (2, LEV), 1, KMAX + 1), jax.random.fold_in(key_list[11], 1), 1, KMAX).astype(jnp.int32),
    }


nudge_gain = 0.5
highest = lax.Precision.HIGHEST
section_fractions = (1.0 / 3.0, 0.5, 1.0)

def mode_numbers():
    mode_index = jnp.arange(2 * KMAX, dtype=jnp.int32)
    return (mode_index, jnp.where(mode_index < KMAX, mode_index, mode_index - KMAX + 1))

def tables(anchor, number, extent):
    positions = anchor + jnp.arange(number, dtype=jnp.int32)
    mode_index, wavenumber = mode_numbers()
    phase_int = wavenumber[:, None] * positions[None, :] % extent
    angles = phase_int.astype(jnp.float32) * (2.0 * math.pi / extent)
    basis_rows = jnp.where((mode_index < KMAX)[:, None], jnp.cos(angles), jnp.sin(angles))
    weights = jnp.where(wavenumber == 0, 1.0 / extent, 2.0 / extent).astype(jnp.float32)
    return (basis_rows * weights[:, None], basis_rows)

def level_mask(cut_rows):
    mode_index, wavenumber = mode_numbers()
    keep_east = wavenumber[None, :, None] <= cut_rows[0][:, None, None]
    keep_north = wavenumber[None, None, :] <= cut_rows[1][:, None, None]
    return jnp.logical_and(keep_east, keep_north).astype(jnp.float32)

def analyze(departure, forward_east, forward_north):
    partial_rows = jnp.einsum('flxy,my->flxm', departure, forward_north, precision=highest)
    return jnp.einsum('flxm,kx->flkm', partial_rows, forward_east, precision=highest)

def synthesize(spectra, back_east, back_north):
    partial_rows = jnp.einsum('flkm,my->flky', spectra, back_north, precision=highest)
    return jnp.einsum('flky,kx->flxy', partial_rows, back_east, precision=highest)

def stencil(padded, offset, dimension):
    length = padded.shape[dimension] - 6
    return lax.slice_in_dim(padded, 3 + offset, 3 + offset + length, axis=dimension)

def differences(padded, dimension):
    centre = stencil(padded, 0, dimension)
    ahead_one = stencil(padded, 1, dimension)
    behind_one = stencil(padded, -1, dimension)
    ahead_two = stencil(padded, 2, dimension)
    behind_two = stencil(padded, -2, dimension)
    ahead_three = stencil(padded, 3, dimension)
    behind_three = stencil(padded, -3, dimension)
    central = (45.0 * (ahead_one - behind_one) - 9.0 * (ahead_two - behind_two) + (ahead_three - behind_three)) / 60.0
    smoothing = (ahead_three + behind_three - 6.0 * (ahead_two + behind_two) + 15.0 * (ahead_one + behind_one) - 20.0 * centre) / 60.0
    return (central, smoothing)

def advect(padded):
    interior = padded[:, :, 3:-3, 3:-3]
    east_speed = interior[0]
    north_speed = interior[1]
    central_east, smooth_east = differences(padded[:, :, :, 3:-3], 2)
    central_north, smooth_north = differences(padded[:, :, 3:-3, :], 3)
    return -(east_speed * central_east - jnp.abs(east_speed) * smooth_east) - (north_speed * central_north - jnp.abs(north_speed) * smooth_north)

def fitch(wind_east, wind_north, tke_field, turbine_count, turbine_type, drag_coeff, tke_coeff):
    type_ids = jnp.arange(NTYPE, dtype=jnp.int32)
    onehot = (turbine_type[None, :, :] == type_ids[:, None, None]).astype(jnp.float32)
    drag_cell = jnp.einsum('tl,txy->lxy', drag_coeff, onehot, precision=highest)
    tke_cell = jnp.einsum('tl,txy->lxy', tke_coeff, onehot, precision=highest)
    speeds = jnp.sqrt(wind_east * wind_east + wind_north * wind_north)
    counts = turbine_count.astype(jnp.float32)[None, :, :]
    drag_rate = counts * drag_cell * speeds
    tke_out = tke_field + counts * tke_cell * speeds * speeds * speeds
    return (drag_rate, tke_out)

def forcing_from(smooth_part, drag_rate, wind_east, wind_north):
    return nudge_gain * smooth_part - jnp.stack([drag_rate * wind_east, drag_rate * wind_north, jnp.zeros_like(wind_east)])

def reference(wind_east, wind_north, theta_pert, tke_field, target_east, target_north, target_theta, turbine_count, turbine_type, drag_coeff, tke_coeff, cutoffs):
    drag_rate, tke_out = fitch(wind_east, wind_north, tke_field, turbine_count, turbine_type, drag_coeff, tke_coeff)
    initial = jnp.stack([wind_east, wind_north, theta_pert])
    departure = jnp.stack([target_east, target_north, target_theta]) - initial
    forward_east, back_east = tables(0, NX, NX)
    forward_north, back_north = tables(0, NY, NY)
    spectra = analyze(departure, forward_east, forward_north) * level_mask(cutoffs)
    smooth_part = synthesize(spectra, back_east, back_north)
    forcing = forcing_from(smooth_part, drag_rate, wind_east, wind_north)
    current = initial
    for fraction in section_fractions:
        padded = jnp.pad(current, ((0, 0), (0, 0), (3, 3), (3, 3)))
        current = initial + fraction * (advect(padded) + forcing)
    return (current[0], current[1], current[2], tke_out)
```

```python
import functools

import jax
import jax.numpy as jnp
import ml_dtypes
import numpy as np
from jax import lax
from jax.experimental import pallas as pl
from jax.experimental.pallas import tpu as pltpu
from jax.sharding import PartitionSpec as P

KMAX = 64
MODES = 2 * KMAX
NTYPE = 8
LEV = 16
FIELDS = 3
BANDS = 8
TILES = 16
NX = 64
NY = 128
RX = 21
RY = 32
PLANES = 6
GROUPS = 4
GLEV = LEV // GROUPS
SLOTS = FIELDS * GLEV
PER = 6
PAD = 8
MESH = pl.DeviceIdType.MESH
BF = jnp.bfloat16
F32 = jnp.float32


def wavenumbers():
    index = np.arange(MODES)
    return np.where(index < KMAX, index, index - KMAX + 1)


def basis(extent, positions):
    number = wavenumbers()
    angle = 2 * np.pi * ((number[:, None] * positions[None, :]) % extent) / extent
    return np.where((np.arange(MODES) < KMAX)[:, None], np.cos(angle), np.sin(angle))


def window(length, extent, rank):
    index = np.arange(length)
    half = (KMAX + 0.5) / extent
    diagonal = ((length - 1 - 2 * index) / 2) ** 2 * np.cos(2 * np.pi * half)
    beside = index[1:] * (length - index[1:]) / 2
    _, vectors = np.linalg.eigh(np.diag(diagonal) + np.diag(beside, 1) + np.diag(beside, -1))
    vectors = vectors[:, ::-1][:, :rank]
    largest = vectors[np.argmax(np.abs(vectors) > 0.02, axis=0), np.arange(rank)]
    return vectors * np.sign(largest)


def halves(table):
    high = table.astype(np.float32).astype(ml_dtypes.bfloat16)
    low = (table - high.astype(np.float64)).astype(np.float32).astype(ml_dtypes.bfloat16)
    return high, low


def stencil_table():
    central = {1: 45.0, -1: -45.0, 2: -9.0, -2: 9.0, 3: 1.0, -3: -1.0}
    smooth = {3: 1.0, -3: 1.0, 2: -6.0, -2: -6.0, 1: 15.0, -1: 15.0, 0: -20.0}
    inner = np.zeros((NY, 2 * NY))
    outer = np.zeros((NY, 2 * NY))
    for column, taps in ((0, central), (NY, smooth)):
        for y in range(NY):
            for offset, tap in taps.items():
                at = y + offset
                if 0 <= at < NY:
                    inner[at, column + y] = tap
                elif at < 0:
                    outer[at + 3, column + y] = tap
                else:
                    outer[at - NY + 3, column + y] = tap
    return np.concatenate([inner, inner, outer, outer]).astype(ml_dtypes.bfloat16)


def make_tables():
    east_n, north_n = NX * TILES, NY * BANDS
    vx = window(NX, east_n, RX)
    vy = window(NY, north_n, RY)
    ux = [basis(east_n, NX * t + np.arange(NX)) @ vx for t in range(TILES)]
    uy = [basis(north_n, NY * b + np.arange(NY)) @ vy for b in range(BANDS)]

    block = np.zeros((PLANES * NX, 128))
    for p in range(PLANES):
        block[p * NX : (p + 1) * NX, p * RX : (p + 1) * RX] = vx
    high, low = halves(block.T)
    x_forward = np.concatenate([high, low], axis=0)
    high, low = halves(0.5 * block)
    x_back = np.concatenate([high, high, low], axis=1)

    high, low = halves(vy.T)
    y_forward = np.concatenate(
        [np.concatenate([high, high], axis=1), np.concatenate([low, 0 * low], axis=1)], axis=0
    )
    diag = np.zeros((4 * RY, 4 * NY))
    for g in range(4):
        diag[g * RY : (g + 1) * RY, g * NY : (g + 1) * NY] = vy.T
    y_back = np.concatenate(halves(diag), axis=1)

    uy_all = np.concatenate(uy, axis=1)
    m_forward = np.concatenate(halves(uy_all), axis=0)
    m_back = np.concatenate(halves(uy_all.T), axis=0)

    ux_all = np.zeros((MODES, 384))
    for t in range(TILES):
        at = 128 * (t // PER) + RX * (t % PER)
        ux_all[:, at : at + RX] = ux[t]
    k_forward = np.concatenate(halves(ux_all.T), axis=1)
    k_back = np.concatenate(halves(ux_all), axis=1)

    number = wavenumbers()
    weight_k = np.where(number == 0, 1.0, 2.0) / east_n
    weight_m = np.where(number == 0, 1.0, 2.0) / north_n
    weights = (weight_m[:, None] * weight_k[None, :]).astype(np.float32)
    number_k = np.broadcast_to(number[None, :], (8, MODES)).astype(np.int32)
    number_m = np.broadcast_to(number[:, None], (MODES, MODES)).astype(np.int32)
    return (
        x_forward,
        y_forward,
        m_forward,
        k_forward,
        k_back,
        m_back,
        y_back,
        x_back,
        stencil_table(),
        weights,
        number_k,
        number_m,
    )


def split(value):
    high = value.astype(BF)
    low = (value - high.astype(F32)).astype(BF)
    return high, low


def dot(a, b):
    return lax.dot_general(a, b, (((1,), (0,)), ((), ())), preferred_element_type=F32)


def quarters(product, rows, columns):
    return (product[:rows, :columns] + product[:rows, columns:]) + (
        product[rows:, :columns] + product[rows:, columns:]
    )


def kernel(
    wind_east,
    wind_north,
    theta_pert,
    tke_field,
    target_east,
    target_north,
    target_theta,
    turbine_count,
    turbine_type,
    drag_coeff,
    tke_coeff,
    cutoffs,
    x_forward,
    y_forward,
    m_forward,
    k_forward,
    k_back,
    m_back,
    y_back,
    x_back,
    stencil,
    weights,
    number_k,
    number_m,
    east_out,
    north_out,
    theta_out,
    tke_out,
    q0,
    q1,
    q2,
    target,
    tke,
    count,
    kind,
    partial,
    drag,
    force,
    result,
    diffs,
    y_halo,
    xs,
    xr,
    ys,
    yr,
    s1,
    r1,
    s2,
    r2,
    s3,
    r3,
    s4,
    r4,
    modes,
    in_sem,
    out_sem,
    xs_sem,
    xr_sem,
    ys_sem,
    yr_sem,
    s1_sem,
    r1_sem,
    s2_sem,
    r2_sem,
    s3_sem,
    r3_sem,
    s4_sem,
    r4_sem,
):
    band = lax.axis_index("band")
    tile = lax.axis_index("tile")

    inputs = []
    for f, source in enumerate((wind_east, wind_north, theta_pert)):
        inputs.append((source, q0.at[pl.ds(f * LEV, LEV), pl.ds(PAD, NX), :]))
    for f, source in enumerate((target_east, target_north, target_theta)):
        inputs.append((source, target.at[pl.ds(f * LEV, LEV)]))
    inputs += [(tke_field, tke), (turbine_count, count), (turbine_type, kind)]
    inputs = [
        pltpu.make_async_copy(source, into, in_sem.at[i])
        for i, (source, into) in enumerate(inputs)
    ]
    for copy in inputs:
        copy.start()

    @pl.when(tile == 0)
    def _():
        xr[:, 0] = jnp.zeros((3, GROUPS, SLOTS, 4, 128), F32)

    @pl.when(tile == TILES - 1)
    def _():
        xr[:, 1] = jnp.zeros((3, GROUPS, SLOTS, 4, 128), F32)

    @pl.when(band == 0)
    def _():
        yr[:, 0] = jnp.zeros((3, GROUPS, NX, 128), F32)

    @pl.when(band == BANDS - 1)
    def _():
        yr[:, 1] = jnp.zeros((3, GROUPS, NX, 128), F32)

    barrier = pltpu.get_barrier_semaphore()
    for step in range(1, BANDS):
        pl.semaphore_signal(
            barrier, inc=1, device_id={"band": lax.rem(band + step, BANDS)}, device_id_type=MESH
        )
    for step in range(1, TILES):
        pl.semaphore_signal(
            barrier, inc=1, device_id={"tile": lax.rem(tile + step, TILES)}, device_id_type=MESH
        )

    lane = lax.broadcasted_iota(jnp.int32, (NX, 128), 1)
    low_lane = lax.rem(lane, 6) < 3


    def pack_edges(turn, group, slot, plane):
        xs[turn, 0, group, slot, 0:3, :] = plane[0:3]
        xs[turn, 1, group, slot, 0:3, :] = plane[NX - 3 : NX]
        first = slot * 6
        mine = jnp.logical_and(lane >= first, lane < first + 6)
        moved = pltpu.roll(plane, first + 3, 1)
        before = jnp.where(slot == 0, jnp.zeros((NX, 128), F32), ys[turn, group])
        ys[turn, group] = jnp.where(mine, moved, before)

    def x_copy(turn, group, side):
        return pltpu.make_async_remote_copy(
            src_ref=xs.at[turn, side, group],
            dst_ref=xr.at[turn, 1 - side, group],
            send_sem=xs_sem.at[turn, side, group],
            recv_sem=xr_sem.at[turn, 1 - side, group],
            device_id={"tile": tile + (1 if side else -1)},
            device_id_type=MESH,
        )

    def y_copy(turn, group, side):
        return pltpu.make_async_remote_copy(
            src_ref=ys.at[turn, group],
            dst_ref=yr.at[turn, 1 - side, group],
            send_sem=ys_sem.at[turn, side, group],
            recv_sem=yr_sem.at[turn, 1 - side, group],
            device_id={"band": band + (1 if side else -1)},
            device_id_type=MESH,
        )

    has = (
        (tile > 0, band > 0),
        (tile < TILES - 1, band < BANDS - 1),
    )

    def send_edges(turn, group):
        for side in range(2):

            @pl.when(has[side][0])
            def _():
                x_copy(turn, group, side).start()

            @pl.when(has[side][1])
            def _():
                y_copy(turn, group, side).start()

    def await_edges(turn, group):
        for side in range(2):

            @pl.when(has[side][0])
            def _():
                x_copy(turn, group, 1 - side).wait_recv()

            @pl.when(has[side][1])
            def _():
                y_copy(turn, group, 1 - side).wait_recv()

        y_halo[...] = jnp.where(low_lane, yr[turn, 0, group], yr[turn, 1, group])

    def edges_sent(turn, group):
        for side in range(2):

            @pl.when(has[side][0])
            def _():
                x_copy(turn, group, side).wait_send()

            @pl.when(has[side][1])
            def _():
                y_copy(turn, group, side).wait_send()


    def advance(turn, group, source, finish):
        @pl.loop(0, GLEV)
        def _(inner):
            level = group * GLEV + inner
            rows = []
            for f in range(FIELDS):
                slot = f * GLEV + inner
                plane = f * LEV + level
                source[plane, PAD - 3 : PAD, :] = xr[turn, 0, group, slot, 0:3, :]
                source[plane, PAD + NX : PAD + NX + 3, :] = xr[turn, 1, group, slot, 0:3, :]
                high, low = split(source[plane, PAD : PAD + NX, :])
                halo_high, halo_low = split(pltpu.roll(y_halo[...], 128 - slot * 6, 1))
                rows.append(jnp.concatenate([high, low, halo_high, halo_low], axis=1))
            diffs[...] = dot(jnp.concatenate(rows, axis=0), stencil[...])
            chunk = 16
            for at in range(0, NX, chunk):
                east = source[level, PAD + at : PAD + at + chunk, :] * (1.0 / 60.0)
                north = source[LEV + level, PAD + at : PAD + at + chunk, :] * (1.0 / 60.0)
                east_size = jnp.abs(east)
                north_size = jnp.abs(north)
                for f in range(FIELDS):
                    plane = f * LEV + level

                    def cell(offset):
                        return source[plane, PAD + at + offset : PAD + at + offset + chunk, :]

                    up1, up2, up3 = cell(1), cell(2), cell(3)
                    down1, down2, down3 = cell(-1), cell(-2), cell(-3)
                    central = 45.0 * (up1 - down1) - 9.0 * (up2 - down2) + (up3 - down3)
                    smooth = (
                        (up3 + down3)
                        - 6.0 * (up2 + down2)
                        + 15.0 * (up1 + down1)
                        - 20.0 * cell(0)
                    )
                    central_y = diffs[f * NX + at : f * NX + at + chunk, 0:NY]
                    smooth_y = diffs[f * NX + at : f * NX + at + chunk, NY : 2 * NY]
                    value = (east_size * smooth - east * central) + (
                        north_size * smooth_y - north * central_y
                    )
                    finish(f, level, plane, at, chunk, value)


    def turbines(group):
        counts = count[...].astype(F32)
        kinds = kind[...]

        @pl.loop(0, GLEV)
        def _(inner):
            level = group * GLEV + inner
            rate = jnp.full((NX, NY), drag_coeff[0, level])
            growth = jnp.full((NX, NY), tke_coeff[0, level])
            for k in range(1, NTYPE):
                here = kinds == k
                rate = jnp.where(here, drag_coeff[k, level], rate)
                growth = jnp.where(here, tke_coeff[k, level], growth)
            east = q0[level, PAD : PAD + NX, :]
            north = q0[LEV + level, PAD : PAD + NX, :]
            speed = jnp.sqrt(east * east + north * north)
            rate = counts * rate * speed
            tke[level] = tke[level] + counts * growth * speed * speed * speed
            drag[level] = -(rate * east)
            drag[LEV + level] = -(rate * north)

    def tke_copy(group):
        rows = pl.ds(group * GLEV, GLEV)
        return pltpu.make_async_copy(tke.at[rows], tke_out.at[rows], out_sem.at[3, group])


    for copy in inputs[:3]:
        copy.wait()

    @pl.loop(0, GROUPS)
    def _(group):
        @pl.loop(0, GLEV)
        def _(inner):
            for f in range(FIELDS):
                plane = f * LEV + group * GLEV + inner
                pack_edges(0, group, f * GLEV + inner, q0[plane, PAD : PAD + NX, :])

    for copy in inputs[3:6]:
        copy.wait()

    @pl.loop(0, BANDS)
    def _(to):
        rows = []
        for f in range(FIELDS):
            part = pl.ds(f * LEV + 2 * to, 2)
            gap = target[part] - q0[part, PAD : PAD + NX, :]
            rows.append(gap.reshape(2 * NX, NY))
        high, low = split(jnp.concatenate(rows, axis=0))
        along_x = quarters(dot(x_forward[...], jnp.concatenate([high, low], axis=1)), 128, NY)
        both = lax.dot_general(
            y_forward[...],
            jnp.concatenate(split(along_x), axis=1),
            (((1,), (1,)), ((), ())),
            preferred_element_type=F32,
        )
        s1[to] = both[:RY] + both[RY:]

    pl.semaphore_wait(barrier, BANDS - 1 + TILES - 1)

    @pl.loop(0, GROUPS)
    def _(group):
        send_edges(0, group)

    def exchange(axis, count, me, source, into, send_sem, recv_sem, step):
        other = lax.rem(me + step, count)
        return (
            other,
            pltpu.make_async_remote_copy(
                src_ref=source.at[other],
                dst_ref=into.at[me],
                send_sem=send_sem.at[other],
                recv_sem=recv_sem.at[me],
                device_id={axis: other},
                device_id_type=MESH,
            ),
        )

    def send_all(axis, count, me, source, into, send_sem, recv_sem):
        for step in range(1, count):
            exchange(axis, count, me, source, into, send_sem, recv_sem, step)[1].start()
        into[me] = source[me]

    def receive_all(axis, count, me, source, into, send_sem, recv_sem):
        for step in range(1, count):
            other = lax.rem(me + step, count)
            pltpu.make_async_remote_copy(
                src_ref=source.at[other],
                dst_ref=into.at[other],
                send_sem=send_sem.at[other],
                recv_sem=recv_sem.at[other],
                device_id={axis: other},
                device_id_type=MESH,
            ).wait_recv()

    def sent_all(axis, count, me, source, into, send_sem, recv_sem):
        for step in range(1, count):
            exchange(axis, count, me, source, into, send_sem, recv_sem, step)[1].wait_send()

    phase1 = ("band", BANDS, band, s1, r1, s1_sem, r1_sem)
    phase2 = ("tile", TILES, tile, s2, r2, s2_sem, r2_sem)
    phase3 = ("tile", TILES, tile, s3, r3, s3_sem, r3_sem)
    phase4 = ("band", BANDS, band, s4, r4, s4_sem, r4_sem)

    send_all(*phase1)
    for copy in inputs[6:]:
        copy.wait()

    def first_finish(f, level, plane, at, chunk, value):
        if f < 2:
            value = value + drag[plane, at : at + chunk, :]
        partial[plane, at : at + chunk, :] = value

    def first_stage(group):
        turbines(group)
        tke_copy(group).start()
        await_edges(0, group)
        advance(0, group, q0, first_finish)

    first_stage(0)
    receive_all(*phase1)

    received = r1[...].reshape(BANDS * RY, 128)
    columns = jnp.concatenate(split(received), axis=1)
    s2[...] = quarters(dot(m_forward[...], columns), MODES, 128).reshape(TILES, 8, 128)
    send_all(*phase2)
    first_stage(1)
    receive_all(*phase2)

    lane8 = lax.broadcasted_iota(jnp.int32, (8, 128), 1)
    inside = [
        jnp.logical_and(lane8 >= RX * i, lane8 < RX * (i + 1)) for i in range(PER)
    ]
    blocks = [r2[t] for t in range(TILES)]
    rows = []
    for p in range(PLANES):
        parts = []
        for first in range(0, TILES, PER):
            value = jnp.zeros((8, 128), F32)
            for i, t in enumerate(range(first, min(first + PER, TILES))):
                moved = pltpu.roll(blocks[t], (RX * (i - p)) % 128, 1)
                value = jnp.where(inside[i], moved, value)
            parts.append(value)
        rows.append(jnp.concatenate(parts, axis=1))
    packed = jnp.concatenate(split(jnp.concatenate(rows, axis=0)), axis=0)
    spectra = quarters(dot(packed, k_forward[...]), 8 * PLANES, MODES)
    mine = pl.ds(pl.multiple_of(tile * 8, 8), 8)
    weight = weights[mine, :]
    east_number = number_k[...]
    north_number = number_m[mine, :]
    masks = []
    for inner in range(2):
        keep = jnp.logical_and(
            east_number <= cutoffs[0, 2 * band + inner],
            north_number <= cutoffs[1, 2 * band + inner],
        )
        masks.append(jnp.where(keep, weight, 0.0))
    spectra = spectra * jnp.concatenate(masks * FIELDS, axis=0)
    high, low = split(spectra)
    back = dot(jnp.concatenate([high, low], axis=0), k_back[...])
    back = quarters(back, 8 * PLANES, 384)
    for t in range(TILES):
        first = 128 * (t // PER)
        value = jnp.zeros((8, 128), F32)
        for p in range(PLANES):
            moved = pltpu.roll(
                back[8 * p : 8 * p + 8, first : first + 128], (RX * (p - t % PER)) % 128, 1
            )
            value = jnp.where(inside[p], moved, value)
        s3[t] = value
    send_all(*phase3)
    first_stage(2)
    receive_all(*phase3)

    received = r3[...].reshape(MODES, 128)
    back = quarters(dot(m_back[...], jnp.concatenate(split(received), axis=1)), BANDS * RY, 128)
    s4[...] = back.reshape(BANDS, RY, 128)
    send_all(*phase4)
    first_stage(3)
    receive_all(*phase4)

    for half in range(2):
        columns = r4[4 * half : 4 * half + 4].reshape(4 * RY, 128).T
        wide = dot(jnp.concatenate(split(columns), axis=0), y_back[...])
        wide = quarters(wide, 128, 4 * NY)
        for i in range(4):
            modes[4 * half + i] = wide[:, i * NY : (i + 1) * NY]

    @pl.loop(0, GROUPS)
    def _(group):
        for pair in range(2):
            high, low = split(modes[2 * group + pair])
            smooth_part = dot(x_back[...], jnp.concatenate([high, low, high], axis=0))
            for f in range(FIELDS):
                for inner in range(2):
                    plane = f * LEV + group * GLEV + 2 * pair + inner
                    at = (2 * f + inner) * NX
                    nudge = smooth_part[at : at + NX]
                    if f < 2:
                        force[plane] = nudge + drag[plane]
                    else:
                        force[plane] = nudge
                    value = q0[plane, PAD : PAD + NX, :] + (1.0 / 3.0) * (nudge + partial[plane])
                    q1[plane, PAD : PAD + NX, :] = value
                    pack_edges(1, group, f * GLEV + 2 * pair + inner, value)
        send_edges(1, group)

    def second_finish(f, level, plane, at, chunk, value):
        q2[plane, PAD + at : PAD + at + chunk, :] = q0[
            plane, PAD + at : PAD + at + chunk, :
        ] + 0.5 * (value + force[plane, at : at + chunk, :])

    @pl.loop(0, GROUPS)
    def _(group):
        await_edges(1, group)
        advance(1, group, q1, second_finish)

        @pl.loop(0, GLEV)
        def _(inner):
            for f in range(FIELDS):
                plane = f * LEV + group * GLEV + inner
                pack_edges(2, group, f * GLEV + inner, q2[plane, PAD : PAD + NX, :])

        send_edges(2, group)

    def third_finish(f, level, plane, at, chunk, value):
        result[plane, at : at + chunk, :] = q0[plane, PAD + at : PAD + at + chunk, :] + (
            value + force[plane, at : at + chunk, :]
        )

    def out_copy(f, group):
        rows = pl.ds(group * GLEV, GLEV)
        into = (east_out, north_out, theta_out)[f]
        return pltpu.make_async_copy(
            result.at[pl.ds(f * LEV + group * GLEV, GLEV)], into.at[rows], out_sem.at[f, group]
        )

    @pl.loop(0, GROUPS)
    def _(group):
        await_edges(2, group)
        advance(2, group, q2, third_finish)
        for f in range(FIELDS):
            out_copy(f, group).start()

    for phase in (phase1, phase2, phase3, phase4):
        sent_all(*phase)

    @pl.loop(0, GROUPS)
    def _(group):
        for turn in range(3):
            edges_sent(turn, group)
        for f in range(FIELDS):
            out_copy(f, group).wait()
        tke_copy(group).wait()


def shards(*arguments):
    tables = [jnp.asarray(table) for table in make_tables()]
    field = jax.ShapeDtypeStruct((LEV, NX, NY), F32)
    anywhere = pl.BlockSpec(memory_space=pl.ANY)
    smem = pl.BlockSpec(memory_space=pltpu.SMEM)
    vmem = pl.BlockSpec(memory_space=pltpu.VMEM)
    padded = pltpu.VMEM((FIELDS * LEV, NX + 2 * PAD, NY), F32)
    planes = pltpu.VMEM((FIELDS * LEV, NX, NY), F32)
    dma = pltpu.SemaphoreType.DMA
    return pl.pallas_call(
        kernel,
        out_shape=(field,) * 4,
        in_specs=[anywhere] * 9 + [smem] * 3 + [vmem] * len(tables),
        out_specs=(anywhere,) * 4,
        scratch_shapes=[
            padded,
            padded,
            padded,
            planes,
            pltpu.VMEM((LEV, NX, NY), F32),
            pltpu.VMEM((NX, NY), jnp.int32),
            pltpu.VMEM((NX, NY), jnp.int32),
            planes,
            pltpu.VMEM((2 * LEV, NX, NY), F32),
            planes,
            planes,
            pltpu.VMEM((FIELDS * NX, 2 * NY), F32),
            pltpu.VMEM((NX, 128), F32),
            pltpu.VMEM((3, 2, GROUPS, SLOTS, 4, 128), F32),
            pltpu.VMEM((3, 2, GROUPS, SLOTS, 4, 128), F32),
            pltpu.VMEM((3, GROUPS, NX, 128), F32),
            pltpu.VMEM((3, 2, GROUPS, NX, 128), F32),
            pltpu.VMEM((BANDS, RY, 128), F32),
            pltpu.VMEM((BANDS, RY, 128), F32),
            pltpu.VMEM((TILES, 8, 128), F32),
            pltpu.VMEM((TILES, 8, 128), F32),
            pltpu.VMEM((TILES, 8, 128), F32),
            pltpu.VMEM((TILES, 8, 128), F32),
            pltpu.VMEM((BANDS, RY, 128), F32),
            pltpu.VMEM((BANDS, RY, 128), F32),
            pltpu.VMEM((BANDS, 128, NY), F32),
            dma((9,)),
            dma((4, GROUPS)),
            dma((3, 2, GROUPS)),
            dma((3, 2, GROUPS)),
            dma((3, 2, GROUPS)),
            dma((3, 2, GROUPS)),
            dma((BANDS,)),
            dma((BANDS,)),
            dma((TILES,)),
            dma((TILES,)),
            dma((TILES,)),
            dma((TILES,)),
            dma((BANDS,)),
            dma((BANDS,)),
        ],
        compiler_params=pltpu.CompilerParams(
            collective_id=0, has_side_effects=True, vmem_limit_bytes=40 * 1024 * 1024
        ),
        cost_estimate=pl.CostEstimate(
            flops=10**9, bytes_accessed=6 * 2**20, transcendentals=LEV * NX * NY
        ),
        name="step",
    )(*arguments, *tables)


def solution(mesh):
    field = P(None, "tile", "band")
    column = P("tile", "band")
    in_specs = (field,) * 7 + (column,) * 2 + (P(),) * 3
    return jax.shard_map(
        shards, mesh=mesh, in_specs=in_specs, out_specs=(field,) * 4, check_vma=False
    )
```

```python
import functools

import jax
import jax.numpy as jnp
import ml_dtypes
import numpy as np
from jax import lax
from jax.experimental import pallas as pl
from jax.experimental.pallas import tpu as pltpu
from jax.sharding import PartitionSpec as P

KMAX = 64
MODES = 2 * KMAX
NTYPE = 8
LEV = 16
FIELDS = 3
BANDS = 8
TILES = 16
NX = 64
NY = 128
RX = 21
RY = 32
PLANES = 6
GROUPS = 4
GLEV = LEV // GROUPS
SLOTS = FIELDS * GLEV
PER = 6
PAD = 8
TABLES = 14
MESH = pl.DeviceIdType.MESH
BF = jnp.bfloat16
F32 = jnp.float32


def wavenumbers():
    index = np.arange(MODES)
    return np.where(index < KMAX, index, index - KMAX + 1)


def basis(extent, positions):
    number = wavenumbers()
    angle = 2 * np.pi * ((number[:, None] * positions[None, :]) % extent) / extent
    return np.where((np.arange(MODES) < KMAX)[:, None], np.cos(angle), np.sin(angle))


def window(length, extent, rank):
    index = np.arange(length)
    half = (KMAX + 0.5) / extent
    diagonal = ((length - 1 - 2 * index) / 2) ** 2 * np.cos(2 * np.pi * half)
    beside = index[1:] * (length - index[1:]) / 2
    _, vectors = np.linalg.eigh(np.diag(diagonal) + np.diag(beside, 1) + np.diag(beside, -1))
    vectors = vectors[:, ::-1][:, :rank]
    largest = vectors[np.argmax(np.abs(vectors) > 0.02, axis=0), np.arange(rank)]
    return vectors * np.sign(largest)


def halves(table):
    high = table.astype(np.float32).astype(ml_dtypes.bfloat16)
    low = (table - high.astype(np.float64)).astype(np.float32).astype(ml_dtypes.bfloat16)
    return high, low


def stencil_table():
    central = {1: 45.0, -1: -45.0, 2: -9.0, -2: 9.0, 3: 1.0, -3: -1.0}
    smooth = {3: 1.0, -3: 1.0, 2: -6.0, -2: -6.0, 1: 15.0, -1: 15.0, 0: -20.0}
    inner = np.zeros((NY, 2 * NY))
    outer = np.zeros((NY, 2 * NY))
    for column, taps in ((0, central), (NY, smooth)):
        for y in range(NY):
            for offset, tap in taps.items():
                at = y + offset
                if 0 <= at < NY:
                    inner[at, column + y] = tap
                elif at < 0:
                    outer[at + 3, column + y] = tap
                else:
                    outer[at - NY + 3, column + y] = tap
    return np.concatenate([inner, inner, outer, outer]).astype(ml_dtypes.bfloat16)


def make_tables():
    east_n, north_n = NX * TILES, NY * BANDS
    vx = window(NX, east_n, RX)
    vy = window(NY, north_n, RY)
    wx = window(NX + 6, east_n, RX)
    wy = window(NY + 6, north_n, RY)
    cells_x = np.arange(NX + 6) - 3
    cells_y = np.arange(NY + 6) - 3
    ux = [basis(east_n, NX * t + np.arange(NX)) @ vx for t in range(TILES)]
    uy = [basis(north_n, NY * b + np.arange(NY)) @ vy for b in range(BANDS)]

    block = np.zeros((PLANES * NX, 128))
    for p in range(PLANES):
        block[p * NX : (p + 1) * NX, p * RX : (p + 1) * RX] = vx
    high, low = halves(block.T)
    x_forward = np.concatenate([high, low], axis=0)
    rows = PLANES * NX
    block = np.zeros((rows + PLANES * 8, 128))
    for p in range(PLANES):
        columns = slice(p * RX, (p + 1) * RX)
        block[p * NX : (p + 1) * NX, columns] = 0.5 * wx[3 : NX + 3]
        block[rows + 8 * p : rows + 8 * p + 3, columns] = 0.5 * wx[:3]
        block[rows + 8 * p + 4 : rows + 8 * p + 7, columns] = 0.5 * wx[NX + 3 :]
    high, low = halves(block)
    x_back = np.concatenate([high, high, low], axis=1)
    shared = sum(block[p * NX : (p + 1) * NX] for p in range(PLANES))
    high, low = halves(shared)
    x_shared = np.concatenate([high, high, low], axis=1)

    high, low = halves(vy.T)
    y_forward = np.concatenate(
        [np.concatenate([high, high], axis=1), np.concatenate([low, 0 * low], axis=1)], axis=0
    )
    inner_y, outer_y = wy[3 : NY + 3].T, np.zeros((RY, NY))
    outer_y[:, : 6 * SLOTS] = np.tile(np.concatenate([wy[:3], wy[NY + 3 :]]).T, (1, SLOTS))
    diag = np.zeros((4 * RY, 8 * NY))
    for g in range(4):
        diag[g * RY : (g + 1) * RY, g * NY : (g + 1) * NY] = inner_y
        diag[g * RY : (g + 1) * RY, (4 + g) * NY : (5 + g) * NY] = outer_y
    y_back = np.concatenate(halves(diag), axis=1)
    own_slot = np.zeros((2, 128, 128), np.float32)
    for pair in range(2):
        for p in range(PLANES):
            slot = (p // 2) * GLEV + 2 * pair + p % 2
            own_slot[pair, p * RX : (p + 1) * RX, 6 * slot : 6 * slot + 6] = 1

    uy_all = np.concatenate(uy, axis=1)
    m_forward = np.concatenate(halves(uy_all), axis=0)
    uy = [basis(north_n, NY * b + cells_y) @ wy for b in range(BANDS)]
    m_back = np.concatenate(halves(np.concatenate(uy, axis=1).T), axis=0)

    ux_all = np.zeros((MODES, 384))
    for t in range(TILES):
        at = 128 * (t // PER) + RX * (t % PER)
        ux_all[:, at : at + RX] = ux[t]
    k_forward = np.concatenate(halves(ux_all.T), axis=1)
    for t in range(TILES):
        at = 128 * (t // PER) + RX * (t % PER)
        ux_all[:, at : at + RX] = basis(east_n, NX * t + cells_x) @ wx
    k_back = np.concatenate(halves(ux_all), axis=1)

    number = wavenumbers()
    weight_k = np.where(number == 0, 1.0, 2.0) / east_n
    weight_m = np.where(number == 0, 1.0, 2.0) / north_n
    weights = (weight_m[:, None] * weight_k[None, :]).astype(np.float32)
    number_k = np.broadcast_to(number[None, :], (8, MODES)).astype(np.int32)
    number_m = np.broadcast_to(number[:, None], (MODES, MODES)).astype(np.int32)
    return (
        x_forward,
        y_forward,
        m_forward,
        k_forward,
        k_back,
        m_back,
        y_back,
        x_back,
        x_shared,
        own_slot,
        stencil_table(),
        weights,
        number_k,
        number_m,
    )


def split(value):
    high = value.astype(BF)
    low = (value - high.astype(F32)).astype(BF)
    return high, low


def dot(a, b):
    return lax.dot_general(a, b, (((1,), (0,)), ((), ())), preferred_element_type=F32)


def quarters(product, rows, columns):
    return (product[:rows, :columns] + product[:rows, columns:]) + (
        product[rows:, :columns] + product[rows:, columns:]
    )


def kernel(
    wind_east,
    wind_north,
    theta_pert,
    tke_field,
    target_east,
    target_north,
    target_theta,
    turbine_count,
    turbine_type,
    drag_coeff,
    tke_coeff,
    cutoffs,
    *rest,
):
    table_sources, rest = rest[:TABLES], rest[TABLES:]
    tables, rest = rest[4 : 4 + TABLES], rest[:4] + rest[4 + TABLES :]
    step_body(
        wind_east,
        wind_north,
        theta_pert,
        tke_field,
        target_east,
        target_north,
        target_theta,
        turbine_count,
        turbine_type,
        drag_coeff,
        tke_coeff,
        cutoffs,
        table_sources,
        tables,
        *rest,
    )


def step_body(
    wind_east,
    wind_north,
    theta_pert,
    tke_field,
    target_east,
    target_north,
    target_theta,
    turbine_count,
    turbine_type,
    drag_coeff,
    tke_coeff,
    cutoffs,
    table_sources,
    tables,
    east_out,
    north_out,
    theta_out,
    tke_out,
    q0,
    q1,
    q2,
    target,
    tke,
    count,
    kind,
    partial,
    drag,
    force,
    result,
    diffs,
    y_halo,
    xs,
    xr,
    ys,
    yr,
    s1,
    r1,
    s2,
    r2,
    s3,
    r3,
    s4,
    r4,
    modes,
    outer_modes,
    operand,
    y_first,
    in_sem,
    table_sem,
    out_sem,
    xs_sem,
    xr_sem,
    ys_sem,
    yr_sem,
    s1_sem,
    r1_sem,
    s2_sem,
    r2_sem,
    s3_sem,
    r3_sem,
    s4_sem,
    r4_sem,
):
    (
        x_forward,
        y_forward,
        m_forward,
        k_forward,
        k_back,
        m_back,
        y_back,
        x_back,
        x_shared,
        own_slot,
        stencil,
        weights,
        number_k,
        number_m,
    ) = tables
    band = lax.axis_index("band")
    tile = lax.axis_index("tile")

    inputs = []
    for f, source in enumerate((wind_east, wind_north, theta_pert)):
        inputs.append((source, q0.at[pl.ds(f * LEV, LEV), pl.ds(PAD, NX), :]))
    for f, source in enumerate((target_east, target_north, target_theta)):
        inputs.append((source, target.at[pl.ds(f * LEV, LEV)]))
    inputs += [(tke_field, tke), (turbine_count, count), (turbine_type, kind)]
    inputs = [
        pltpu.make_async_copy(source, into, in_sem.at[i])
        for i, (source, into) in enumerate(inputs)
    ]
    table_copies = [
        pltpu.make_async_copy(source, into, table_sem.at[i])
        for i, (source, into) in enumerate(zip(table_sources, tables))
    ]
    for copy in inputs[:6] + table_copies + inputs[6:]:
        copy.start()

    @pl.when(tile == 0)
    def _():
        xr[:, 0] = jnp.zeros((3, GROUPS, SLOTS, 4, 128), F32)

    @pl.when(tile == TILES - 1)
    def _():
        xr[:, 1] = jnp.zeros((3, GROUPS, SLOTS, 4, 128), F32)

    @pl.when(band == 0)
    def _():
        yr[:, 0] = jnp.zeros((3, GROUPS, NX, 128), F32)

    @pl.when(band == BANDS - 1)
    def _():
        yr[:, 1] = jnp.zeros((3, GROUPS, NX, 128), F32)

    barrier = pltpu.get_barrier_semaphore()
    for step in range(1, BANDS):
        pl.semaphore_signal(
            barrier, inc=1, device_id={"band": lax.rem(band + step, BANDS)}, device_id_type=MESH
        )
    for step in range(1, TILES):
        pl.semaphore_signal(
            barrier, inc=1, device_id={"tile": lax.rem(tile + step, TILES)}, device_id_type=MESH
        )

    lane = lax.broadcasted_iota(jnp.int32, (NX, 128), 1)
    low_lane = lax.rem(lane, 6) < 3


    def pack_edges(turn, group, plane_of):
        packed = jnp.zeros((NX, 128), F32)
        for slot in range(SLOTS):
            plane = plane_of((slot // GLEV) * LEV + group * GLEV + slot % GLEV)
            xs[turn, 0, group, slot, 0:3, :] = plane[0:3]
            xs[turn, 1, group, slot, 0:3, :] = plane[NX - 3 : NX]
            mine = jnp.logical_and(lane >= slot * 6, lane < slot * 6 + 6)
            packed = jnp.where(mine, pltpu.roll(plane, slot * 6 + 3, 1), packed)
        ys[turn, group] = packed

    def interior(source):
        return lambda plane: source[plane, PAD : PAD + NX, :]

    def x_copy(turn, group, side):
        return pltpu.make_async_remote_copy(
            src_ref=xs.at[turn, side, group],
            dst_ref=xr.at[turn, 1 - side, group],
            send_sem=xs_sem.at[turn, side, group],
            recv_sem=xr_sem.at[turn, 1 - side, group],
            device_id={"tile": tile + (1 if side else -1)},
            device_id_type=MESH,
        )

    def y_copy(turn, group, side):
        return pltpu.make_async_remote_copy(
            src_ref=ys.at[turn, group],
            dst_ref=yr.at[turn, 1 - side, group],
            send_sem=ys_sem.at[turn, side, group],
            recv_sem=yr_sem.at[turn, 1 - side, group],
            device_id={"band": band + (1 if side else -1)},
            device_id_type=MESH,
        )

    has = (
        (tile > 0, band > 0),
        (tile < TILES - 1, band < BANDS - 1),
    )

    def send_edges(turn, group):
        for side in range(2):

            @pl.when(has[side][0])
            def _():
                x_copy(turn, group, side).start()

            @pl.when(has[side][1])
            def _():
                y_copy(turn, group, side).start()

    def await_edges(turn, group):
        for side in range(2):

            @pl.when(has[side][0])
            def _():
                x_copy(turn, group, 1 - side).wait_recv()

            @pl.when(has[side][1])
            def _():
                y_copy(turn, group, 1 - side).wait_recv()

    def merged_halo(turn, group):
        return jnp.where(low_lane, yr[turn, 0, group], yr[turn, 1, group])

    def fill_pads(turn, group, source):
        for f in range(FIELDS):
            for inner in range(GLEV):
                plane, slot = f * LEV + group * GLEV + inner, f * GLEV + inner
                source[plane, PAD - 3 : PAD, :] = xr[turn, 0, group, slot, 0:3, :]
                source[plane, PAD + NX : PAD + NX + 3, :] = xr[turn, 1, group, slot, 0:3, :]

    def edges_sent(turn, group):
        for side in range(2):

            @pl.when(has[side][0])
            def _():
                x_copy(turn, group, side).wait_send()

            @pl.when(has[side][1])
            def _():
                y_copy(turn, group, side).wait_send()


    def advance(group, source, finish):
        halo = y_halo[...]
        for slot in range(SLOTS):
            plane = (slot // GLEV) * LEV + group * GLEV + slot % GLEV
            high, low = split(source[plane, PAD : PAD + NX, :])
            halo_high, halo_low = split(pltpu.roll(halo, 128 - slot * 6, 1) if slot else halo)
            operand[slot * NX : (slot + 1) * NX, :] = jnp.concatenate(
                [high, low, halo_high, halo_low], axis=1
            )

        diffs[...] = dot(operand[...], stencil[...])

        @pl.loop(0, GLEV)
        def _(inner):
            level = group * GLEV + inner
            chunk = 16
            for at in range(0, NX, chunk):
                east = source[level, PAD + at : PAD + at + chunk, :] * (1.0 / 60.0)
                north = source[LEV + level, PAD + at : PAD + at + chunk, :] * (1.0 / 60.0)
                east_size = jnp.abs(east)
                north_size = jnp.abs(north)
                for f in range(FIELDS):
                    plane = f * LEV + level

                    def cell(offset):
                        return source[plane, PAD + at + offset : PAD + at + offset + chunk, :]

                    up1, up2, up3 = cell(1), cell(2), cell(3)
                    down1, down2, down3 = cell(-1), cell(-2), cell(-3)
                    central = 45.0 * (up1 - down1) - 9.0 * (up2 - down2) + (up3 - down3)
                    smooth = (
                        (up3 + down3)
                        - 6.0 * (up2 + down2)
                        + 15.0 * (up1 + down1)
                        - 20.0 * cell(0)
                    )
                    first = pl.multiple_of((f * GLEV + inner) * NX + at, 8)
                    central_y = diffs[pl.ds(first, chunk), 0:NY]
                    smooth_y = diffs[pl.ds(first, chunk), NY : 2 * NY]
                    value = (east_size * smooth - east * central) + (
                        north_size * smooth_y - north * central_y
                    )
                    finish(f, plane, at, chunk, value)


    def turbines(group):
        counts = count[...].astype(F32)
        kinds = kind[...]

        @pl.loop(0, GLEV)
        def _(inner):
            level = group * GLEV + inner
            rate = jnp.full((NX, NY), drag_coeff[0, level])
            growth = jnp.full((NX, NY), tke_coeff[0, level])
            for k in range(1, NTYPE):
                here = kinds == k
                rate = jnp.where(here, drag_coeff[k, level], rate)
                growth = jnp.where(here, tke_coeff[k, level], growth)
            east = q0[level, PAD : PAD + NX, :]
            north = q0[LEV + level, PAD : PAD + NX, :]
            speed = jnp.sqrt(east * east + north * north)
            rate = counts * rate * speed
            tke[level] = tke[level] + counts * growth * speed * speed * speed
            drag[level] = -(rate * east)
            drag[LEV + level] = -(rate * north)

    def tke_copy(group):
        rows = pl.ds(group * GLEV, GLEV)
        return pltpu.make_async_copy(tke.at[rows], tke_out.at[rows], out_sem.at[3, group])


    for copy in inputs[:3]:
        copy.wait()

    @pl.loop(0, GROUPS)
    def _(group):
        pack_edges(0, group, interior(q0))

    for copy in inputs[3:6] + table_copies:
        copy.wait()

    @pl.loop(0, BANDS)
    def _(to):
        rows = []
        for f in range(FIELDS):
            part = pl.ds(f * LEV + 2 * to, 2)
            gap = target[part] - q0[part, PAD : PAD + NX, :]
            rows.append(gap.reshape(2 * NX, NY))
        high, low = split(jnp.concatenate(rows, axis=0))
        along_x = quarters(dot(x_forward[...], jnp.concatenate([high, low], axis=1)), 128, NY)
        both = lax.dot_general(
            y_forward[...],
            jnp.concatenate(split(along_x), axis=1),
            (((1,), (1,)), ((), ())),
            preferred_element_type=F32,
        )
        s1[to] = both[:RY] + both[RY:]

    pl.semaphore_wait(barrier, BANDS - 1 + TILES - 1)

    @pl.loop(0, GROUPS)
    def _(group):
        send_edges(0, group)

    def exchange(axis, count, me, source, into, send_sem, recv_sem, step):
        other = lax.rem(me + step, count)
        return (
            other,
            pltpu.make_async_remote_copy(
                src_ref=source.at[other],
                dst_ref=into.at[me],
                send_sem=send_sem.at[other],
                recv_sem=recv_sem.at[me],
                device_id={axis: other},
                device_id_type=MESH,
            ),
        )

    def send_all(axis, count, me, source, into, send_sem, recv_sem):
        for step in range(1, count):
            exchange(axis, count, me, source, into, send_sem, recv_sem, step)[1].start()
        into[me] = source[me]

    def receive_all(axis, count, me, source, into, send_sem, recv_sem):
        for step in range(1, count):
            other = lax.rem(me + step, count)
            pltpu.make_async_remote_copy(
                src_ref=source.at[other],
                dst_ref=into.at[other],
                send_sem=send_sem.at[other],
                recv_sem=recv_sem.at[other],
                device_id={axis: other},
                device_id_type=MESH,
            ).wait_recv()

    def sent_all(axis, count, me, source, into, send_sem, recv_sem):
        for step in range(1, count):
            exchange(axis, count, me, source, into, send_sem, recv_sem, step)[1].wait_send()

    phase1 = ("band", BANDS, band, s1, r1, s1_sem, r1_sem)
    phase2 = ("tile", TILES, tile, s2, r2, s2_sem, r2_sem)
    phase3 = ("tile", TILES, tile, s3, r3, s3_sem, r3_sem)
    phase4 = ("band", BANDS, band, s4, r4, s4_sem, r4_sem)

    send_all(*phase1)
    for copy in inputs[6:]:
        copy.wait()

    def first_finish(f, plane, at, chunk, value):
        if f < 2:
            value = value + drag[plane, at : at + chunk, :]
        partial[plane, at : at + chunk, :] = value

    def first_stage(group):
        turbines(group)
        tke_copy(group).start()
        await_edges(0, group)
        fill_pads(0, group, q0)
        halo = merged_halo(0, group)
        y_first[group] = halo
        y_halo[...] = halo
        advance(group, q0, first_finish)
        pack_edges(1, group, lambda plane: partial[plane])
        send_edges(1, group)

    first_stage(0)
    receive_all(*phase1)

    received = r1[...].reshape(BANDS * RY, 128)
    columns = jnp.concatenate(split(received), axis=1)
    s2[...] = quarters(dot(m_forward[...], columns), MODES, 128).reshape(TILES, 8, 128)
    send_all(*phase2)
    first_stage(1)
    receive_all(*phase2)

    lane8 = lax.broadcasted_iota(jnp.int32, (8, 128), 1)
    inside = [
        jnp.logical_and(lane8 >= RX * i, lane8 < RX * (i + 1)) for i in range(PER)
    ]
    blocks = [r2[t] for t in range(TILES)]
    rows = []
    for p in range(PLANES):
        parts = []
        for first in range(0, TILES, PER):
            value = jnp.zeros((8, 128), F32)
            for i, t in enumerate(range(first, min(first + PER, TILES))):
                moved = pltpu.roll(blocks[t], (RX * (i - p)) % 128, 1)
                value = jnp.where(inside[i], moved, value)
            parts.append(value)
        rows.append(jnp.concatenate(parts, axis=1))
    packed = jnp.concatenate(split(jnp.concatenate(rows, axis=0)), axis=0)
    spectra = quarters(dot(packed, k_forward[...]), 8 * PLANES, MODES)
    mine = pl.ds(pl.multiple_of(tile * 8, 8), 8)
    weight = weights[mine, :]
    east_number = number_k[...]
    north_number = number_m[mine, :]
    masks = []
    for inner in range(2):
        keep = jnp.logical_and(
            east_number <= cutoffs[0, 2 * band + inner],
            north_number <= cutoffs[1, 2 * band + inner],
        )
        masks.append(jnp.where(keep, weight, 0.0))
    spectra = spectra * jnp.concatenate(masks * FIELDS, axis=0)
    high, low = split(spectra)
    back = dot(jnp.concatenate([high, low], axis=0), k_back[...])
    back = quarters(back, 8 * PLANES, 384)
    for t in range(TILES):
        first = 128 * (t // PER)
        value = jnp.zeros((8, 128), F32)
        for p in range(PLANES):
            moved = pltpu.roll(
                back[8 * p : 8 * p + 8, first : first + 128], (RX * (p - t % PER)) % 128, 1
            )
            value = jnp.where(inside[p], moved, value)
        s3[t] = value
    send_all(*phase3)
    first_stage(2)
    receive_all(*phase3)

    received = r3[...].reshape(MODES, 128)
    back = quarters(dot(m_back[...], jnp.concatenate(split(received), axis=1)), BANDS * RY, 128)
    s4[...] = back.reshape(BANDS, RY, 128)
    send_all(*phase4)
    first_stage(3)
    receive_all(*phase4)

    for half in range(2):
        columns = r4[4 * half : 4 * half + 4].reshape(4 * RY, 128).T
        wide = dot(jnp.concatenate(split(columns), axis=0), y_back[...])
        wide = quarters(wide, 128, 8 * NY)
        for i in range(4):
            modes[4 * half + i] = wide[:, i * NY : (i + 1) * NY]
            outer_modes[4 * half + i] = wide[:, (4 + i) * NY : (5 + i) * NY] * own_slot[i % 2]

    third = 1.0 / 3.0
    inside_x = [jnp.where(flag[0], 1.0, 0.0) for flag in has]
    inside_y = jnp.where(
        low_lane, jnp.where(has[0][1], 1.0, 0.0), jnp.where(has[1][1], 1.0, 0.0)
    )

    def second_finish(f, plane, at, chunk, value):
        q2[plane, PAD + at : PAD + at + chunk, :] = q0[
            plane, PAD + at : PAD + at + chunk, :
        ] + 0.5 * (value + force[plane, at : at + chunk, :])

    @pl.loop(0, GROUPS)
    def _(group):
        await_edges(1, group)
        outer = jnp.zeros((NX, 128), F32)
        for pair in range(2):
            high, low = split(modes[2 * group + pair])
            smooth_part = dot(x_back[...], jnp.concatenate([high, low, high], axis=0))
            high, low = split(outer_modes[2 * group + pair])
            outer = outer + dot(x_shared[...], jnp.concatenate([high, low, high], axis=0))
            for f in range(FIELDS):
                for inner in range(2):
                    plane = f * LEV + group * GLEV + 2 * pair + inner
                    slot = f * GLEV + 2 * pair + inner
                    p = 2 * f + inner
                    nudge = smooth_part[p * NX : (p + 1) * NX]
                    if f < 2:
                        force[plane] = nudge + drag[plane]
                    else:
                        force[plane] = nudge
                    q1[plane, PAD : PAD + NX, :] = q0[plane, PAD : PAD + NX, :] + third * (
                        nudge + partial[plane]
                    )
                    for side, into in ((0, PAD - 3), (1, PAD + NX)):
                        first = PLANES * NX + 8 * p + 4 * side
                        q1[plane, into : into + 3, :] = xr[0, side, group, slot, 0:3, :] + third * (
                            smooth_part[first : first + 3] * inside_x[side]
                            + xr[1, side, group, slot, 0:3, :]
                        )
        y_halo[...] = y_first[group] + third * (outer * inside_y + merged_halo(1, group))

        advance(group, q1, second_finish)
        pack_edges(2, group, interior(q2))
        send_edges(2, group)

    def third_finish(f, plane, at, chunk, value):
        result[plane, at : at + chunk, :] = q0[plane, PAD + at : PAD + at + chunk, :] + (
            value + force[plane, at : at + chunk, :]
        )

    def out_copy(f, group):
        rows = pl.ds(group * GLEV, GLEV)
        into = (east_out, north_out, theta_out)[f]
        return pltpu.make_async_copy(
            result.at[pl.ds(f * LEV + group * GLEV, GLEV)], into.at[rows], out_sem.at[f, group]
        )

    @pl.loop(0, GROUPS)
    def _(group):
        await_edges(2, group)
        fill_pads(2, group, q2)
        y_halo[...] = merged_halo(2, group)
        advance(group, q2, third_finish)
        for f in range(FIELDS):
            out_copy(f, group).start()

    for phase in (phase1, phase2, phase3, phase4):
        sent_all(*phase)

    @pl.loop(0, GROUPS)
    def _(group):
        for turn in range(3):
            edges_sent(turn, group)
        for f in range(FIELDS):
            out_copy(f, group).wait()
        tke_copy(group).wait()


def shards(*arguments):
    tables = [jnp.asarray(table) for table in make_tables()]
    field = jax.ShapeDtypeStruct((LEV, NX, NY), F32)
    anywhere = pl.BlockSpec(memory_space=pl.ANY)
    smem = pl.BlockSpec(memory_space=pltpu.SMEM)
    padded = pltpu.VMEM((FIELDS * LEV, NX + 2 * PAD, NY), F32)
    planes = pltpu.VMEM((FIELDS * LEV, NX, NY), F32)
    dma = pltpu.SemaphoreType.DMA
    return pl.pallas_call(
        kernel,
        out_shape=(field,) * 4,
        in_specs=[anywhere] * 9 + [smem] * 3 + [anywhere] * TABLES,
        out_specs=(anywhere,) * 4,
        scratch_shapes=[pltpu.VMEM(table.shape, table.dtype) for table in tables]
        + [
            padded,
            padded,
            padded,
            planes,
            pltpu.VMEM((LEV, NX, NY), F32),
            pltpu.VMEM((NX, NY), jnp.int32),
            pltpu.VMEM((NX, NY), jnp.int32),
            planes,
            pltpu.VMEM((2 * LEV, NX, NY), F32),
            planes,
            planes,
            pltpu.VMEM((SLOTS * NX, 2 * NY), F32),
            pltpu.VMEM((NX, 128), F32),
            pltpu.VMEM((3, 2, GROUPS, SLOTS, 4, 128), F32),
            pltpu.VMEM((3, 2, GROUPS, SLOTS, 4, 128), F32),
            pltpu.VMEM((3, GROUPS, NX, 128), F32),
            pltpu.VMEM((3, 2, GROUPS, NX, 128), F32),
            pltpu.VMEM((BANDS, RY, 128), F32),
            pltpu.VMEM((BANDS, RY, 128), F32),
            pltpu.VMEM((TILES, 8, 128), F32),
            pltpu.VMEM((TILES, 8, 128), F32),
            pltpu.VMEM((TILES, 8, 128), F32),
            pltpu.VMEM((TILES, 8, 128), F32),
            pltpu.VMEM((BANDS, RY, 128), F32),
            pltpu.VMEM((BANDS, RY, 128), F32),
            pltpu.VMEM((BANDS, 128, NY), F32),
            pltpu.VMEM((BANDS, 128, NY), F32),
            pltpu.VMEM((SLOTS * NX, 4 * NY), BF),
            pltpu.VMEM((GROUPS, NX, 128), F32),
            dma((9,)),
            dma((TABLES,)),
            dma((4, GROUPS)),
            dma((3, 2, GROUPS)),
            dma((3, 2, GROUPS)),
            dma((3, 2, GROUPS)),
            dma((3, 2, GROUPS)),
            dma((BANDS,)),
            dma((BANDS,)),
            dma((TILES,)),
            dma((TILES,)),
            dma((TILES,)),
            dma((TILES,)),
            dma((BANDS,)),
            dma((BANDS,)),
        ],
        compiler_params=pltpu.CompilerParams(
            collective_id=0, has_side_effects=True, vmem_limit_bytes=61 * 1024 * 1024
        ),
        cost_estimate=pl.CostEstimate(
            flops=10**9, bytes_accessed=6 * 2**20, transcendentals=LEV * NX * NY
        ),
        name="step",
    )(*arguments, *tables)


def solution(mesh):
    field = P(None, "tile", "band")
    column = P("tile", "band")
    in_specs = (field,) * 7 + (column,) * 2 + (P(),) * 3
    return jax.shard_map(
        shards, mesh=mesh, in_specs=in_specs, out_specs=(field,) * 4, check_vma=False
    )
```

```python
import functools

import jax
import jax.numpy as jnp
import ml_dtypes
import numpy as np
from jax import lax
from jax.experimental import pallas as pl
from jax.experimental.pallas import tpu as pltpu
from jax.sharding import PartitionSpec as P

KMAX = 64
MODES = 2 * KMAX
NTYPE = 8
LEV = 16
FIELDS = 3
BANDS = 8
TILES = 16
NX = 64
NY = 128
RX = 21
RY = 32
PLANES = 6
GROUPS = 4
GLEV = LEV // GROUPS
SLOTS = FIELDS * GLEV
PER = 6
PAD = 8
TABLES = 14
MESH = pl.DeviceIdType.MESH
BF = jnp.bfloat16
F32 = jnp.float32


def wavenumbers():
    index = np.arange(MODES)
    return np.where(index < KMAX, index, index - KMAX + 1)


def basis(extent, positions):
    number = wavenumbers()
    angle = 2 * np.pi * ((number[:, None] * positions[None, :]) % extent) / extent
    return np.where((np.arange(MODES) < KMAX)[:, None], np.cos(angle), np.sin(angle))


def window(length, extent, rank):
    index = np.arange(length)
    half = (KMAX + 0.5) / extent
    diagonal = ((length - 1 - 2 * index) / 2) ** 2 * np.cos(2 * np.pi * half)
    beside = index[1:] * (length - index[1:]) / 2
    _, vectors = np.linalg.eigh(np.diag(diagonal) + np.diag(beside, 1) + np.diag(beside, -1))
    vectors = vectors[:, ::-1][:, :rank]
    largest = vectors[np.argmax(np.abs(vectors) > 0.02, axis=0), np.arange(rank)]
    return vectors * np.sign(largest)


def halves(table):
    high = table.astype(np.float32).astype(ml_dtypes.bfloat16)
    low = (table - high.astype(np.float64)).astype(np.float32).astype(ml_dtypes.bfloat16)
    return high, low


def stencil_table():
    central = {1: 45.0, -1: -45.0, 2: -9.0, -2: 9.0, 3: 1.0, -3: -1.0}
    smooth = {3: 1.0, -3: 1.0, 2: -6.0, -2: -6.0, 1: 15.0, -1: 15.0, 0: -20.0}
    inner = np.zeros((NY, 2 * NY))
    outer = np.zeros((NY, 2 * NY))
    for column, taps in ((0, central), (NY, smooth)):
        for y in range(NY):
            for offset, tap in taps.items():
                at = y + offset
                if 0 <= at < NY:
                    inner[at, column + y] = tap
                elif at < 0:
                    outer[at + 3, column + y] = tap
                else:
                    outer[at - NY + 3, column + y] = tap
    return np.concatenate([inner, inner, outer, outer]).astype(ml_dtypes.bfloat16)


def make_tables():
    east_n, north_n = NX * TILES, NY * BANDS
    vx = window(NX, east_n, RX)
    vy = window(NY, north_n, RY)
    wx = window(NX + 6, east_n, RX)
    wy = window(NY + 6, north_n, RY)
    cells_x = np.arange(NX + 6) - 3
    cells_y = np.arange(NY + 6) - 3
    ux = [basis(east_n, NX * t + np.arange(NX)) @ vx for t in range(TILES)]
    uy = [basis(north_n, NY * b + np.arange(NY)) @ vy for b in range(BANDS)]

    block = np.zeros((PLANES * NX, 128))
    for p in range(PLANES):
        block[p * NX : (p + 1) * NX, p * RX : (p + 1) * RX] = vx
    high, low = halves(block.T)
    x_forward = np.concatenate([high, low], axis=0)
    rows = PLANES * NX
    block = np.zeros((rows + PLANES * 8, 128))
    for p in range(PLANES):
        columns = slice(p * RX, (p + 1) * RX)
        block[p * NX : (p + 1) * NX, columns] = 0.5 * wx[3 : NX + 3]
        block[rows + 8 * p : rows + 8 * p + 3, columns] = 0.5 * wx[:3]
        block[rows + 8 * p + 4 : rows + 8 * p + 7, columns] = 0.5 * wx[NX + 3 :]
    high, low = halves(block)
    x_back = np.concatenate([high, high, low], axis=1)
    shared = sum(block[p * NX : (p + 1) * NX] for p in range(PLANES))
    high, low = halves(shared)
    x_shared = np.concatenate([high, high, low], axis=1)

    high, low = halves(vy.T)
    y_forward = np.concatenate(
        [np.concatenate([high, high], axis=1), np.concatenate([low, 0 * low], axis=1)], axis=0
    )
    inner_y, outer_y = wy[3 : NY + 3].T, np.zeros((RY, NY))
    outer_y[:, : 6 * SLOTS] = np.tile(np.concatenate([wy[:3], wy[NY + 3 :]]).T, (1, SLOTS))
    diag = np.zeros((4 * RY, 8 * NY))
    for g in range(4):
        diag[g * RY : (g + 1) * RY, g * NY : (g + 1) * NY] = inner_y
        diag[g * RY : (g + 1) * RY, (4 + g) * NY : (5 + g) * NY] = outer_y
    y_back = np.concatenate(halves(diag), axis=1)
    own_slot = np.zeros((2, 128, 128), np.float32)
    for pair in range(2):
        for p in range(PLANES):
            slot = (p // 2) * GLEV + 2 * pair + p % 2
            own_slot[pair, p * RX : (p + 1) * RX, 6 * slot : 6 * slot + 6] = 1

    uy_all = np.concatenate(uy, axis=1)
    m_forward = np.concatenate(halves(uy_all), axis=0)
    uy = [basis(north_n, NY * b + cells_y) @ wy for b in range(BANDS)]
    m_back = np.concatenate(halves(np.concatenate(uy, axis=1).T), axis=0)

    ux_all = np.zeros((MODES, 384))
    for t in range(TILES):
        at = 128 * (t // PER) + RX * (t % PER)
        ux_all[:, at : at + RX] = ux[t]
    k_forward = np.concatenate(halves(ux_all.T), axis=1)
    for t in range(TILES):
        at = 128 * (t // PER) + RX * (t % PER)
        ux_all[:, at : at + RX] = basis(east_n, NX * t + cells_x) @ wx
    k_back = np.concatenate(halves(ux_all), axis=1)

    number = wavenumbers()
    weight_k = np.where(number == 0, 1.0, 2.0) / east_n
    weight_m = np.where(number == 0, 1.0, 2.0) / north_n
    weights = (weight_m[:, None] * weight_k[None, :]).astype(np.float32)
    number_k = np.broadcast_to(number[None, :], (8, MODES)).astype(np.int32)
    number_m = np.broadcast_to(number[:, None], (MODES, MODES)).astype(np.int32)
    return (
        x_forward,
        y_forward,
        m_forward,
        k_forward,
        k_back,
        m_back,
        y_back,
        x_back,
        x_shared,
        own_slot,
        stencil_table(),
        weights,
        number_k,
        number_m,
    )


def split(value):
    high = value.astype(BF)
    low = (value - high.astype(F32)).astype(BF)
    return high, low


def dot(a, b):
    return lax.dot_general(a, b, (((1,), (0,)), ((), ())), preferred_element_type=F32)


def quarters(product, rows, columns):
    return (product[:rows, :columns] + product[:rows, columns:]) + (
        product[rows:, :columns] + product[rows:, columns:]
    )


def kernel(
    wind_east,
    wind_north,
    theta_pert,
    tke_field,
    target_east,
    target_north,
    target_theta,
    turbine_count,
    turbine_type,
    drag_coeff,
    tke_coeff,
    cutoffs,
    *rest,
):
    table_sources, rest = rest[:TABLES], rest[TABLES:]
    tables, rest = rest[4 : 4 + TABLES], rest[:4] + rest[4 + TABLES :]
    step_body(
        wind_east,
        wind_north,
        theta_pert,
        tke_field,
        target_east,
        target_north,
        target_theta,
        turbine_count,
        turbine_type,
        drag_coeff,
        tke_coeff,
        cutoffs,
        table_sources,
        tables,
        *rest,
    )


def step_body(
    wind_east,
    wind_north,
    theta_pert,
    tke_field,
    target_east,
    target_north,
    target_theta,
    turbine_count,
    turbine_type,
    drag_coeff,
    tke_coeff,
    cutoffs,
    table_sources,
    tables,
    east_out,
    north_out,
    theta_out,
    tke_out,
    q0,
    q1,
    q2,
    target,
    tke,
    count,
    kind,
    partial,
    drag,
    force,
    result,
    diffs,
    y_halo,
    xs,
    xr,
    ys,
    yr,
    s1,
    r1,
    s2,
    r2,
    s3,
    r3,
    s4,
    r4,
    modes,
    outer_modes,
    operand,
    y_first,
    in_sem,
    table_sem,
    out_sem,
    xs_sem,
    xr_sem,
    ys_sem,
    yr_sem,
    s1_sem,
    r1_sem,
    s2_sem,
    r2_sem,
    s3_sem,
    r3_sem,
    s4_sem,
    r4_sem,
):
    (
        x_forward,
        y_forward,
        m_forward,
        k_forward,
        k_back,
        m_back,
        y_back,
        x_back,
        x_shared,
        own_slot,
        stencil,
        weights,
        number_k,
        number_m,
    ) = tables
    band = lax.axis_index("band")
    tile = lax.axis_index("tile")

    inputs = []
    for f, source in enumerate((wind_east, wind_north, theta_pert)):
        inputs.append((source, q0.at[pl.ds(f * LEV, LEV), pl.ds(PAD, NX), :]))
    for f, source in enumerate((target_east, target_north, target_theta)):
        inputs.append((source, target.at[pl.ds(f * LEV, LEV)]))
    inputs += [(tke_field, tke), (turbine_count, count), (turbine_type, kind)]
    inputs = [
        pltpu.make_async_copy(source, into, in_sem.at[i])
        for i, (source, into) in enumerate(inputs)
    ]
    table_copies = [
        pltpu.make_async_copy(source, into, table_sem.at[i])
        for i, (source, into) in enumerate(zip(table_sources, tables))
    ]
    for copy in inputs[:6] + table_copies + inputs[6:]:
        copy.start()

    @pl.when(tile == 0)
    def _():
        xr[:, 0] = jnp.zeros((3, GROUPS, SLOTS, 4, 128), F32)

    @pl.when(tile == TILES - 1)
    def _():
        xr[:, 1] = jnp.zeros((3, GROUPS, SLOTS, 4, 128), F32)

    @pl.when(band == 0)
    def _():
        yr[:, 0] = jnp.zeros((3, GROUPS, NX, 128), F32)

    @pl.when(band == BANDS - 1)
    def _():
        yr[:, 1] = jnp.zeros((3, GROUPS, NX, 128), F32)

    barrier = pltpu.get_barrier_semaphore()
    for step in range(1, BANDS):
        pl.semaphore_signal(
            barrier, inc=1, device_id={"band": lax.rem(band + step, BANDS)}, device_id_type=MESH
        )
    for step in range(1, TILES):
        pl.semaphore_signal(
            barrier, inc=1, device_id={"tile": lax.rem(tile + step, TILES)}, device_id_type=MESH
        )

    lane = lax.broadcasted_iota(jnp.int32, (NX, 128), 1)
    low_lane = lax.rem(lane, 6) < 3


    def pack_edges(turn, group, plane_of):
        packed = jnp.zeros((NX, 128), F32)
        for slot in range(SLOTS):
            plane = plane_of((slot // GLEV) * LEV + group * GLEV + slot % GLEV)
            xs[turn, 0, group, slot, 0:3, :] = plane[0:3]
            xs[turn, 1, group, slot, 0:3, :] = plane[NX - 3 : NX]
            mine = jnp.logical_and(lane >= slot * 6, lane < slot * 6 + 6)
            packed = jnp.where(mine, pltpu.roll(plane, slot * 6 + 3, 1), packed)
        ys[turn, group] = packed

    def interior(source):
        return lambda plane: source[plane, PAD : PAD + NX, :]

    def x_copy(turn, group, side):
        return pltpu.make_async_remote_copy(
            src_ref=xs.at[turn, side, group],
            dst_ref=xr.at[turn, 1 - side, group],
            send_sem=xs_sem.at[turn, side, group],
            recv_sem=xr_sem.at[turn, 1 - side, group],
            device_id={"tile": tile + (1 if side else -1)},
            device_id_type=MESH,
        )

    def y_copy(turn, group, side):
        return pltpu.make_async_remote_copy(
            src_ref=ys.at[turn, group],
            dst_ref=yr.at[turn, 1 - side, group],
            send_sem=ys_sem.at[turn, side, group],
            recv_sem=yr_sem.at[turn, 1 - side, group],
            device_id={"band": band + (1 if side else -1)},
            device_id_type=MESH,
        )

    has = (
        (tile > 0, band > 0),
        (tile < TILES - 1, band < BANDS - 1),
    )

    def send_edges(turn, group):
        for side in range(2):

            @pl.when(has[side][0])
            def _():
                x_copy(turn, group, side).start()

            @pl.when(has[side][1])
            def _():
                y_copy(turn, group, side).start()

    def await_edges(turn, group):
        for side in range(2):

            @pl.when(has[side][0])
            def _():
                x_copy(turn, group, 1 - side).wait_recv()

            @pl.when(has[side][1])
            def _():
                y_copy(turn, group, 1 - side).wait_recv()

    def merged_halo(turn, group):
        return jnp.where(low_lane, yr[turn, 0, group], yr[turn, 1, group])

    def fill_pads(turn, group, source):
        for f in range(FIELDS):
            for inner in range(GLEV):
                plane, slot = f * LEV + group * GLEV + inner, f * GLEV + inner
                source[plane, PAD - 3 : PAD, :] = xr[turn, 0, group, slot, 0:3, :]
                source[plane, PAD + NX : PAD + NX + 3, :] = xr[turn, 1, group, slot, 0:3, :]

    def edges_sent(turn, group):
        for side in range(2):

            @pl.when(has[side][0])
            def _():
                x_copy(turn, group, side).wait_send()

            @pl.when(has[side][1])
            def _():
                y_copy(turn, group, side).wait_send()


    def advance(group, source, finish):
        halo = y_halo[...]
        for slot in range(SLOTS):
            place = (slot % GLEV) * FIELDS + slot // GLEV
            plane = (slot // GLEV) * LEV + group * GLEV + slot % GLEV
            high, low = split(source[plane, PAD : PAD + NX, :])
            halo_high, halo_low = split(pltpu.roll(halo, 128 - slot * 6, 1) if slot else halo)
            operand[place * NX : (place + 1) * NX, :] = jnp.concatenate(
                [high, low, halo_high, halo_low], axis=1
            )


        for inner in range(GLEV):
            level = group * GLEV + inner
            chunk = 16
            own = pl.ds(inner * FIELDS * NX, FIELDS * NX)
            diffs[own, :] = dot(operand[own, :], stencil[...])
            for at in range(0, NX, chunk):
                east = source[level, PAD + at : PAD + at + chunk, :] * (1.0 / 60.0)
                north = source[LEV + level, PAD + at : PAD + at + chunk, :] * (1.0 / 60.0)
                east_size = jnp.abs(east)
                north_size = jnp.abs(north)
                for f in range(FIELDS):
                    plane = f * LEV + level

                    def cell(offset):
                        return source[plane, PAD + at + offset : PAD + at + offset + chunk, :]

                    up1, up2, up3 = cell(1), cell(2), cell(3)
                    down1, down2, down3 = cell(-1), cell(-2), cell(-3)
                    central = 45.0 * (up1 - down1) - 9.0 * (up2 - down2) + (up3 - down3)
                    smooth = (
                        (up3 + down3)
                        - 6.0 * (up2 + down2)
                        + 15.0 * (up1 + down1)
                        - 20.0 * cell(0)
                    )
                    first = (inner * FIELDS + f) * NX + at
                    central_y = diffs[pl.ds(first, chunk), 0:NY]
                    smooth_y = diffs[pl.ds(first, chunk), NY : 2 * NY]
                    value = (east_size * smooth - east * central) + (
                        north_size * smooth_y - north * central_y
                    )
                    finish(f, plane, at, chunk, value)


    def turbines(group):
        counts = count[...].astype(F32)
        kinds = kind[...]

        @pl.loop(0, GLEV)
        def _(inner):
            level = group * GLEV + inner
            rate = jnp.full((NX, NY), drag_coeff[0, level])
            growth = jnp.full((NX, NY), tke_coeff[0, level])
            for k in range(1, NTYPE):
                here = kinds == k
                rate = jnp.where(here, drag_coeff[k, level], rate)
                growth = jnp.where(here, tke_coeff[k, level], growth)
            east = q0[level, PAD : PAD + NX, :]
            north = q0[LEV + level, PAD : PAD + NX, :]
            speed = jnp.sqrt(east * east + north * north)
            rate = counts * rate * speed
            tke[level] = tke[level] + counts * growth * speed * speed * speed
            drag[level] = -(rate * east)
            drag[LEV + level] = -(rate * north)

    def tke_copy(group):
        rows = pl.ds(group * GLEV, GLEV)
        return pltpu.make_async_copy(tke.at[rows], tke_out.at[rows], out_sem.at[3, group])


    for copy in inputs[:3]:
        copy.wait()

    @pl.loop(0, GROUPS)
    def _(group):
        pack_edges(0, group, interior(q0))

    for copy in inputs[3:6] + table_copies:
        copy.wait()

    @pl.loop(0, BANDS)
    def _(to):
        rows = []
        for f in range(FIELDS):
            part = pl.ds(f * LEV + 2 * to, 2)
            gap = target[part] - q0[part, PAD : PAD + NX, :]
            rows.append(gap.reshape(2 * NX, NY))
        high, low = split(jnp.concatenate(rows, axis=0))
        along_x = quarters(dot(x_forward[...], jnp.concatenate([high, low], axis=1)), 128, NY)
        both = lax.dot_general(
            y_forward[...],
            jnp.concatenate(split(along_x), axis=1),
            (((1,), (1,)), ((), ())),
            preferred_element_type=F32,
        )
        s1[to] = both[:RY] + both[RY:]

    pl.semaphore_wait(barrier, BANDS - 1 + TILES - 1)

    @pl.loop(0, GROUPS)
    def _(group):
        send_edges(0, group)

    def partners(axis):
        if axis == "band":
            return [lax.rem(band + step, BANDS) for step in (4, 3, 5, 2, 6, 1, 7)]
        apart = sorted(
            ((dx, dz) for dx in range(4) for dz in range(4) if dx or dz),
            key=lambda at: -(min(at[0], 4 - at[0]) + min(at[1], 4 - at[1])),
        )
        x, z = tile // 4, lax.rem(tile, 4)
        return [lax.rem(x + dx, 4) * 4 + lax.rem(z + dz, 4) for dx, dz in apart]

    def outgoing(axis, me, source, into, send_sem, recv_sem, other):
        return pltpu.make_async_remote_copy(
            src_ref=source.at[other],
            dst_ref=into.at[me],
            send_sem=send_sem.at[other],
            recv_sem=recv_sem.at[me],
            device_id={axis: other},
            device_id_type=MESH,
        )

    def send_all(axis, me, source, into, send_sem, recv_sem):
        for other in partners(axis):
            outgoing(axis, me, source, into, send_sem, recv_sem, other).start()
        into[me] = source[me]

    def receive_all(axis, me, source, into, send_sem, recv_sem):
        for other in partners(axis)[::-1]:
            pltpu.make_async_remote_copy(
                src_ref=source.at[other],
                dst_ref=into.at[other],
                send_sem=send_sem.at[other],
                recv_sem=recv_sem.at[other],
                device_id={axis: other},
                device_id_type=MESH,
            ).wait_recv()

    def sent_all(axis, me, source, into, send_sem, recv_sem):
        for other in partners(axis):
            outgoing(axis, me, source, into, send_sem, recv_sem, other).wait_send()

    phase1 = ("band", band, s1, r1, s1_sem, r1_sem)
    phase2 = ("tile", tile, s2, r2, s2_sem, r2_sem)
    phase3 = ("tile", tile, s3, r3, s3_sem, r3_sem)
    phase4 = ("band", band, s4, r4, s4_sem, r4_sem)

    send_all(*phase1)
    for copy in inputs[6:]:
        copy.wait()

    def first_finish(f, plane, at, chunk, value):
        if f < 2:
            value = value + drag[plane, at : at + chunk, :]
        partial[plane, at : at + chunk, :] = value

    def first_stage(group):
        turbines(group)
        tke_copy(group).start()
        await_edges(0, group)
        fill_pads(0, group, q0)
        halo = merged_halo(0, group)
        y_first[group] = halo
        y_halo[...] = halo
        advance(group, q0, first_finish)
        pack_edges(1, group, lambda plane: partial[plane])
        send_edges(1, group)

    first_stage(0)
    receive_all(*phase1)

    received = r1[...].reshape(BANDS * RY, 128)
    columns = jnp.concatenate(split(received), axis=1)
    s2[...] = quarters(dot(m_forward[...], columns), MODES, 128).reshape(TILES, 8, 128)
    send_all(*phase2)
    first_stage(1)
    receive_all(*phase2)

    lane8 = lax.broadcasted_iota(jnp.int32, (8, 128), 1)
    inside = [
        jnp.logical_and(lane8 >= RX * i, lane8 < RX * (i + 1)) for i in range(PER)
    ]
    blocks = [r2[t] for t in range(TILES)]
    rows = []
    for p in range(PLANES):
        parts = []
        for first in range(0, TILES, PER):
            value = jnp.zeros((8, 128), F32)
            for i, t in enumerate(range(first, min(first + PER, TILES))):
                moved = pltpu.roll(blocks[t], (RX * (i - p)) % 128, 1)
                value = jnp.where(inside[i], moved, value)
            parts.append(value)
        rows.append(jnp.concatenate(parts, axis=1))
    packed = jnp.concatenate(split(jnp.concatenate(rows, axis=0)), axis=0)
    spectra = quarters(dot(packed, k_forward[...]), 8 * PLANES, MODES)
    mine = pl.ds(pl.multiple_of(tile * 8, 8), 8)
    weight = weights[mine, :]
    east_number = number_k[...]
    north_number = number_m[mine, :]
    masks = []
    for inner in range(2):
        keep = jnp.logical_and(
            east_number <= cutoffs[0, 2 * band + inner],
            north_number <= cutoffs[1, 2 * band + inner],
        )
        masks.append(jnp.where(keep, weight, 0.0))
    spectra = spectra * jnp.concatenate(masks * FIELDS, axis=0)
    high, low = split(spectra)
    back = dot(jnp.concatenate([high, low], axis=0), k_back[...])
    back = quarters(back, 8 * PLANES, 384)
    for t in range(TILES):
        first = 128 * (t // PER)
        value = jnp.zeros((8, 128), F32)
        for p in range(PLANES):
            moved = pltpu.roll(
                back[8 * p : 8 * p + 8, first : first + 128], (RX * (p - t % PER)) % 128, 1
            )
            value = jnp.where(inside[p], moved, value)
        s3[t] = value
    send_all(*phase3)
    first_stage(2)
    receive_all(*phase3)

    received = r3[...].reshape(MODES, 128)
    back = quarters(dot(m_back[...], jnp.concatenate(split(received), axis=1)), BANDS * RY, 128)
    s4[...] = back.reshape(BANDS, RY, 128)
    send_all(*phase4)
    first_stage(3)
    receive_all(*phase4)

    for half in range(2):
        columns = r4[4 * half : 4 * half + 4].reshape(4 * RY, 128).T
        wide = dot(jnp.concatenate(split(columns), axis=0), y_back[...])
        wide = quarters(wide, 128, 8 * NY)
        for i in range(4):
            modes[4 * half + i] = wide[:, i * NY : (i + 1) * NY]
            outer_modes[4 * half + i] = wide[:, (4 + i) * NY : (5 + i) * NY] * own_slot[i % 2]

    third = 1.0 / 3.0
    inside_x = [jnp.where(flag[0], 1.0, 0.0) for flag in has]
    inside_y = jnp.where(
        low_lane, jnp.where(has[0][1], 1.0, 0.0), jnp.where(has[1][1], 1.0, 0.0)
    )

    def second_finish(f, plane, at, chunk, value):
        q2[plane, PAD + at : PAD + at + chunk, :] = q0[
            plane, PAD + at : PAD + at + chunk, :
        ] + 0.5 * (value + force[plane, at : at + chunk, :])

    @pl.loop(0, GROUPS)
    def _(group):
        await_edges(1, group)
        outer = jnp.zeros((NX, 128), F32)
        for pair in range(2):
            high, low = split(modes[2 * group + pair])
            smooth_part = dot(x_back[...], jnp.concatenate([high, low, high], axis=0))
            high, low = split(outer_modes[2 * group + pair])
            outer = outer + dot(x_shared[...], jnp.concatenate([high, low, high], axis=0))
            for f in range(FIELDS):
                for inner in range(2):
                    plane = f * LEV + group * GLEV + 2 * pair + inner
                    slot = f * GLEV + 2 * pair + inner
                    p = 2 * f + inner
                    nudge = smooth_part[p * NX : (p + 1) * NX]
                    if f < 2:
                        force[plane] = nudge + drag[plane]
                    else:
                        force[plane] = nudge
                    q1[plane, PAD : PAD + NX, :] = q0[plane, PAD : PAD + NX, :] + third * (
                        nudge + partial[plane]
                    )
                    for side, into in ((0, PAD - 3), (1, PAD + NX)):
                        first = PLANES * NX + 8 * p + 4 * side
                        q1[plane, into : into + 3, :] = xr[0, side, group, slot, 0:3, :] + third * (
                            smooth_part[first : first + 3] * inside_x[side]
                            + xr[1, side, group, slot, 0:3, :]
                        )
        y_halo[...] = y_first[group] + third * (outer * inside_y + merged_halo(1, group))

        advance(group, q1, second_finish)
        pack_edges(2, group, interior(q2))
        send_edges(2, group)

    def third_finish(f, plane, at, chunk, value):
        result[plane, at : at + chunk, :] = q0[plane, PAD + at : PAD + at + chunk, :] + (
            value + force[plane, at : at + chunk, :]
        )

    def out_copy(f, group):
        rows = pl.ds(group * GLEV, GLEV)
        into = (east_out, north_out, theta_out)[f]
        return pltpu.make_async_copy(
            result.at[pl.ds(f * LEV + group * GLEV, GLEV)], into.at[rows], out_sem.at[f, group]
        )

    @pl.loop(0, GROUPS)
    def _(group):
        await_edges(2, group)
        fill_pads(2, group, q2)
        y_halo[...] = merged_halo(2, group)
        advance(group, q2, third_finish)
        for f in range(FIELDS):
            out_copy(f, group).start()

    for phase in (phase1, phase2, phase3, phase4):
        sent_all(*phase)

    @pl.loop(0, GROUPS)
    def _(group):
        for turn in range(3):
            edges_sent(turn, group)
        for f in range(FIELDS):
            out_copy(f, group).wait()
        tke_copy(group).wait()


PARTS = 4


def deliver(*refs):
    sources, results, held, in_sems, out_sems = refs[:4], refs[4:8], refs[8], refs[9], refs[10]
    inward, outward = [], []
    for j in range(PARTS):
        rows = pl.ds(j * (LEV // PARTS), LEV // PARTS)
        for i in range(4):
            inward.append(
                pltpu.make_async_copy(sources[i].at[rows], held.at[i, rows], in_sems.at[i, j])
            )
            outward.append(
                pltpu.make_async_copy(held.at[i, rows], results[i].at[rows], out_sems.at[i, j])
            )
    for copy in inward:
        copy.start()
    for first, second in zip(inward, outward):
        first.wait()
        second.start()
    for copy in outward:
        copy.wait()


def shards(*arguments):
    tables = [jnp.asarray(table) for table in make_tables()]
    field = jax.ShapeDtypeStruct((LEV, NX, NY), F32)
    anywhere = pl.BlockSpec(memory_space=pl.ANY)
    smem = pl.BlockSpec(memory_space=pltpu.SMEM)
    padded = pltpu.VMEM((FIELDS * LEV, NX + 2 * PAD, NY), F32)
    planes = pltpu.VMEM((FIELDS * LEV, NX, NY), F32)
    dma = pltpu.SemaphoreType.DMA
    outcome = pl.pallas_call(
        kernel,
        out_shape=(field,) * 4,
        in_specs=[anywhere] * 9 + [smem] * 3 + [anywhere] * TABLES,
        out_specs=(anywhere,) * 4,
        scratch_shapes=[pltpu.VMEM(table.shape, table.dtype) for table in tables]
        + [
            padded,
            padded,
            padded,
            planes,
            pltpu.VMEM((LEV, NX, NY), F32),
            pltpu.VMEM((NX, NY), jnp.int32),
            pltpu.VMEM((NX, NY), jnp.int32),
            planes,
            pltpu.VMEM((2 * LEV, NX, NY), F32),
            planes,
            planes,
            pltpu.VMEM((SLOTS * NX, 2 * NY), F32),
            pltpu.VMEM((NX, 128), F32),
            pltpu.VMEM((3, 2, GROUPS, SLOTS, 4, 128), F32),
            pltpu.VMEM((3, 2, GROUPS, SLOTS, 4, 128), F32),
            pltpu.VMEM((3, GROUPS, NX, 128), F32),
            pltpu.VMEM((3, 2, GROUPS, NX, 128), F32),
            pltpu.VMEM((BANDS, RY, 128), F32),
            pltpu.VMEM((BANDS, RY, 128), F32),
            pltpu.VMEM((TILES, 8, 128), F32),
            pltpu.VMEM((TILES, 8, 128), F32),
            pltpu.VMEM((TILES, 8, 128), F32),
            pltpu.VMEM((TILES, 8, 128), F32),
            pltpu.VMEM((BANDS, RY, 128), F32),
            pltpu.VMEM((BANDS, RY, 128), F32),
            pltpu.VMEM((BANDS, 128, NY), F32),
            pltpu.VMEM((BANDS, 128, NY), F32),
            pltpu.VMEM((SLOTS * NX, 4 * NY), BF),
            pltpu.VMEM((GROUPS, NX, 128), F32),
            dma((9,)),
            dma((TABLES,)),
            dma((4, GROUPS)),
            dma((3, 2, GROUPS)),
            dma((3, 2, GROUPS)),
            dma((3, 2, GROUPS)),
            dma((3, 2, GROUPS)),
            dma((BANDS,)),
            dma((BANDS,)),
            dma((TILES,)),
            dma((TILES,)),
            dma((TILES,)),
            dma((TILES,)),
            dma((BANDS,)),
            dma((BANDS,)),
        ],
        compiler_params=pltpu.CompilerParams(
            collective_id=0, has_side_effects=True, vmem_limit_bytes=61 * 1024 * 1024
        ),
        cost_estimate=pl.CostEstimate(
            flops=10**9, bytes_accessed=6 * 2**20, transcendentals=LEV * NX * NY
        ),
        name="step",
    )(*arguments, *tables)
    return pl.pallas_call(
        deliver,
        out_shape=(field,) * 4,
        in_specs=[anywhere] * 4,
        out_specs=(anywhere,) * 4,
        scratch_shapes=[
            pltpu.VMEM((4, LEV, NX, NY), F32),
            dma((4, PARTS)),
            dma((4, PARTS)),
        ],
        compiler_params=pltpu.CompilerParams(vmem_limit_bytes=61 * 1024 * 1024),
        name="deliver",
    )(*outcome)


def solution(mesh):
    field = P(None, "tile", "band")
    column = P("tile", "band")
    in_specs = (field,) * 7 + (column,) * 2 + (P(),) * 3
    return jax.shard_map(
        shards, mesh=mesh, in_specs=in_specs, out_specs=(field,) * 4, check_vma=False
    )
```

```python
import functools

import jax
import jax.numpy as jnp
import ml_dtypes
import numpy as np
from jax import lax
from jax.experimental import pallas as pl
from jax.experimental.pallas import tpu as pltpu
from jax.sharding import PartitionSpec as P

KMAX = 64
MODES = 2 * KMAX
NTYPE = 8
LEV = 16
FIELDS = 3
BANDS = 8
TILES = 16
NX = 64
NY = 128
RX = 21
RY = 32
PLANES = 6
GROUPS = 4
GLEV = LEV // GROUPS
SLOTS = FIELDS * GLEV
PER = 6
PAD = 8
TABLES = 14
MESH = pl.DeviceIdType.MESH
BF = jnp.bfloat16
F32 = jnp.float32


def wavenumbers():
    index = np.arange(MODES)
    return np.where(index < KMAX, index, index - KMAX + 1)


def basis(extent, positions):
    number = wavenumbers()
    angle = 2 * np.pi * ((number[:, None] * positions[None, :]) % extent) / extent
    return np.where((np.arange(MODES) < KMAX)[:, None], np.cos(angle), np.sin(angle))


def window(length, extent, rank):
    index = np.arange(length)
    half = (KMAX + 0.5) / extent
    diagonal = ((length - 1 - 2 * index) / 2) ** 2 * np.cos(2 * np.pi * half)
    beside = index[1:] * (length - index[1:]) / 2
    _, vectors = np.linalg.eigh(np.diag(diagonal) + np.diag(beside, 1) + np.diag(beside, -1))
    vectors = vectors[:, ::-1][:, :rank]
    largest = vectors[np.argmax(np.abs(vectors) > 0.02, axis=0), np.arange(rank)]
    return vectors * np.sign(largest)


def halves(table):
    high = table.astype(np.float32).astype(ml_dtypes.bfloat16)
    low = (table - high.astype(np.float64)).astype(np.float32).astype(ml_dtypes.bfloat16)
    return high, low


def stencil_table():
    central = {1: 45.0, -1: -45.0, 2: -9.0, -2: 9.0, 3: 1.0, -3: -1.0}
    smooth = {3: 1.0, -3: 1.0, 2: -6.0, -2: -6.0, 1: 15.0, -1: 15.0, 0: -20.0}
    inner = np.zeros((NY, 2 * NY))
    outer = np.zeros((NY, 2 * NY))
    for column, taps in ((0, central), (NY, smooth)):
        for y in range(NY):
            for offset, tap in taps.items():
                at = y + offset
                if 0 <= at < NY:
                    inner[at, column + y] = tap
                elif at < 0:
                    outer[at + 3, column + y] = tap
                else:
                    outer[at - NY + 3, column + y] = tap
    return np.concatenate([inner, inner, outer, outer]).astype(ml_dtypes.bfloat16)


def make_tables():
    east_n, north_n = NX * TILES, NY * BANDS
    vx = window(NX, east_n, RX)
    vy = window(NY, north_n, RY)
    wx = window(NX + 6, east_n, RX)
    wy = window(NY + 6, north_n, RY)
    cells_x = np.arange(NX + 6) - 3
    cells_y = np.arange(NY + 6) - 3
    ux = [basis(east_n, NX * t + np.arange(NX)) @ vx for t in range(TILES)]
    uy = [basis(north_n, NY * b + np.arange(NY)) @ vy for b in range(BANDS)]

    block = np.zeros((PLANES * NX, 128))
    for p in range(PLANES):
        block[p * NX : (p + 1) * NX, p * RX : (p + 1) * RX] = vx
    high, low = halves(block.T)
    x_forward = np.concatenate([high, low], axis=0)
    rows = PLANES * NX
    block = np.zeros((rows + PLANES * 8, 128))
    for p in range(PLANES):
        columns = slice(p * RX, (p + 1) * RX)
        block[p * NX : (p + 1) * NX, columns] = 0.5 * wx[3 : NX + 3]
        block[rows + 8 * p : rows + 8 * p + 3, columns] = 0.5 * wx[:3]
        block[rows + 8 * p + 4 : rows + 8 * p + 7, columns] = 0.5 * wx[NX + 3 :]
    high, low = halves(block)
    x_back = np.concatenate([high, high, low], axis=1)
    shared = sum(block[p * NX : (p + 1) * NX] for p in range(PLANES))
    high, low = halves(shared)
    x_shared = np.concatenate([high, high, low], axis=1)

    high, low = halves(vy.T)
    y_forward = np.concatenate(
        [np.concatenate([high, high], axis=1), np.concatenate([low, 0 * low], axis=1)], axis=0
    )
    both_y = np.zeros((2 * NY, RY))
    both_y[:NY] = wy[3 : NY + 3]
    both_y[NY : NY + 6 * SLOTS] = np.tile(np.concatenate([wy[:3], wy[NY + 3 :]]), (SLOTS, 1))
    high, low = halves(both_y)
    y_back = np.concatenate([high, high, low, 0 * low], axis=1)
    own_slot = np.zeros((2, 128, 128), np.float32)
    for pair in range(2):
        for p in range(PLANES):
            slot = (p // 2) * GLEV + 2 * pair + p % 2
            own_slot[pair, 6 * slot : 6 * slot + 6, p * RX : (p + 1) * RX] = 1

    uy_all = np.concatenate(uy, axis=1)
    m_forward = np.concatenate(halves(uy_all), axis=0)
    uy = [basis(north_n, NY * b + cells_y) @ wy for b in range(BANDS)]
    m_back = np.concatenate(halves(np.concatenate(uy, axis=1).T), axis=0)

    ux_all = np.zeros((MODES, 384))
    for t in range(TILES):
        at = 128 * (t // PER) + RX * (t % PER)
        ux_all[:, at : at + RX] = ux[t]
    k_forward = np.concatenate(halves(ux_all.T), axis=1)
    for t in range(TILES):
        at = 128 * (t // PER) + RX * (t % PER)
        ux_all[:, at : at + RX] = basis(east_n, NX * t + cells_x) @ wx
    k_back = np.concatenate(halves(ux_all), axis=1)

    number = wavenumbers()
    weight_k = np.where(number == 0, 1.0, 2.0) / east_n
    weight_m = np.where(number == 0, 1.0, 2.0) / north_n
    weights = (weight_m[:, None] * weight_k[None, :]).astype(np.float32)
    number_k = np.broadcast_to(number[None, :], (8, MODES)).astype(np.int32)
    number_m = np.broadcast_to(number[:, None], (MODES, MODES)).astype(np.int32)
    return (
        x_forward,
        y_forward,
        m_forward,
        k_forward,
        k_back,
        m_back,
        y_back,
        x_back,
        x_shared,
        own_slot,
        stencil_table(),
        weights,
        number_k,
        number_m,
    )


def split(value):
    high = value.astype(BF)
    low = (value - high.astype(F32)).astype(BF)
    return high, low


def dot(a, b):
    return lax.dot_general(a, b, (((1,), (0,)), ((), ())), preferred_element_type=F32)


def quarters(product, rows, columns):
    return (product[:rows, :columns] + product[:rows, columns:]) + (
        product[rows:, :columns] + product[rows:, columns:]
    )


def kernel(
    wind_east,
    wind_north,
    theta_pert,
    tke_field,
    target_east,
    target_north,
    target_theta,
    turbine_count,
    turbine_type,
    drag_coeff,
    tke_coeff,
    cutoffs,
    *rest,
):
    table_sources, rest = rest[:TABLES], rest[TABLES:]
    tables, rest = rest[4 : 4 + TABLES], rest[:4] + rest[4 + TABLES :]
    step_body(
        wind_east,
        wind_north,
        theta_pert,
        tke_field,
        target_east,
        target_north,
        target_theta,
        turbine_count,
        turbine_type,
        drag_coeff,
        tke_coeff,
        cutoffs,
        table_sources,
        tables,
        *rest,
    )


def step_body(
    wind_east,
    wind_north,
    theta_pert,
    tke_field,
    target_east,
    target_north,
    target_theta,
    turbine_count,
    turbine_type,
    drag_coeff,
    tke_coeff,
    cutoffs,
    table_sources,
    tables,
    east_out,
    north_out,
    theta_out,
    tke_out,
    q0,
    q1,
    q2,
    target,
    tke,
    count,
    kind,
    partial,
    drag,
    force,
    result,
    diffs,
    y_halo,
    xs,
    xr,
    ys,
    yr,
    s1,
    r1,
    s2,
    r2,
    s3,
    r3,
    s4,
    r4,
    modes,
    outer_modes,
    operand,
    y_first,
    in_sem,
    table_sem,
    out_sem,
    xs_sem,
    xr_sem,
    ys_sem,
    yr_sem,
    s1_sem,
    r1_sem,
    s2_sem,
    r2_sem,
    s3_sem,
    r3_sem,
    s4_sem,
    r4_sem,
):
    (
        x_forward,
        y_forward,
        m_forward,
        k_forward,
        k_back,
        m_back,
        y_back,
        x_back,
        x_shared,
        own_slot,
        stencil,
        weights,
        number_k,
        number_m,
    ) = tables
    band = lax.axis_index("band")
    tile = lax.axis_index("tile")

    def field_copies(group):
        rows = pl.ds(group * GLEV, GLEV)
        copies = []
        for f, source in enumerate((wind_east, wind_north, theta_pert)):
            into = q0.at[pl.ds(f * LEV + group * GLEV, GLEV), pl.ds(PAD, NX), :]
            copies.append(pltpu.make_async_copy(source.at[rows], into, in_sem.at[f, group]))
        for f, source in enumerate((target_east, target_north, target_theta)):
            into = target.at[pl.ds(f * LEV + group * GLEV, GLEV)]
            copies.append(pltpu.make_async_copy(source.at[rows], into, in_sem.at[3 + f, group]))
        return copies

    others = [
        pltpu.make_async_copy(source, into, in_sem.at[6 + i, 0])
        for i, (source, into) in enumerate(
            ((tke_field, tke), (turbine_count, count), (turbine_type, kind))
        )
    ]
    table_copies = [
        pltpu.make_async_copy(source, into, table_sem.at[i])
        for i, (source, into) in enumerate(zip(table_sources, tables))
    ]
    for copy in table_copies[:2]:
        copy.start()

    for group in range(GROUPS):
        for copy in field_copies(group):
            copy.start()
    for copy in others + table_copies[2:]:
        copy.start()

    @pl.when(tile == 0)
    def _():
        xr[:, 0] = jnp.zeros((3, GROUPS, SLOTS, 4, 128), F32)

    @pl.when(tile == TILES - 1)
    def _():
        xr[:, 1] = jnp.zeros((3, GROUPS, SLOTS, 4, 128), F32)

    @pl.when(band == 0)
    def _():
        yr[:, 0] = jnp.zeros((3, GROUPS, NX, 128), F32)

    @pl.when(band == BANDS - 1)
    def _():
        yr[:, 1] = jnp.zeros((3, GROUPS, NX, 128), F32)

    barrier = pltpu.get_barrier_semaphore()
    for step in range(1, BANDS):
        pl.semaphore_signal(
            barrier, inc=1, device_id={"band": lax.rem(band + step, BANDS)}, device_id_type=MESH
        )
    for step in range(1, TILES):
        pl.semaphore_signal(
            barrier, inc=1, device_id={"tile": lax.rem(tile + step, TILES)}, device_id_type=MESH
        )

    lane = lax.broadcasted_iota(jnp.int32, (NX, 128), 1)
    low_lane = lax.rem(lane, 6) < 3


    def pack_edges(turn, group, plane_of):
        packed = jnp.zeros((NX, 128), F32)
        for slot in range(SLOTS):
            plane = plane_of((slot // GLEV) * LEV + group * GLEV + slot % GLEV)
            xs[turn, 0, group, slot, 0:3, :] = plane[0:3]
            xs[turn, 1, group, slot, 0:3, :] = plane[NX - 3 : NX]
            mine = jnp.logical_and(lane >= slot * 6, lane < slot * 6 + 6)
            packed = jnp.where(mine, pltpu.roll(plane, slot * 6 + 3, 1), packed)
        ys[turn, group] = packed

    def interior(source):
        return lambda plane: source[plane, PAD : PAD + NX, :]

    def x_copy(turn, group, side):
        return pltpu.make_async_remote_copy(
            src_ref=xs.at[turn, side, group],
            dst_ref=xr.at[turn, 1 - side, group],
            send_sem=xs_sem.at[turn, side, group],
            recv_sem=xr_sem.at[turn, 1 - side, group],
            device_id={"tile": tile + (1 if side else -1)},
            device_id_type=MESH,
        )

    def y_copy(turn, group, side):
        return pltpu.make_async_remote_copy(
            src_ref=ys.at[turn, group],
            dst_ref=yr.at[turn, 1 - side, group],
            send_sem=ys_sem.at[turn, side, group],
            recv_sem=yr_sem.at[turn, 1 - side, group],
            device_id={"band": band + (1 if side else -1)},
            device_id_type=MESH,
        )

    has = (
        (tile > 0, band > 0),
        (tile < TILES - 1, band < BANDS - 1),
    )

    def send_edges(turn, group):
        for side in range(2):

            @pl.when(has[side][0])
            def _():
                x_copy(turn, group, side).start()

            @pl.when(has[side][1])
            def _():
                y_copy(turn, group, side).start()

    def await_edges(turn, group):
        for side in range(2):

            @pl.when(has[side][0])
            def _():
                x_copy(turn, group, 1 - side).wait_recv()

            @pl.when(has[side][1])
            def _():
                y_copy(turn, group, 1 - side).wait_recv()

    def merged_halo(turn, group):
        return jnp.where(low_lane, yr[turn, 0, group], yr[turn, 1, group])

    def fill_pads(turn, group, source):
        for f in range(FIELDS):
            for inner in range(GLEV):
                plane, slot = f * LEV + group * GLEV + inner, f * GLEV + inner
                source[plane, PAD - 3 : PAD, :] = xr[turn, 0, group, slot, 0:3, :]
                source[plane, PAD + NX : PAD + NX + 3, :] = xr[turn, 1, group, slot, 0:3, :]

    def edges_sent(turn, group):
        for side in range(2):

            @pl.when(has[side][0])
            def _():
                x_copy(turn, group, side).wait_send()

            @pl.when(has[side][1])
            def _():
                y_copy(turn, group, side).wait_send()


    def advance(group, source, finish):
        halo = y_halo[...]
        for slot in range(SLOTS):
            place = (slot % GLEV) * FIELDS + slot // GLEV
            plane = (slot // GLEV) * LEV + group * GLEV + slot % GLEV
            high, low = split(source[plane, PAD : PAD + NX, :])
            halo_high, halo_low = split(pltpu.roll(halo, 128 - slot * 6, 1) if slot else halo)
            operand[place * NX : (place + 1) * NX, :] = jnp.concatenate(
                [high, low, halo_high, halo_low], axis=1
            )


        for inner in range(GLEV):
            level = group * GLEV + inner
            chunk = 16
            own = pl.ds(inner * FIELDS * NX, FIELDS * NX)
            diffs[own, :] = dot(operand[own, :], stencil[...])
            for at in range(0, NX, chunk):
                east = source[level, PAD + at : PAD + at + chunk, :] * (1.0 / 60.0)
                north = source[LEV + level, PAD + at : PAD + at + chunk, :] * (1.0 / 60.0)
                east_size = jnp.abs(east)
                north_size = jnp.abs(north)
                for f in range(FIELDS):
                    plane = f * LEV + level

                    def cell(offset):
                        return source[plane, PAD + at + offset : PAD + at + offset + chunk, :]

                    up1, up2, up3 = cell(1), cell(2), cell(3)
                    down1, down2, down3 = cell(-1), cell(-2), cell(-3)
                    central = 45.0 * (up1 - down1) - 9.0 * (up2 - down2) + (up3 - down3)
                    smooth = (
                        (up3 + down3)
                        - 6.0 * (up2 + down2)
                        + 15.0 * (up1 + down1)
                        - 20.0 * cell(0)
                    )
                    first = (inner * FIELDS + f) * NX + at
                    central_y = diffs[pl.ds(first, chunk), 0:NY]
                    smooth_y = diffs[pl.ds(first, chunk), NY : 2 * NY]
                    value = (east_size * smooth - east * central) + (
                        north_size * smooth_y - north * central_y
                    )
                    finish(f, plane, at, chunk, value)


    def turbines(group):
        counts = count[...].astype(F32)
        kinds = kind[...]

        @pl.loop(0, GLEV)
        def _(inner):
            level = group * GLEV + inner
            rate = jnp.full((NX, NY), drag_coeff[0, level])
            growth = jnp.full((NX, NY), tke_coeff[0, level])
            for k in range(1, NTYPE):
                here = kinds == k
                rate = jnp.where(here, drag_coeff[k, level], rate)
                growth = jnp.where(here, tke_coeff[k, level], growth)
            east = q0[level, PAD : PAD + NX, :]
            north = q0[LEV + level, PAD : PAD + NX, :]
            speed = jnp.sqrt(east * east + north * north)
            rate = counts * rate * speed
            tke[level] = tke[level] + counts * growth * speed * speed * speed
            drag[level] = -(rate * east)
            drag[LEV + level] = -(rate * north)

    def tke_copy(group):
        rows = pl.ds(group * GLEV, GLEV)
        return pltpu.make_async_copy(tke.at[rows], tke_out.at[rows], out_sem.at[3, group])


    for copy in table_copies[:2]:
        copy.wait()

    def coefficients(to):
        rows = []
        for f in range(FIELDS):
            part = pl.ds(f * LEV + 2 * to, 2)
            gap = target[part] - q0[part, PAD : PAD + NX, :]
            rows.append(gap.reshape(2 * NX, NY))
        high, low = split(jnp.concatenate(rows, axis=0))
        along_x = quarters(dot(x_forward[...], jnp.concatenate([high, low], axis=1)), 128, NY)
        both = lax.dot_general(
            y_forward[...],
            jnp.concatenate(split(along_x), axis=1),
            (((1,), (1,)), ((), ())),
            preferred_element_type=F32,
        )
        s1[to] = both[:RY] + both[RY:]

    @pl.loop(0, GROUPS)
    def _(group):
        for copy in field_copies(group):
            copy.wait()
        for pair in range(2):
            coefficients(2 * group + pair)

    pl.semaphore_wait(barrier, BANDS - 1 + TILES - 1)

    def partners(axis):
        if axis == "band":
            return [lax.rem(band + step, BANDS) for step in (4, 3, 5, 2, 6, 1, 7)]
        apart = sorted(
            ((dx, dz) for dx in range(4) for dz in range(4) if dx or dz),
            key=lambda at: -(min(at[0], 4 - at[0]) + min(at[1], 4 - at[1])),
        )
        x, z = tile // 4, lax.rem(tile, 4)
        return [lax.rem(x + dx, 4) * 4 + lax.rem(z + dz, 4) for dx, dz in apart]

    def outgoing(axis, me, source, into, send_sem, recv_sem, other):
        return pltpu.make_async_remote_copy(
            src_ref=source.at[other],
            dst_ref=into.at[me],
            send_sem=send_sem.at[other],
            recv_sem=recv_sem.at[me],
            device_id={axis: other},
            device_id_type=MESH,
        )

    def send_all(axis, me, source, into, send_sem, recv_sem):
        for other in partners(axis):
            outgoing(axis, me, source, into, send_sem, recv_sem, other).start()
        into[me] = source[me]

    def receive_all(axis, me, source, into, send_sem, recv_sem):
        for other in partners(axis)[::-1]:
            pltpu.make_async_remote_copy(
                src_ref=source.at[other],
                dst_ref=into.at[other],
                send_sem=send_sem.at[other],
                recv_sem=recv_sem.at[other],
                device_id={axis: other},
                device_id_type=MESH,
            ).wait_recv()

    def sent_all(axis, me, source, into, send_sem, recv_sem):
        for other in partners(axis):
            outgoing(axis, me, source, into, send_sem, recv_sem, other).wait_send()

    phase1 = ("band", band, s1, r1, s1_sem, r1_sem)
    phase2 = ("tile", tile, s2, r2, s2_sem, r2_sem)
    phase3 = ("tile", tile, s3, r3, s3_sem, r3_sem)
    phase4 = ("band", band, s4, r4, s4_sem, r4_sem)

    send_all(*phase1)

    @pl.loop(0, GROUPS)
    def _(group):
        pack_edges(0, group, interior(q0))
        send_edges(0, group)

    for copy in others + table_copies[2:]:
        copy.wait()

    @pl.loop(0, GROUPS)
    def _(group):
        turbines(group)
        tke_copy(group).start()

    def first_finish(f, plane, at, chunk, value):
        if f < 2:
            value = value + drag[plane, at : at + chunk, :]
        partial[plane, at : at + chunk, :] = value

    def first_stage(group):
        await_edges(0, group)
        fill_pads(0, group, q0)
        halo = merged_halo(0, group)
        y_first[group] = halo
        y_halo[...] = halo
        advance(group, q0, first_finish)
        pack_edges(1, group, lambda plane: partial[plane])
        send_edges(1, group)

    receive_all(*phase1)

    received = r1[...].reshape(BANDS * RY, 128)
    columns = jnp.concatenate(split(received), axis=1)
    s2[...] = quarters(dot(m_forward[...], columns), MODES, 128).reshape(TILES, 8, 128)
    send_all(*phase2)

    @pl.loop(0, 2)
    def _(group):
        first_stage(group)

    receive_all(*phase2)

    lane8 = lax.broadcasted_iota(jnp.int32, (8, 128), 1)
    inside = [
        jnp.logical_and(lane8 >= RX * i, lane8 < RX * (i + 1)) for i in range(PER)
    ]
    blocks = [r2[t] for t in range(TILES)]
    rows = []
    for p in range(PLANES):
        parts = []
        for first in range(0, TILES, PER):
            value = jnp.zeros((8, 128), F32)
            for i, t in enumerate(range(first, min(first + PER, TILES))):
                moved = pltpu.roll(blocks[t], (RX * (i - p)) % 128, 1)
                value = jnp.where(inside[i], moved, value)
            parts.append(value)
        rows.append(jnp.concatenate(parts, axis=1))
    packed = jnp.concatenate(split(jnp.concatenate(rows, axis=0)), axis=0)
    spectra = quarters(dot(packed, k_forward[...]), 8 * PLANES, MODES)
    mine = pl.ds(pl.multiple_of(tile * 8, 8), 8)
    weight = weights[mine, :]
    east_number = number_k[...]
    north_number = number_m[mine, :]
    masks = []
    for inner in range(2):
        keep = jnp.logical_and(
            east_number <= cutoffs[0, 2 * band + inner],
            north_number <= cutoffs[1, 2 * band + inner],
        )
        masks.append(jnp.where(keep, weight, 0.0))
    spectra = spectra * jnp.concatenate(masks * FIELDS, axis=0)
    high, low = split(spectra)
    back = dot(jnp.concatenate([high, low], axis=0), k_back[...])
    back = quarters(back, 8 * PLANES, 384)
    for t in range(TILES):
        first = 128 * (t // PER)
        value = jnp.zeros((8, 128), F32)
        for p in range(PLANES):
            moved = pltpu.roll(
                back[8 * p : 8 * p + 8, first : first + 128], (RX * (p - t % PER)) % 128, 1
            )
            value = jnp.where(inside[p], moved, value)
        s3[t] = value
    send_all(*phase3)

    @pl.loop(2, 4)
    def _(group):
        first_stage(group)

    receive_all(*phase3)

    received = r3[...].reshape(MODES, 128)
    back = quarters(dot(m_back[...], jnp.concatenate(split(received), axis=1)), BANDS * RY, 128)
    s4[...] = back.reshape(BANDS, RY, 128)
    send_all(*phase4)
    receive_all(*phase4)

    columns = []
    for of in range(BANDS):
        high, low = split(r4[of])
        columns.append(jnp.concatenate([high, low, high, jnp.zeros((RY, 128), BF)], axis=0))
    wide = dot(y_back[...], jnp.concatenate(columns, axis=1))
    for of in range(BANDS):
        modes[of] = wide[:NY, of * 128 : (of + 1) * 128]
    for group in range(GROUPS):
        first = 2 * group * 128
        outer_modes[group] = (
            wide[NY:, first : first + 128] * own_slot[0]
            + wide[NY:, first + 128 : first + 256] * own_slot[1]
        )

    def across(table, value):
        high, low = split(value)
        return lax.dot_general(
            table,
            jnp.concatenate([high, low, high], axis=1),
            (((1,), (1,)), ((), ())),
            preferred_element_type=F32,
        )

    third = 1.0 / 3.0
    inside_x = [jnp.where(flag[0], 1.0, 0.0) for flag in has]
    inside_y = jnp.where(
        low_lane, jnp.where(has[0][1], 1.0, 0.0), jnp.where(has[1][1], 1.0, 0.0)
    )

    def second_finish(f, plane, at, chunk, value):
        q2[plane, PAD + at : PAD + at + chunk, :] = q0[
            plane, PAD + at : PAD + at + chunk, :
        ] + 0.5 * (value + force[plane, at : at + chunk, :])

    @pl.loop(0, GROUPS)
    def _(group):
        await_edges(1, group)
        outer = across(x_shared[...], outer_modes[group])
        pairs = modes[pl.ds(2 * group, 2)].reshape(2 * NY, 128)
        smooth_pairs = across(x_back[...], pairs)
        for pair in range(2):
            smooth_part = smooth_pairs[:, pair * NY : (pair + 1) * NY]
            for f in range(FIELDS):
                for inner in range(2):
                    plane = f * LEV + group * GLEV + 2 * pair + inner
                    slot = f * GLEV + 2 * pair + inner
                    p = 2 * f + inner
                    nudge = smooth_part[p * NX : (p + 1) * NX]
                    if f < 2:
                        force[plane] = nudge + drag[plane]
                    else:
                        force[plane] = nudge
                    q1[plane, PAD : PAD + NX, :] = q0[plane, PAD : PAD + NX, :] + third * (
                        nudge + partial[plane]
                    )
                    for side, into in ((0, PAD - 3), (1, PAD + NX)):
                        first = PLANES * NX + 8 * p + 4 * side
                        q1[plane, into : into + 3, :] = xr[0, side, group, slot, 0:3, :] + third * (
                            smooth_part[first : first + 3] * inside_x[side]
                            + xr[1, side, group, slot, 0:3, :]
                        )
        y_halo[...] = y_first[group] + third * (outer * inside_y + merged_halo(1, group))

        advance(group, q1, second_finish)
        pack_edges(2, group, interior(q2))
        send_edges(2, group)

    def third_finish(f, plane, at, chunk, value):
        result[plane, at : at + chunk, :] = q0[plane, PAD + at : PAD + at + chunk, :] + (
            value + force[plane, at : at + chunk, :]
        )

    def out_copy(f, group):
        rows = pl.ds(group * GLEV, GLEV)
        into = (east_out, north_out, theta_out)[f]
        return pltpu.make_async_copy(
            result.at[pl.ds(f * LEV + group * GLEV, GLEV)], into.at[rows], out_sem.at[f, group]
        )

    @pl.loop(0, GROUPS)
    def _(group):
        await_edges(2, group)
        fill_pads(2, group, q2)
        y_halo[...] = merged_halo(2, group)
        advance(group, q2, third_finish)
        for f in range(FIELDS):
            out_copy(f, group).start()

    for phase in (phase1, phase2, phase3, phase4):
        sent_all(*phase)

    @pl.loop(0, GROUPS)
    def _(group):
        for turn in range(3):
            edges_sent(turn, group)
        for f in range(FIELDS):
            out_copy(f, group).wait()
        tke_copy(group).wait()


PARTS = 2


def deliver(*refs):
    sources, results, held, in_sems, out_sems = refs[:4], refs[4:8], refs[8], refs[9], refs[10]
    inward, outward = [], []
    for j in range(PARTS):
        rows = pl.ds(j * (LEV // PARTS), LEV // PARTS)
        for i in range(4):
            inward.append(
                pltpu.make_async_copy(sources[i].at[rows], held.at[i, rows], in_sems.at[i, j])
            )
            outward.append(
                pltpu.make_async_copy(held.at[i, rows], results[i].at[rows], out_sems.at[i, j])
            )
    for copy in inward:
        copy.start()
    for first, second in zip(inward, outward):
        first.wait()
        second.start()
    for copy in outward:
        copy.wait()


def shards(*arguments):
    tables = [jnp.asarray(table) for table in make_tables()]
    field = jax.ShapeDtypeStruct((LEV, NX, NY), F32)
    anywhere = pl.BlockSpec(memory_space=pl.ANY)
    smem = pl.BlockSpec(memory_space=pltpu.SMEM)
    padded = pltpu.VMEM((FIELDS * LEV, NX + 2 * PAD, NY), F32)
    planes = pltpu.VMEM((FIELDS * LEV, NX, NY), F32)
    dma = pltpu.SemaphoreType.DMA
    outcome = pl.pallas_call(
        kernel,
        out_shape=(field,) * 4,
        in_specs=[anywhere] * 9 + [smem] * 3 + [anywhere] * TABLES,
        out_specs=(anywhere,) * 4,
        scratch_shapes=[pltpu.VMEM(table.shape, table.dtype) for table in tables]
        + [
            padded,
            padded,
            padded,
            planes,
            pltpu.VMEM((LEV, NX, NY), F32),
            pltpu.VMEM((NX, NY), jnp.int32),
            pltpu.VMEM((NX, NY), jnp.int32),
            planes,
            pltpu.VMEM((2 * LEV, NX, NY), F32),
            planes,
            planes,
            pltpu.VMEM((SLOTS * NX, 2 * NY), F32),
            pltpu.VMEM((NX, 128), F32),
            pltpu.VMEM((3, 2, GROUPS, SLOTS, 4, 128), F32),
            pltpu.VMEM((3, 2, GROUPS, SLOTS, 4, 128), F32),
            pltpu.VMEM((3, GROUPS, NX, 128), F32),
            pltpu.VMEM((3, 2, GROUPS, NX, 128), F32),
            pltpu.VMEM((BANDS, RY, 128), F32),
            pltpu.VMEM((BANDS, RY, 128), F32),
            pltpu.VMEM((TILES, 8, 128), F32),
            pltpu.VMEM((TILES, 8, 128), F32),
            pltpu.VMEM((TILES, 8, 128), F32),
            pltpu.VMEM((TILES, 8, 128), F32),
            pltpu.VMEM((BANDS, RY, 128), F32),
            pltpu.VMEM((BANDS, RY, 128), F32),
            pltpu.VMEM((BANDS, NY, 128), F32),
            pltpu.VMEM((GROUPS, NY, 128), F32),
            pltpu.VMEM((SLOTS * NX, 4 * NY), BF),
            pltpu.VMEM((GROUPS, NX, 128), F32),
            dma((9, GROUPS)),
            dma((TABLES,)),
            dma((4, GROUPS)),
            dma((3, 2, GROUPS)),
            dma((3, 2, GROUPS)),
            dma((3, 2, GROUPS)),
            dma((3, 2, GROUPS)),
            dma((BANDS,)),
            dma((BANDS,)),
            dma((TILES,)),
            dma((TILES,)),
            dma((TILES,)),
            dma((TILES,)),
            dma((BANDS,)),
            dma((BANDS,)),
        ],
        compiler_params=pltpu.CompilerParams(
            collective_id=0, has_side_effects=True, vmem_limit_bytes=61 * 1024 * 1024
        ),
        cost_estimate=pl.CostEstimate(
            flops=10**9, bytes_accessed=6 * 2**20, transcendentals=LEV * NX * NY
        ),
        name="step",
    )(*arguments, *tables)
    return pl.pallas_call(
        deliver,
        out_shape=(field,) * 4,
        in_specs=[anywhere] * 4,
        out_specs=(anywhere,) * 4,
        scratch_shapes=[
            pltpu.VMEM((4, LEV, NX, NY), F32),
            dma((4, PARTS)),
            dma((4, PARTS)),
        ],
        compiler_params=pltpu.CompilerParams(vmem_limit_bytes=61 * 1024 * 1024),
        name="deliver",
    )(*outcome)


def solution(mesh):
    field = P(None, "tile", "band")
    column = P("tile", "band")
    in_specs = (field,) * 7 + (column,) * 2 + (P(),) * 3
    return jax.shard_map(
        shards, mesh=mesh, in_specs=in_specs, out_specs=(field,) * 4, check_vma=False
    )
```

```python
import functools

import jax
import jax.numpy as jnp
import ml_dtypes
import numpy as np
from jax import lax
from jax.experimental import pallas as pl
from jax.experimental.pallas import tpu as pltpu
from jax.sharding import PartitionSpec as P

KMAX = 64
MODES = 2 * KMAX
NTYPE = 8
LEV = 16
FIELDS = 3
BANDS = 8
TILES = 16
NX = 64
NY = 128
RX = 21
RY = 32
PLANES = 6
GROUPS = 4
GLEV = LEV // GROUPS
SLOTS = FIELDS * GLEV
PER = 6
PAD = 8
TABLES = 14
MESH = pl.DeviceIdType.MESH
BF = jnp.bfloat16
F32 = jnp.float32


def wavenumbers():
    index = np.arange(MODES)
    return np.where(index < KMAX, index, index - KMAX + 1)


def basis(extent, positions):
    number = wavenumbers()
    angle = 2 * np.pi * ((number[:, None] * positions[None, :]) % extent) / extent
    return np.where((np.arange(MODES) < KMAX)[:, None], np.cos(angle), np.sin(angle))


def window(length, extent, rank):
    index = np.arange(length)
    half = (KMAX + 0.5) / extent
    diagonal = ((length - 1 - 2 * index) / 2) ** 2 * np.cos(2 * np.pi * half)
    beside = index[1:] * (length - index[1:]) / 2
    _, vectors = np.linalg.eigh(np.diag(diagonal) + np.diag(beside, 1) + np.diag(beside, -1))
    vectors = vectors[:, ::-1][:, :rank]
    largest = vectors[np.argmax(np.abs(vectors) > 0.02, axis=0), np.arange(rank)]
    return vectors * np.sign(largest)


def halves(table):
    high = table.astype(np.float32).astype(ml_dtypes.bfloat16)
    low = (table - high.astype(np.float64)).astype(np.float32).astype(ml_dtypes.bfloat16)
    return high, low


def stencil_table():
    central = {1: 45.0, -1: -45.0, 2: -9.0, -2: 9.0, 3: 1.0, -3: -1.0}
    smooth = {3: 1.0, -3: 1.0, 2: -6.0, -2: -6.0, 1: 15.0, -1: 15.0, 0: -20.0}
    inner = np.zeros((NY, 2 * NY))
    outer = np.zeros((NY, 2 * NY))
    for column, taps in ((0, central), (NY, smooth)):
        for y in range(NY):
            for offset, tap in taps.items():
                at = y + offset
                if 0 <= at < NY:
                    inner[at, column + y] = tap
                elif at < 0:
                    outer[at + 3, column + y] = tap
                else:
                    outer[at - NY + 3, column + y] = tap
    return np.concatenate([inner, inner, outer, outer]).astype(ml_dtypes.bfloat16)


def make_tables():
    east_n, north_n = NX * TILES, NY * BANDS
    vx = window(NX, east_n, RX)
    vy = window(NY, north_n, RY)
    wx = window(NX + 6, east_n, RX)
    wy = window(NY + 6, north_n, RY)
    cells_x = np.arange(NX + 6) - 3
    cells_y = np.arange(NY + 6) - 3
    ux = [basis(east_n, NX * t + np.arange(NX)) @ vx for t in range(TILES)]
    uy = [basis(north_n, NY * b + np.arange(NY)) @ vy for b in range(BANDS)]

    block = np.zeros((PLANES * NX, 128))
    for p in range(PLANES):
        block[p * NX : (p + 1) * NX, p * RX : (p + 1) * RX] = vx
    high, low = halves(block.T)
    x_forward = np.concatenate([high, low], axis=0)
    rows = PLANES * NX
    block = np.zeros((rows + PLANES * 8, 128))
    for p in range(PLANES):
        columns = slice(p * RX, (p + 1) * RX)
        block[p * NX : (p + 1) * NX, columns] = 0.5 * wx[3 : NX + 3]
        block[rows + 8 * p : rows + 8 * p + 3, columns] = 0.5 * wx[:3]
        block[rows + 8 * p + 4 : rows + 8 * p + 7, columns] = 0.5 * wx[NX + 3 :]
    high, low = halves(block)
    x_back = np.concatenate([high, high, low], axis=1)
    shared = sum(block[p * NX : (p + 1) * NX] for p in range(PLANES))
    high, low = halves(shared)
    x_shared = np.concatenate([high, high, low], axis=1)

    high, low = halves(vy.T)
    y_forward = np.concatenate(
        [np.concatenate([high, high], axis=1), np.concatenate([low, 0 * low], axis=1)], axis=0
    )
    both_y = np.zeros((2 * NY, RY))
    both_y[:NY] = wy[3 : NY + 3]
    both_y[NY : NY + 6 * SLOTS] = np.tile(np.concatenate([wy[:3], wy[NY + 3 :]]), (SLOTS, 1))
    high, low = halves(both_y)
    y_back = np.concatenate([high, high, low, 0 * low], axis=1)
    own_slot = np.zeros((2, 128, 128), np.float32)
    for pair in range(2):
        for p in range(PLANES):
            slot = (p // 2) * GLEV + 2 * pair + p % 2
            own_slot[pair, 6 * slot : 6 * slot + 6, p * RX : (p + 1) * RX] = 1

    uy_all = np.concatenate(uy, axis=1)
    m_forward = np.concatenate(halves(uy_all), axis=0)
    uy = [basis(north_n, NY * b + cells_y) @ wy for b in range(BANDS)]
    m_back = np.concatenate(halves(np.concatenate(uy, axis=1).T), axis=0)

    ux_all = np.zeros((MODES, 384))
    for t in range(TILES):
        at = 128 * (t // PER) + RX * (t % PER)
        ux_all[:, at : at + RX] = ux[t]
    k_forward = np.concatenate(halves(ux_all.T), axis=1)
    for t in range(TILES):
        at = 128 * (t // PER) + RX * (t % PER)
        ux_all[:, at : at + RX] = basis(east_n, NX * t + cells_x) @ wx
    k_back = np.concatenate(halves(ux_all), axis=1)

    number = wavenumbers()
    weight_k = np.where(number == 0, 1.0, 2.0) / east_n
    weight_m = np.where(number == 0, 1.0, 2.0) / north_n
    weights = (weight_m[:, None] * weight_k[None, :]).astype(np.float32)
    number_k = np.broadcast_to(number[None, :], (8, MODES)).astype(np.int32)
    number_m = np.broadcast_to(number[:, None], (MODES, MODES)).astype(np.int32)
    return (
        x_forward,
        y_forward,
        m_forward,
        k_forward,
        k_back,
        m_back,
        y_back,
        x_back,
        x_shared,
        own_slot,
        stencil_table(),
        weights,
        number_k,
        number_m,
    )


def split(value):
    high = value.astype(BF)
    low = (value - high.astype(F32)).astype(BF)
    return high, low


def dot(a, b):
    return lax.dot_general(a, b, (((1,), (0,)), ((), ())), preferred_element_type=F32)


def quarters(product, rows, columns):
    return (product[:rows, :columns] + product[:rows, columns:]) + (
        product[rows:, :columns] + product[rows:, columns:]
    )


def kernel(
    wind_east,
    wind_north,
    theta_pert,
    tke_field,
    target_east,
    target_north,
    target_theta,
    turbine_count,
    turbine_type,
    drag_coeff,
    tke_coeff,
    cutoffs,
    *rest,
):
    table_sources, rest = rest[:TABLES], rest[TABLES:]
    tables, rest = rest[4 : 4 + TABLES], rest[:4] + rest[4 + TABLES :]
    step_body(
        wind_east,
        wind_north,
        theta_pert,
        tke_field,
        target_east,
        target_north,
        target_theta,
        turbine_count,
        turbine_type,
        drag_coeff,
        tke_coeff,
        cutoffs,
        table_sources,
        tables,
        *rest,
    )


def step_body(
    wind_east,
    wind_north,
    theta_pert,
    tke_field,
    target_east,
    target_north,
    target_theta,
    turbine_count,
    turbine_type,
    drag_coeff,
    tke_coeff,
    cutoffs,
    table_sources,
    tables,
    east_out,
    north_out,
    theta_out,
    tke_out,
    q0,
    q1,
    q2,
    target,
    tke,
    count,
    kind,
    partial,
    drag,
    force,
    result,
    diffs,
    y_halo,
    xs,
    xr,
    ys,
    yr,
    s1,
    r1,
    s2,
    r2,
    s3,
    r3,
    s4,
    r4,
    modes,
    outer_modes,
    operand,
    in_sem,
    table_sem,
    out_sem,
    xs_sem,
    xr_sem,
    ys_sem,
    yr_sem,
    s1_sem,
    r1_sem,
    s2_sem,
    r2_sem,
    s3_sem,
    r3_sem,
    s4_sem,
    r4_sem,
):
    (
        x_forward,
        y_forward,
        m_forward,
        k_forward,
        k_back,
        m_back,
        y_back,
        x_back,
        x_shared,
        own_slot,
        stencil,
        weights,
        number_k,
        number_m,
    ) = tables
    band = lax.axis_index("band")
    tile = lax.axis_index("tile")

    def field_copies(group):
        rows = pl.ds(group * GLEV, GLEV)
        copies = []
        for f, source in enumerate((wind_east, wind_north, theta_pert)):
            into = q0.at[pl.ds(f * LEV + group * GLEV, GLEV), pl.ds(PAD, NX), :]
            copies.append(pltpu.make_async_copy(source.at[rows], into, in_sem.at[f, group]))
        for f, source in enumerate((target_east, target_north, target_theta)):
            into = target.at[pl.ds(f * LEV + group * GLEV, GLEV)]
            copies.append(pltpu.make_async_copy(source.at[rows], into, in_sem.at[3 + f, group]))
        return copies

    others = [
        pltpu.make_async_copy(source, into, in_sem.at[6 + i, 0])
        for i, (source, into) in enumerate(
            ((tke_field, tke), (turbine_count, count), (turbine_type, kind))
        )
    ]
    table_copies = [
        pltpu.make_async_copy(source, into, table_sem.at[i])
        for i, (source, into) in enumerate(zip(table_sources, tables))
    ]
    for copy in table_copies[:2]:
        copy.start()

    for group in range(GROUPS):
        for copy in field_copies(group):
            copy.start()
    for copy in others + table_copies[2:]:
        copy.start()

    @pl.when(tile == 0)
    def _():
        xr[:, 0] = jnp.zeros((3, GROUPS, SLOTS, 4, 128), F32)

    @pl.when(tile == TILES - 1)
    def _():
        xr[:, 1] = jnp.zeros((3, GROUPS, SLOTS, 4, 128), F32)

    @pl.when(band == 0)
    def _():
        yr[:, 0] = jnp.zeros((3, GROUPS, NX, 128), F32)

    @pl.when(band == BANDS - 1)
    def _():
        yr[:, 1] = jnp.zeros((3, GROUPS, NX, 128), F32)

    barrier = pltpu.get_barrier_semaphore()
    for step in range(1, TILES):
        pl.semaphore_signal(
            barrier, inc=1, device_id={"tile": lax.rem(tile + step, TILES)}, device_id_type=MESH
        )
    for step in range(1, BANDS):
        pl.semaphore_signal(
            barrier, inc=1, device_id={"band": lax.rem(band + step, BANDS)}, device_id_type=MESH
        )

    lane = lax.broadcasted_iota(jnp.int32, (NX, 128), 1)
    low_lane = lax.rem(lane, 6) < 3


    def pack_edges(turn, group, plane_of):
        packed = jnp.zeros((NX, 128), F32)
        for slot in range(SLOTS):
            plane = plane_of((slot // GLEV) * LEV + group * GLEV + slot % GLEV)
            xs[turn, 0, group, slot, 0:3, :] = plane[0:3]
            xs[turn, 1, group, slot, 0:3, :] = plane[NX - 3 : NX]
            mine = jnp.logical_and(lane >= slot * 6, lane < slot * 6 + 6)
            packed = jnp.where(mine, pltpu.roll(plane, slot * 6 + 3, 1), packed)
        ys[turn, group] = packed

    def interior(source):
        return lambda plane: source[plane, PAD : PAD + NX, :]

    def x_copy(turn, group, side):
        return pltpu.make_async_remote_copy(
            src_ref=xs.at[turn, side, group],
            dst_ref=xr.at[turn, 1 - side, group],
            send_sem=xs_sem.at[turn, side, group],
            recv_sem=xr_sem.at[turn, 1 - side, group],
            device_id={"tile": tile + (1 if side else -1)},
            device_id_type=MESH,
        )

    def y_copy(turn, group, side):
        return pltpu.make_async_remote_copy(
            src_ref=ys.at[turn, group],
            dst_ref=yr.at[turn, 1 - side, group],
            send_sem=ys_sem.at[turn, side, group],
            recv_sem=yr_sem.at[turn, 1 - side, group],
            device_id={"band": band + (1 if side else -1)},
            device_id_type=MESH,
        )

    has = (
        (tile > 0, band > 0),
        (tile < TILES - 1, band < BANDS - 1),
    )

    def send_edges(turn, group):
        for side in range(2):

            @pl.when(has[side][0])
            def _():
                x_copy(turn, group, side).start()

            @pl.when(has[side][1])
            def _():
                y_copy(turn, group, side).start()

    def await_edges(turn, group):
        for side in range(2):

            @pl.when(has[side][0])
            def _():
                x_copy(turn, group, 1 - side).wait_recv()

            @pl.when(has[side][1])
            def _():
                y_copy(turn, group, 1 - side).wait_recv()

    def merged_halo(turn, group):
        return jnp.where(low_lane, yr[turn, 0, group], yr[turn, 1, group])

    def fill_pads(turn, group, source):
        for f in range(FIELDS):
            for inner in range(GLEV):
                plane, slot = f * LEV + group * GLEV + inner, f * GLEV + inner
                source[plane, PAD - 3 : PAD, :] = xr[turn, 0, group, slot, 0:3, :]
                source[plane, PAD + NX : PAD + NX + 3, :] = xr[turn, 1, group, slot, 0:3, :]

    def edges_sent(turn, group):
        for side in range(2):

            @pl.when(has[side][0])
            def _():
                x_copy(turn, group, side).wait_send()

            @pl.when(has[side][1])
            def _():
                y_copy(turn, group, side).wait_send()


    def advance(group, source, finish):
        halo = y_halo[...]
        for slot in range(SLOTS):
            place = (slot % GLEV) * FIELDS + slot // GLEV
            plane = (slot // GLEV) * LEV + group * GLEV + slot % GLEV
            high, low = split(source[plane, PAD : PAD + NX, :])
            halo_high, halo_low = split(pltpu.roll(halo, 128 - slot * 6, 1) if slot else halo)
            operand[place * NX : (place + 1) * NX, :] = jnp.concatenate(
                [high, low, halo_high, halo_low], axis=1
            )


        for inner in range(GLEV):
            level = group * GLEV + inner
            chunk = 16
            own = pl.ds(inner * FIELDS * NX, FIELDS * NX)
            diffs[own, :] = dot(operand[own, :], stencil[...])
            for at in range(0, NX, chunk):
                east = source[level, PAD + at : PAD + at + chunk, :] * (1.0 / 60.0)
                north = source[LEV + level, PAD + at : PAD + at + chunk, :] * (1.0 / 60.0)
                east_size = jnp.abs(east)
                north_size = jnp.abs(north)
                for f in range(FIELDS):
                    plane = f * LEV + level

                    def cell(offset):
                        return source[plane, PAD + at + offset : PAD + at + offset + chunk, :]

                    up1, up2, up3 = cell(1), cell(2), cell(3)
                    down1, down2, down3 = cell(-1), cell(-2), cell(-3)
                    central = 45.0 * (up1 - down1) - 9.0 * (up2 - down2) + (up3 - down3)
                    smooth = (
                        (up3 + down3)
                        - 6.0 * (up2 + down2)
                        + 15.0 * (up1 + down1)
                        - 20.0 * cell(0)
                    )
                    first = (inner * FIELDS + f) * NX + at
                    central_y = diffs[pl.ds(first, chunk), 0:NY]
                    smooth_y = diffs[pl.ds(first, chunk), NY : 2 * NY]
                    value = (east_size * smooth - east * central) + (
                        north_size * smooth_y - north * central_y
                    )
                    finish(f, plane, at, chunk, value)


    def turbines(group):
        counts = count[...].astype(F32)
        kinds = kind[...]

        @pl.loop(0, GLEV)
        def _(inner):
            level = group * GLEV + inner
            rate = jnp.full((NX, NY), drag_coeff[0, level])
            growth = jnp.full((NX, NY), tke_coeff[0, level])
            for k in range(1, NTYPE):
                here = kinds == k
                rate = jnp.where(here, drag_coeff[k, level], rate)
                growth = jnp.where(here, tke_coeff[k, level], growth)
            east = q0[level, PAD : PAD + NX, :]
            north = q0[LEV + level, PAD : PAD + NX, :]
            speed = jnp.sqrt(east * east + north * north)
            rate = counts * rate * speed
            tke[level] = tke[level] + counts * growth * speed * speed * speed
            drag[level] = -(rate * east)
            drag[LEV + level] = -(rate * north)

    def tke_copy(group):
        rows = pl.ds(group * GLEV, GLEV)
        return pltpu.make_async_copy(tke.at[rows], tke_out.at[rows], out_sem.at[3, group])


    for copy in table_copies[:2]:
        copy.wait()

    def coefficients(to):
        rows = []
        for f in range(FIELDS):
            part = pl.ds(f * LEV + 2 * to, 2)
            gap = target[part] - q0[part, PAD : PAD + NX, :]
            rows.append(gap.reshape(2 * NX, NY))
        high, low = split(jnp.concatenate(rows, axis=0))
        along_x = quarters(dot(x_forward[...], jnp.concatenate([high, low], axis=1)), 128, NY)
        both = lax.dot_general(
            y_forward[...],
            jnp.concatenate(split(along_x), axis=1),
            (((1,), (1,)), ((), ())),
            preferred_element_type=F32,
        )
        s1[to] = both[:RY] + both[RY:]

    @pl.loop(0, GROUPS)
    def _(group):
        for copy in field_copies(group):
            copy.wait()
        for pair in range(2):
            coefficients(2 * group + pair)

    pl.semaphore_wait(barrier, BANDS - 1 + TILES - 1)

    def partners(axis):
        if axis == "band":
            return [lax.rem(band + step, BANDS) for step in (4, 3, 5, 2, 6, 1, 7)]
        apart = sorted(
            ((dx, dz) for dx in range(4) for dz in range(4) if dx or dz),
            key=lambda at: -(min(at[0], 4 - at[0]) + min(at[1], 4 - at[1])),
        )
        x, z = tile // 4, lax.rem(tile, 4)
        return [lax.rem(x + dx, 4) * 4 + lax.rem(z + dz, 4) for dx, dz in apart]

    def outgoing(axis, me, source, into, send_sem, recv_sem, other):
        return pltpu.make_async_remote_copy(
            src_ref=source.at[other],
            dst_ref=into.at[me],
            send_sem=send_sem.at[other],
            recv_sem=recv_sem.at[me],
            device_id={axis: other},
            device_id_type=MESH,
        )

    def send_all(axis, me, source, into, send_sem, recv_sem):
        for other in partners(axis):
            outgoing(axis, me, source, into, send_sem, recv_sem, other).start()
        into[me] = source[me]

    def receive_all(axis, me, source, into, send_sem, recv_sem):
        for other in partners(axis)[::-1]:
            pltpu.make_async_remote_copy(
                src_ref=source.at[other],
                dst_ref=into.at[other],
                send_sem=send_sem.at[other],
                recv_sem=recv_sem.at[other],
                device_id={axis: other},
                device_id_type=MESH,
            ).wait_recv()

    def sent_all(axis, me, source, into, send_sem, recv_sem):
        for other in partners(axis):
            outgoing(axis, me, source, into, send_sem, recv_sem, other).wait_send()

    phase1 = ("band", band, s1, r1, s1_sem, r1_sem)
    phase2 = ("tile", tile, s2, r2, s2_sem, r2_sem)
    phase3 = ("tile", tile, s3, r3, s3_sem, r3_sem)
    phase4 = ("band", band, s4, r4, s4_sem, r4_sem)

    send_all(*phase1)

    @pl.loop(0, GROUPS)
    def _(group):
        pack_edges(0, group, interior(q0))
        send_edges(0, group)

    for copy in others + table_copies[2:]:
        copy.wait()

    @pl.loop(0, GROUPS)
    def _(group):
        turbines(group)
        tke_copy(group).start()

    third = 1.0 / 3.0

    def first_finish(f, plane, at, chunk, value):
        if f < 2:
            value = value + drag[plane, at : at + chunk, :]
        partial[plane, at : at + chunk, :] = (
            q0[plane, PAD + at : PAD + at + chunk, :] + third * value
        )

    def first_stage(group):
        await_edges(0, group)
        fill_pads(0, group, q0)
        y_halo[...] = merged_halo(0, group)
        advance(group, q0, first_finish)
        pack_edges(1, group, lambda plane: partial[plane])
        send_edges(1, group)

    receive_all(*phase1)

    received = r1[...].reshape(BANDS * RY, 128)
    columns = jnp.concatenate(split(received), axis=1)
    s2[...] = quarters(dot(m_forward[...], columns), MODES, 128).reshape(TILES, 8, 128)
    send_all(*phase2)

    @pl.loop(0, GROUPS)
    def _(group):
        first_stage(group)

    receive_all(*phase2)

    lane8 = lax.broadcasted_iota(jnp.int32, (8, 128), 1)
    inside = [
        jnp.logical_and(lane8 >= RX * i, lane8 < RX * (i + 1)) for i in range(PER)
    ]
    blocks = [r2[t] for t in range(TILES)]
    rows = []
    for p in range(PLANES):
        parts = []
        for first in range(0, TILES, PER):
            value = jnp.zeros((8, 128), F32)
            for i, t in enumerate(range(first, min(first + PER, TILES))):
                moved = pltpu.roll(blocks[t], (RX * (i - p)) % 128, 1)
                value = jnp.where(inside[i], moved, value)
            parts.append(value)
        rows.append(jnp.concatenate(parts, axis=1))
    packed = jnp.concatenate(split(jnp.concatenate(rows, axis=0)), axis=0)
    spectra = quarters(dot(packed, k_forward[...]), 8 * PLANES, MODES)
    mine = pl.ds(pl.multiple_of(tile * 8, 8), 8)
    weight = weights[mine, :]
    east_number = number_k[...]
    north_number = number_m[mine, :]
    masks = []
    for inner in range(2):
        keep = jnp.logical_and(
            east_number <= cutoffs[0, 2 * band + inner],
            north_number <= cutoffs[1, 2 * band + inner],
        )
        masks.append(jnp.where(keep, weight, 0.0))
    spectra = spectra * jnp.concatenate(masks * FIELDS, axis=0)
    high, low = split(spectra)
    back = dot(jnp.concatenate([high, low], axis=0), k_back[...])
    back = quarters(back, 8 * PLANES, 384)
    for t in range(TILES):
        first = 128 * (t // PER)
        value = jnp.zeros((8, 128), F32)
        for p in range(PLANES):
            moved = pltpu.roll(
                back[8 * p : 8 * p + 8, first : first + 128], (RX * (p - t % PER)) % 128, 1
            )
            value = jnp.where(inside[p], moved, value)
        s3[t] = value
    send_all(*phase3)

    receive_all(*phase3)

    received = r3[...].reshape(MODES, 128)
    back = quarters(dot(m_back[...], jnp.concatenate(split(received), axis=1)), BANDS * RY, 128)
    s4[...] = back.reshape(BANDS, RY, 128)
    send_all(*phase4)
    for phase in (phase1, phase2, phase3):
        sent_all(*phase)

    @pl.loop(0, GROUPS)
    def _(group):
        edges_sent(0, group)
        edges_sent(1, group)
        tke_copy(group).wait()
        await_edges(1, group)

    receive_all(*phase4)

    columns = []
    for of in range(BANDS):
        high, low = split(r4[of])
        columns.append(jnp.concatenate([high, low, high, jnp.zeros((RY, 128), BF)], axis=0))
    wide = dot(y_back[...], jnp.concatenate(columns, axis=1))
    for of in range(BANDS):
        modes[of] = wide[:NY, of * 128 : (of + 1) * 128]
    for group in range(GROUPS):
        first = 2 * group * 128
        outer_modes[group] = (
            wide[NY:, first : first + 128] * own_slot[0]
            + wide[NY:, first + 128 : first + 256] * own_slot[1]
        )

    def across(table, value):
        high, low = split(value)
        return lax.dot_general(
            table,
            jnp.concatenate([high, low, high], axis=1),
            (((1,), (1,)), ((), ())),
            preferred_element_type=F32,
        )

    inside_x = [jnp.where(flag[0], third, 0.0) for flag in has]
    inside_y = jnp.where(
        low_lane, jnp.where(has[0][1], third, 0.0), jnp.where(has[1][1], third, 0.0)
    )

    def second_finish(f, plane, at, chunk, value):
        q2[plane, PAD + at : PAD + at + chunk, :] = q0[
            plane, PAD + at : PAD + at + chunk, :
        ] + 0.5 * (value + force[plane, at : at + chunk, :])

    @pl.loop(0, GROUPS)
    def _(group):
        outer = across(x_shared[...], outer_modes[group])
        pairs = modes[pl.ds(2 * group, 2)].reshape(2 * NY, 128)
        smooth_pairs = across(x_back[...], pairs)
        for pair in range(2):
            smooth_part = smooth_pairs[:, pair * NY : (pair + 1) * NY]
            for f in range(FIELDS):
                for inner in range(2):
                    plane = f * LEV + group * GLEV + 2 * pair + inner
                    slot = f * GLEV + 2 * pair + inner
                    p = 2 * f + inner
                    nudge = smooth_part[p * NX : (p + 1) * NX]
                    if f < 2:
                        force[plane] = nudge + drag[plane]
                    else:
                        force[plane] = nudge
                    q1[plane, PAD : PAD + NX, :] = partial[plane] + third * nudge
                    for side, into in ((0, PAD - 3), (1, PAD + NX)):
                        first = PLANES * NX + 8 * p + 4 * side
                        q1[plane, into : into + 3, :] = xr[
                            1, side, group, slot, 0:3, :
                        ] + smooth_part[first : first + 3] * inside_x[side]
        y_halo[...] = merged_halo(1, group) + outer * inside_y

        advance(group, q1, second_finish)
        pack_edges(2, group, interior(q2))
        send_edges(2, group)

    def third_finish(f, plane, at, chunk, value):
        result[plane, at : at + chunk, :] = q0[plane, PAD + at : PAD + at + chunk, :] + (
            value + force[plane, at : at + chunk, :]
        )

    def out_copy(f, group):
        rows = pl.ds(group * GLEV, GLEV)
        into = (east_out, north_out, theta_out)[f]
        return pltpu.make_async_copy(
            result.at[pl.ds(f * LEV + group * GLEV, GLEV)], into.at[rows], out_sem.at[f, group]
        )

    @pl.loop(0, GROUPS)
    def _(group):
        await_edges(2, group)
        fill_pads(2, group, q2)
        y_halo[...] = merged_halo(2, group)
        advance(group, q2, third_finish)
        for f in range(FIELDS):
            out_copy(f, group).start()

    sent_all(*phase4)

    @pl.loop(0, GROUPS)
    def _(group):
        edges_sent(2, group)
        for f in range(FIELDS):
            out_copy(f, group).wait()


PARTS = 2


def deliver(*refs):
    sources, results, held, in_sems, out_sems = refs[:4], refs[4:8], refs[8], refs[9], refs[10]
    inward, outward = [], []
    for j in range(PARTS):
        rows = pl.ds(j * (LEV // PARTS), LEV // PARTS)
        for i in range(4):
            inward.append(
                pltpu.make_async_copy(sources[i].at[rows], held.at[i, rows], in_sems.at[i, j])
            )
            outward.append(
                pltpu.make_async_copy(held.at[i, rows], results[i].at[rows], out_sems.at[i, j])
            )
    for copy in inward:
        copy.start()
    for first, second in zip(inward, outward):
        first.wait()
        second.start()
    for copy in outward:
        copy.wait()


def shards(*arguments):
    tables = [jnp.asarray(table) for table in make_tables()]
    field = jax.ShapeDtypeStruct((LEV, NX, NY), F32)
    anywhere = pl.BlockSpec(memory_space=pl.ANY)
    smem = pl.BlockSpec(memory_space=pltpu.SMEM)
    padded = pltpu.VMEM((FIELDS * LEV, NX + 2 * PAD, NY), F32)
    planes = pltpu.VMEM((FIELDS * LEV, NX, NY), F32)
    dma = pltpu.SemaphoreType.DMA
    outcome = pl.pallas_call(
        kernel,
        out_shape=(field,) * 4,
        in_specs=[anywhere] * 9 + [smem] * 3 + [anywhere] * TABLES,
        out_specs=(anywhere,) * 4,
        scratch_shapes=[pltpu.VMEM(table.shape, table.dtype) for table in tables]
        + [
            padded,
            padded,
            padded,
            planes,
            pltpu.VMEM((LEV, NX, NY), F32),
            pltpu.VMEM((NX, NY), jnp.int32),
            pltpu.VMEM((NX, NY), jnp.int32),
            planes,
            pltpu.VMEM((2 * LEV, NX, NY), F32),
            planes,
            planes,
            pltpu.VMEM((SLOTS * NX, 2 * NY), F32),
            pltpu.VMEM((NX, 128), F32),
            pltpu.VMEM((3, 2, GROUPS, SLOTS, 4, 128), F32),
            pltpu.VMEM((3, 2, GROUPS, SLOTS, 4, 128), F32),
            pltpu.VMEM((3, GROUPS, NX, 128), F32),
            pltpu.VMEM((3, 2, GROUPS, NX, 128), F32),
            pltpu.VMEM((BANDS, RY, 128), F32),
            pltpu.VMEM((BANDS, RY, 128), F32),
            pltpu.VMEM((TILES, 8, 128), F32),
            pltpu.VMEM((TILES, 8, 128), F32),
            pltpu.VMEM((TILES, 8, 128), F32),
            pltpu.VMEM((TILES, 8, 128), F32),
            pltpu.VMEM((BANDS, RY, 128), F32),
            pltpu.VMEM((BANDS, RY, 128), F32),
            pltpu.VMEM((BANDS, NY, 128), F32),
            pltpu.VMEM((GROUPS, NY, 128), F32),
            pltpu.VMEM((SLOTS * NX, 4 * NY), BF),
            dma((9, GROUPS)),
            dma((TABLES,)),
            dma((4, GROUPS)),
            dma((3, 2, GROUPS)),
            dma((3, 2, GROUPS)),
            dma((3, 2, GROUPS)),
            dma((3, 2, GROUPS)),
            dma((BANDS,)),
            dma((BANDS,)),
            dma((TILES,)),
            dma((TILES,)),
            dma((TILES,)),
            dma((TILES,)),
            dma((BANDS,)),
            dma((BANDS,)),
        ],
        compiler_params=pltpu.CompilerParams(
            collective_id=0, has_side_effects=True, vmem_limit_bytes=61 * 1024 * 1024
        ),
        cost_estimate=pl.CostEstimate(
            flops=10**9, bytes_accessed=6 * 2**20, transcendentals=LEV * NX * NY
        ),
        name="step",
    )(*arguments, *tables)
    return pl.pallas_call(
        deliver,
        out_shape=(field,) * 4,
        in_specs=[anywhere] * 4,
        out_specs=(anywhere,) * 4,
        scratch_shapes=[
            pltpu.VMEM((4, LEV, NX, NY), F32),
            dma((4, PARTS)),
            dma((4, PARTS)),
        ],
        compiler_params=pltpu.CompilerParams(vmem_limit_bytes=61 * 1024 * 1024),
        name="deliver",
    )(*outcome)


def solution(mesh):
    field = P(None, "tile", "band")
    column = P("tile", "band")
    in_specs = (field,) * 7 + (column,) * 2 + (P(),) * 3
    return jax.shard_map(
        shards, mesh=mesh, in_specs=in_specs, out_specs=(field,) * 4, check_vma=False
    )
```

```python
import functools

import jax
import jax.numpy as jnp
import ml_dtypes
import numpy as np
from jax import lax
from jax.experimental import pallas as pl
from jax.experimental.pallas import tpu as pltpu
from jax.sharding import PartitionSpec as P

KMAX = 64
MODES = 2 * KMAX
NTYPE = 8
LEV = 16
FIELDS = 3
BANDS = 8
TILES = 16
NX = 64
NY = 128
RX = 21
RY = 32
PLANES = 6
GROUPS = 4
GLEV = LEV // GROUPS
SLOTS = FIELDS * GLEV
PER = 6
PAD = 8
TABLES = 14
MESH = pl.DeviceIdType.MESH
BF = jnp.bfloat16
F32 = jnp.float32


def wavenumbers():
    index = np.arange(MODES)
    return np.where(index < KMAX, index, index - KMAX + 1)


def basis(extent, positions):
    number = wavenumbers()
    angle = 2 * np.pi * ((number[:, None] * positions[None, :]) % extent) / extent
    return np.where((np.arange(MODES) < KMAX)[:, None], np.cos(angle), np.sin(angle))


def window(length, extent, rank):
    index = np.arange(length)
    half = (KMAX + 0.5) / extent
    diagonal = ((length - 1 - 2 * index) / 2) ** 2 * np.cos(2 * np.pi * half)
    beside = index[1:] * (length - index[1:]) / 2
    _, vectors = np.linalg.eigh(np.diag(diagonal) + np.diag(beside, 1) + np.diag(beside, -1))
    vectors = vectors[:, ::-1][:, :rank]
    largest = vectors[np.argmax(np.abs(vectors) > 0.02, axis=0), np.arange(rank)]
    return vectors * np.sign(largest)


def halves(table):
    high = table.astype(np.float32).astype(ml_dtypes.bfloat16)
    low = (table - high.astype(np.float64)).astype(np.float32).astype(ml_dtypes.bfloat16)
    return high, low


def stencil_table():
    central = {1: 45.0, -1: -45.0, 2: -9.0, -2: 9.0, 3: 1.0, -3: -1.0}
    smooth = {3: 1.0, -3: 1.0, 2: -6.0, -2: -6.0, 1: 15.0, -1: 15.0, 0: -20.0}
    inner = np.zeros((NY, 2 * NY))
    outer = np.zeros((NY, 2 * NY))
    for column, taps in ((0, central), (NY, smooth)):
        for y in range(NY):
            for offset, tap in taps.items():
                at = y + offset
                if 0 <= at < NY:
                    inner[at, column + y] = tap
                elif at < 0:
                    outer[at + 3, column + y] = tap
                else:
                    outer[at - NY + 3, column + y] = tap
    return np.concatenate([inner, inner, outer, outer]).astype(ml_dtypes.bfloat16)


def make_tables():
    east_n, north_n = NX * TILES, NY * BANDS
    vx = window(NX, east_n, RX)
    vy = window(NY, north_n, RY)
    wx = window(NX + 6, east_n, RX)
    wy = window(NY + 6, north_n, RY)
    cells_x = np.arange(NX + 6) - 3
    cells_y = np.arange(NY + 6) - 3
    ux = [basis(east_n, NX * t + np.arange(NX)) @ vx for t in range(TILES)]
    uy = [basis(north_n, NY * b + np.arange(NY)) @ vy for b in range(BANDS)]

    block = np.zeros((PLANES * NX, 128))
    for p in range(PLANES):
        block[p * NX : (p + 1) * NX, p * RX : (p + 1) * RX] = vx
    high, low = halves(block.T)
    x_forward = np.concatenate([high, low], axis=0)
    rows = PLANES * NX
    block = np.zeros((rows + PLANES * 8, 128))
    for p in range(PLANES):
        columns = slice(p * RX, (p + 1) * RX)
        block[p * NX : (p + 1) * NX, columns] = 0.5 * wx[3 : NX + 3]
        block[rows + 8 * p : rows + 8 * p + 3, columns] = 0.5 * wx[:3]
        block[rows + 8 * p + 4 : rows + 8 * p + 7, columns] = 0.5 * wx[NX + 3 :]
    high, low = halves(block)
    x_back = np.concatenate([high, high, low], axis=1)
    shared = sum(block[p * NX : (p + 1) * NX] for p in range(PLANES))
    high, low = halves(shared)
    x_shared = np.concatenate([high, high, low], axis=1)

    high, low = halves(vy.T)
    y_forward = np.concatenate(
        [np.concatenate([high, high], axis=1), np.concatenate([low, 0 * low], axis=1)], axis=0
    )
    both_y = np.zeros((2 * NY, RY))
    both_y[:NY] = wy[3 : NY + 3]
    both_y[NY : NY + 6 * SLOTS] = np.tile(np.concatenate([wy[:3], wy[NY + 3 :]]), (SLOTS, 1))
    high, low = halves(both_y)
    y_back = np.concatenate([high, high, low, 0 * low], axis=1)
    own_slot = np.zeros((2, 128, 128), np.float32)
    for pair in range(2):
        for p in range(PLANES):
            slot = (p // 2) * GLEV + 2 * pair + p % 2
            own_slot[pair, 6 * slot : 6 * slot + 6, p * RX : (p + 1) * RX] = 1

    uy_all = np.concatenate(uy, axis=1)
    m_forward = np.concatenate(halves(uy_all), axis=0)
    uy = [basis(north_n, NY * b + cells_y) @ wy for b in range(BANDS)]
    m_back = np.concatenate(halves(np.concatenate(uy, axis=1).T), axis=0)

    ux_all = np.zeros((MODES, 384))
    for t in range(TILES):
        at = 128 * (t // PER) + RX * (t % PER)
        ux_all[:, at : at + RX] = ux[t]
    k_forward = np.concatenate(halves(ux_all.T), axis=1)
    for t in range(TILES):
        at = 128 * (t // PER) + RX * (t % PER)
        ux_all[:, at : at + RX] = basis(east_n, NX * t + cells_x) @ wx
    k_back = np.concatenate(halves(ux_all), axis=1)

    number = wavenumbers()
    weight_k = np.where(number == 0, 1.0, 2.0) / east_n
    weight_m = np.where(number == 0, 1.0, 2.0) / north_n
    weights = (weight_m[:, None] * weight_k[None, :]).astype(np.float32)
    number_k = np.broadcast_to(number[None, :], (8, MODES)).astype(np.int32)
    number_m = np.broadcast_to(number[:, None], (MODES, MODES)).astype(np.int32)
    return (
        x_forward,
        y_forward,
        m_forward,
        k_forward,
        k_back,
        m_back,
        y_back,
        x_back,
        x_shared,
        own_slot,
        stencil_table(),
        weights,
        number_k,
        number_m,
    )


def split(value):
    high = value.astype(BF)
    low = (value - high.astype(F32)).astype(BF)
    return high, low


def dot(a, b):
    return lax.dot_general(a, b, (((1,), (0,)), ((), ())), preferred_element_type=F32)


def quarters(product, rows, columns):
    return (product[:rows, :columns] + product[:rows, columns:]) + (
        product[rows:, :columns] + product[rows:, columns:]
    )


def kernel(
    wind_east,
    wind_north,
    theta_pert,
    tke_field,
    target_east,
    target_north,
    target_theta,
    turbine_count,
    turbine_type,
    drag_coeff,
    tke_coeff,
    cutoffs,
    *rest,
):
    table_sources, rest = rest[:TABLES], rest[TABLES:]
    tables, rest = rest[4 : 4 + TABLES], rest[:4] + rest[4 + TABLES :]
    step_body(
        wind_east,
        wind_north,
        theta_pert,
        tke_field,
        target_east,
        target_north,
        target_theta,
        turbine_count,
        turbine_type,
        drag_coeff,
        tke_coeff,
        cutoffs,
        table_sources,
        tables,
        *rest,
    )


def step_body(
    wind_east,
    wind_north,
    theta_pert,
    tke_field,
    target_east,
    target_north,
    target_theta,
    turbine_count,
    turbine_type,
    drag_coeff,
    tke_coeff,
    cutoffs,
    table_sources,
    tables,
    east_out,
    north_out,
    theta_out,
    tke_out,
    q0,
    q1,
    q2,
    target,
    tke,
    count,
    kind,
    partial,
    drag,
    force,
    result,
    diffs,
    y_halo,
    xs,
    xr,
    ys,
    yr,
    s1,
    r1,
    s2,
    r2,
    s3,
    r3,
    s4,
    r4,
    modes,
    outer_modes,
    operand,
    in_sem,
    table_sem,
    out_sem,
    xs_sem,
    xr_sem,
    ys_sem,
    yr_sem,
    s1_sem,
    r1_sem,
    s2_sem,
    r2_sem,
    s3_sem,
    r3_sem,
    s4_sem,
    r4_sem,
):
    (
        x_forward,
        y_forward,
        m_forward,
        k_forward,
        k_back,
        m_back,
        y_back,
        x_back,
        x_shared,
        own_slot,
        stencil,
        weights,
        number_k,
        number_m,
    ) = tables
    band = lax.axis_index("band")
    tile = lax.axis_index("tile")

    def field_copies(group):
        rows = pl.ds(group * GLEV, GLEV)
        copies = []
        for f, source in enumerate((wind_east, wind_north, theta_pert)):
            into = q0.at[pl.ds(f * LEV + group * GLEV, GLEV), pl.ds(PAD, NX), :]
            copies.append(pltpu.make_async_copy(source.at[rows], into, in_sem.at[f, group]))
        for f, source in enumerate((target_east, target_north, target_theta)):
            into = target.at[pl.ds(f * LEV + group * GLEV, GLEV)]
            copies.append(pltpu.make_async_copy(source.at[rows], into, in_sem.at[3 + f, group]))
        return copies

    others = [
        pltpu.make_async_copy(source, into, in_sem.at[6 + i, 0])
        for i, (source, into) in enumerate(
            ((tke_field, tke), (turbine_count, count), (turbine_type, kind))
        )
    ]
    table_copies = [
        pltpu.make_async_copy(source, into, table_sem.at[i])
        for i, (source, into) in enumerate(zip(table_sources, tables))
    ]
    for copy in table_copies[:2]:
        copy.start()

    for group in range(1):
        for copy in field_copies(group):
            copy.start()

    barrier = pltpu.get_barrier_semaphore()
    for step in range(1, TILES):
        pl.semaphore_signal(
            barrier, inc=1, device_id={"tile": lax.rem(tile + step, TILES)}, device_id_type=MESH
        )
    for step in range(1, BANDS):
        pl.semaphore_signal(
            barrier, inc=1, device_id={"band": lax.rem(band + step, BANDS)}, device_id_type=MESH
        )

    for group in range(1, GROUPS):
        for copy in field_copies(group):
            copy.start()
    for copy in others + table_copies[2:]:
        copy.start()

    @pl.when(tile == 0)
    def _():
        xr[:, 0] = jnp.zeros((3, GROUPS, SLOTS, 4, 128), F32)

    @pl.when(tile == TILES - 1)
    def _():
        xr[:, 1] = jnp.zeros((3, GROUPS, SLOTS, 4, 128), F32)

    @pl.when(band == 0)
    def _():
        yr[:, 0] = jnp.zeros((3, GROUPS, NX, 128), F32)

    @pl.when(band == BANDS - 1)
    def _():
        yr[:, 1] = jnp.zeros((3, GROUPS, NX, 128), F32)

    lane = lax.broadcasted_iota(jnp.int32, (NX, 128), 1)
    low_lane = lax.rem(lane, 6) < 3


    def pack_edges(turn, group, plane_of):
        packed = jnp.zeros((NX, 128), F32)
        for slot in range(SLOTS):
            plane = plane_of((slot // GLEV) * LEV + group * GLEV + slot % GLEV)
            xs[turn, 0, group, slot, 0:3, :] = plane[0:3]
            xs[turn, 1, group, slot, 0:3, :] = plane[NX - 3 : NX]
            mine = jnp.logical_and(lane >= slot * 6, lane < slot * 6 + 6)
            packed = jnp.where(mine, pltpu.roll(plane, slot * 6 + 3, 1), packed)
        ys[turn, group] = packed

    def interior(source):
        return lambda plane: source[plane, PAD : PAD + NX, :]

    def x_copy(turn, group, side):
        return pltpu.make_async_remote_copy(
            src_ref=xs.at[turn, side, group],
            dst_ref=xr.at[turn, 1 - side, group],
            send_sem=xs_sem.at[turn, side, group],
            recv_sem=xr_sem.at[turn, 1 - side, group],
            device_id={"tile": tile + (1 if side else -1)},
            device_id_type=MESH,
        )

    def y_copy(turn, group, side):
        return pltpu.make_async_remote_copy(
            src_ref=ys.at[turn, group],
            dst_ref=yr.at[turn, 1 - side, group],
            send_sem=ys_sem.at[turn, side, group],
            recv_sem=yr_sem.at[turn, 1 - side, group],
            device_id={"band": band + (1 if side else -1)},
            device_id_type=MESH,
        )

    has = (
        (tile > 0, band > 0),
        (tile < TILES - 1, band < BANDS - 1),
    )

    def send_edges(turn, group):
        for side in range(2):

            @pl.when(has[side][0])
            def _():
                x_copy(turn, group, side).start()

            @pl.when(has[side][1])
            def _():
                y_copy(turn, group, side).start()

    def await_edges(turn, group):
        for side in range(2):

            @pl.when(has[side][0])
            def _():
                x_copy(turn, group, 1 - side).wait_recv()

            @pl.when(has[side][1])
            def _():
                y_copy(turn, group, 1 - side).wait_recv()

    def merged_halo(turn, group):
        return jnp.where(low_lane, yr[turn, 0, group], yr[turn, 1, group])

    def fill_pads(turn, group, source):
        for f in range(FIELDS):
            for inner in range(GLEV):
                plane, slot = f * LEV + group * GLEV + inner, f * GLEV + inner
                source[plane, PAD - 3 : PAD, :] = xr[turn, 0, group, slot, 0:3, :]
                source[plane, PAD + NX : PAD + NX + 3, :] = xr[turn, 1, group, slot, 0:3, :]

    def edges_sent(turn, group):
        for side in range(2):

            @pl.when(has[side][0])
            def _():
                x_copy(turn, group, side).wait_send()

            @pl.when(has[side][1])
            def _():
                y_copy(turn, group, side).wait_send()


    def advance(group, source, finish):
        halo = y_halo[...]
        for slot in range(SLOTS):
            place = (slot % GLEV) * FIELDS + slot // GLEV
            plane = (slot // GLEV) * LEV + group * GLEV + slot % GLEV
            high, low = split(source[plane, PAD : PAD + NX, :])
            halo_high, halo_low = split(pltpu.roll(halo, 128 - slot * 6, 1) if slot else halo)
            operand[place * NX : (place + 1) * NX, :] = jnp.concatenate(
                [high, low, halo_high, halo_low], axis=1
            )


        for inner in range(GLEV):
            level = group * GLEV + inner
            chunk = 16
            own = pl.ds(inner * FIELDS * NX, FIELDS * NX)
            diffs[own, :] = dot(operand[own, :], stencil[...])
            for at in range(0, NX, chunk):
                east = source[level, PAD + at : PAD + at + chunk, :] * (1.0 / 60.0)
                north = source[LEV + level, PAD + at : PAD + at + chunk, :] * (1.0 / 60.0)
                east_size = jnp.abs(east)
                north_size = jnp.abs(north)
                for f in range(FIELDS):
                    plane = f * LEV + level

                    def cell(offset):
                        return source[plane, PAD + at + offset : PAD + at + offset + chunk, :]

                    up1, up2, up3 = cell(1), cell(2), cell(3)
                    down1, down2, down3 = cell(-1), cell(-2), cell(-3)
                    central = 45.0 * (up1 - down1) - 9.0 * (up2 - down2) + (up3 - down3)
                    smooth = (
                        (up3 + down3)
                        - 6.0 * (up2 + down2)
                        + 15.0 * (up1 + down1)
                        - 20.0 * cell(0)
                    )
                    first = (inner * FIELDS + f) * NX + at
                    central_y = diffs[pl.ds(first, chunk), 0:NY]
                    smooth_y = diffs[pl.ds(first, chunk), NY : 2 * NY]
                    value = (east_size * smooth - east * central) + (
                        north_size * smooth_y - north * central_y
                    )
                    finish(f, plane, at, chunk, value)


    def turbines(group):
        counts = count[...].astype(F32)
        kinds = kind[...]

        @pl.loop(0, GLEV)
        def _(inner):
            level = group * GLEV + inner
            rate = jnp.full((NX, NY), drag_coeff[0, level])
            growth = jnp.full((NX, NY), tke_coeff[0, level])
            for k in range(1, NTYPE):
                here = kinds == k
                rate = jnp.where(here, drag_coeff[k, level], rate)
                growth = jnp.where(here, tke_coeff[k, level], growth)
            east = q0[level, PAD : PAD + NX, :]
            north = q0[LEV + level, PAD : PAD + NX, :]
            speed = jnp.sqrt(east * east + north * north)
            rate = counts * rate * speed
            tke[level] = tke[level] + counts * growth * speed * speed * speed
            drag[level] = -(rate * east)
            drag[LEV + level] = -(rate * north)

    def tke_copy(group):
        rows = pl.ds(group * GLEV, GLEV)
        return pltpu.make_async_copy(tke.at[rows], tke_out.at[rows], out_sem.at[3, group])


    for copy in table_copies[:2]:
        copy.wait()

    def coefficients(to):
        rows = []
        for f in range(FIELDS):
            part = pl.ds(f * LEV + 2 * to, 2)
            gap = target[part] - q0[part, PAD : PAD + NX, :]
            rows.append(gap.reshape(2 * NX, NY))
        high, low = split(jnp.concatenate(rows, axis=0))
        along_x = quarters(dot(x_forward[...], jnp.concatenate([high, low], axis=1)), 128, NY)
        both = lax.dot_general(
            y_forward[...],
            jnp.concatenate(split(along_x), axis=1),
            (((1,), (1,)), ((), ())),
            preferred_element_type=F32,
        )
        s1[to] = both[:RY] + both[RY:]

    @pl.loop(0, GROUPS)
    def _(group):
        for copy in field_copies(group):
            copy.wait()
        for pair in range(2):
            coefficients(2 * group + pair)

    pl.semaphore_wait(barrier, BANDS - 1 + TILES - 1)

    def partners(axis):
        if axis == "band":
            return [lax.rem(band + step, BANDS) for step in (4, 3, 5, 2, 6, 1, 7)]
        apart = sorted(
            ((dx, dz) for dx in range(4) for dz in range(4) if dx or dz),
            key=lambda at: -(min(at[0], 4 - at[0]) + min(at[1], 4 - at[1])),
        )
        x, z = tile // 4, lax.rem(tile, 4)
        return [lax.rem(x + dx, 4) * 4 + lax.rem(z + dz, 4) for dx, dz in apart]

    def outgoing(axis, me, source, into, send_sem, recv_sem, other):
        return pltpu.make_async_remote_copy(
            src_ref=source.at[other],
            dst_ref=into.at[me],
            send_sem=send_sem.at[other],
            recv_sem=recv_sem.at[me],
            device_id={axis: other},
            device_id_type=MESH,
        )

    def send_all(axis, me, source, into, send_sem, recv_sem):
        for other in partners(axis):
            outgoing(axis, me, source, into, send_sem, recv_sem, other).start()
        into[me] = source[me]

    def receive_all(axis, me, source, into, send_sem, recv_sem):
        for other in partners(axis)[::-1]:
            pltpu.make_async_remote_copy(
                src_ref=source.at[other],
                dst_ref=into.at[other],
                send_sem=send_sem.at[other],
                recv_sem=recv_sem.at[other],
                device_id={axis: other},
                device_id_type=MESH,
            ).wait_recv()

    def sent_all(axis, me, source, into, send_sem, recv_sem):
        for other in partners(axis):
            outgoing(axis, me, source, into, send_sem, recv_sem, other).wait_send()

    phase1 = ("band", band, s1, r1, s1_sem, r1_sem)
    phase2 = ("tile", tile, s2, r2, s2_sem, r2_sem)
    phase3 = ("tile", tile, s3, r3, s3_sem, r3_sem)
    phase4 = ("band", band, s4, r4, s4_sem, r4_sem)

    send_all(*phase1)

    @pl.loop(0, GROUPS)
    def _(group):
        pack_edges(0, group, interior(q0))
        send_edges(0, group)

    for copy in others + table_copies[2:]:
        copy.wait()

    @pl.loop(0, GROUPS)
    def _(group):
        turbines(group)
        tke_copy(group).start()

    third = 1.0 / 3.0

    def first_finish(f, plane, at, chunk, value):
        if f < 2:
            value = value + drag[plane, at : at + chunk, :]
        partial[plane, at : at + chunk, :] = (
            q0[plane, PAD + at : PAD + at + chunk, :] + third * value
        )

    def first_stage(group):
        await_edges(0, group)
        fill_pads(0, group, q0)
        y_halo[...] = merged_halo(0, group)
        advance(group, q0, first_finish)
        pack_edges(1, group, lambda plane: partial[plane])
        send_edges(1, group)

    receive_all(*phase1)

    received = r1[...].reshape(BANDS * RY, 128)
    columns = jnp.concatenate(split(received), axis=1)
    s2[...] = quarters(dot(m_forward[...], columns), MODES, 128).reshape(TILES, 8, 128)
    send_all(*phase2)

    @pl.loop(0, GROUPS)
    def _(group):
        first_stage(group)

    receive_all(*phase2)

    lane8 = lax.broadcasted_iota(jnp.int32, (8, 128), 1)
    inside = [
        jnp.logical_and(lane8 >= RX * i, lane8 < RX * (i + 1)) for i in range(PER)
    ]
    blocks = [r2[t] for t in range(TILES)]
    rows = []
    for p in range(PLANES):
        parts = []
        for first in range(0, TILES, PER):
            value = jnp.zeros((8, 128), F32)
            for i, t in enumerate(range(first, min(first + PER, TILES))):
                moved = pltpu.roll(blocks[t], (RX * (i - p)) % 128, 1)
                value = jnp.where(inside[i], moved, value)
            parts.append(value)
        rows.append(jnp.concatenate(parts, axis=1))
    packed = jnp.concatenate(split(jnp.concatenate(rows, axis=0)), axis=0)
    spectra = quarters(dot(packed, k_forward[...]), 8 * PLANES, MODES)
    mine = pl.ds(pl.multiple_of(tile * 8, 8), 8)
    weight = weights[mine, :]
    east_number = number_k[...]
    north_number = number_m[mine, :]
    masks = []
    for inner in range(2):
        keep = jnp.logical_and(
            east_number <= cutoffs[0, 2 * band + inner],
            north_number <= cutoffs[1, 2 * band + inner],
        )
        masks.append(jnp.where(keep, weight, 0.0))
    spectra = spectra * jnp.concatenate(masks * FIELDS, axis=0)
    high, low = split(spectra)
    back = dot(jnp.concatenate([high, low], axis=0), k_back[...])
    back = quarters(back, 8 * PLANES, 384)
    for t in range(TILES):
        first = 128 * (t // PER)
        value = jnp.zeros((8, 128), F32)
        for p in range(PLANES):
            moved = pltpu.roll(
                back[8 * p : 8 * p + 8, first : first + 128], (RX * (p - t % PER)) % 128, 1
            )
            value = jnp.where(inside[p], moved, value)
        s3[t] = value
    send_all(*phase3)

    receive_all(*phase3)

    received = r3[...].reshape(MODES, 128)
    back = quarters(dot(m_back[...], jnp.concatenate(split(received), axis=1)), BANDS * RY, 128)
    s4[...] = back.reshape(BANDS, RY, 128)
    send_all(*phase4)
    for phase in (phase1, phase2, phase3):
        sent_all(*phase)

    @pl.loop(0, GROUPS)
    def _(group):
        edges_sent(0, group)
        edges_sent(1, group)
        tke_copy(group).wait()
        await_edges(1, group)

    receive_all(*phase4)

    columns = []
    for of in range(BANDS):
        high, low = split(r4[of])
        columns.append(jnp.concatenate([high, low, high, jnp.zeros((RY, 128), BF)], axis=0))
    wide = dot(y_back[...], jnp.concatenate(columns, axis=1))
    for of in range(BANDS):
        modes[of] = wide[:NY, of * 128 : (of + 1) * 128]
    for group in range(GROUPS):
        first = 2 * group * 128
        outer_modes[group] = (
            wide[NY:, first : first + 128] * own_slot[0]
            + wide[NY:, first + 128 : first + 256] * own_slot[1]
        )

    def across(table, value):
        high, low = split(value)
        return lax.dot_general(
            table,
            jnp.concatenate([high, low, high], axis=1),
            (((1,), (1,)), ((), ())),
            preferred_element_type=F32,
        )

    inside_x = [jnp.where(flag[0], third, 0.0) for flag in has]
    inside_y = jnp.where(
        low_lane, jnp.where(has[0][1], third, 0.0), jnp.where(has[1][1], third, 0.0)
    )

    def second_finish(f, plane, at, chunk, value):
        q2[plane, PAD + at : PAD + at + chunk, :] = q0[
            plane, PAD + at : PAD + at + chunk, :
        ] + 0.5 * (value + force[plane, at : at + chunk, :])

    @pl.loop(0, GROUPS)
    def _(group):
        outer = across(x_shared[...], outer_modes[group])
        pairs = modes[pl.ds(2 * group, 2)].reshape(2 * NY, 128)
        smooth_pairs = across(x_back[...], pairs)
        for pair in range(2):
            smooth_part = smooth_pairs[:, pair * NY : (pair + 1) * NY]
            for f in range(FIELDS):
                for inner in range(2):
                    plane = f * LEV + group * GLEV + 2 * pair + inner
                    slot = f * GLEV + 2 * pair + inner
                    p = 2 * f + inner
                    nudge = smooth_part[p * NX : (p + 1) * NX]
                    if f < 2:
                        force[plane] = nudge + drag[plane]
                    else:
                        force[plane] = nudge
                    q1[plane, PAD : PAD + NX, :] = partial[plane] + third * nudge
                    for side, into in ((0, PAD - 3), (1, PAD + NX)):
                        first = PLANES * NX + 8 * p + 4 * side
                        q1[plane, into : into + 3, :] = xr[
                            1, side, group, slot, 0:3, :
                        ] + smooth_part[first : first + 3] * inside_x[side]
        y_halo[...] = merged_halo(1, group) + outer * inside_y

        advance(group, q1, second_finish)
        pack_edges(2, group, interior(q2))
        send_edges(2, group)

    def third_finish(f, plane, at, chunk, value):
        result[plane, at : at + chunk, :] = q0[plane, PAD + at : PAD + at + chunk, :] + (
            value + force[plane, at : at + chunk, :]
        )

    def out_copy(f, group):
        rows = pl.ds(group * GLEV, GLEV)
        into = (east_out, north_out, theta_out)[f]
        return pltpu.make_async_copy(
            result.at[pl.ds(f * LEV + group * GLEV, GLEV)], into.at[rows], out_sem.at[f, group]
        )

    @pl.loop(0, GROUPS)
    def _(group):
        await_edges(2, group)
        fill_pads(2, group, q2)
        y_halo[...] = merged_halo(2, group)
        advance(group, q2, third_finish)
        for f in range(FIELDS):
            out_copy(f, group).start()

    sent_all(*phase4)

    @pl.loop(0, GROUPS)
    def _(group):
        edges_sent(2, group)
        for f in range(FIELDS):
            out_copy(f, group).wait()


PARTS = 2


def deliver(*refs):
    sources, results, held, in_sems, out_sems = refs[:4], refs[4:8], refs[8], refs[9], refs[10]
    inward, outward = [], []
    for j in range(PARTS):
        rows = pl.ds(j * (LEV // PARTS), LEV // PARTS)
        for i in range(4):
            inward.append(
                pltpu.make_async_copy(sources[i].at[rows], held.at[i, rows], in_sems.at[i, j])
            )
            outward.append(
                pltpu.make_async_copy(held.at[i, rows], results[i].at[rows], out_sems.at[i, j])
            )
    for copy in inward:
        copy.start()
    for first, second in zip(inward, outward):
        first.wait()
        second.start()
    for copy in outward:
        copy.wait()


def shards(*arguments):
    tables = [jnp.asarray(table) for table in make_tables()]
    field = jax.ShapeDtypeStruct((LEV, NX, NY), F32)
    anywhere = pl.BlockSpec(memory_space=pl.ANY)
    smem = pl.BlockSpec(memory_space=pltpu.SMEM)
    padded = pltpu.VMEM((FIELDS * LEV, NX + 2 * PAD, NY), F32)
    planes = pltpu.VMEM((FIELDS * LEV, NX, NY), F32)
    dma = pltpu.SemaphoreType.DMA
    outcome = pl.pallas_call(
        kernel,
        out_shape=(field,) * 4,
        in_specs=[anywhere] * 9 + [smem] * 3 + [anywhere] * TABLES,
        out_specs=(anywhere,) * 4,
        scratch_shapes=[pltpu.VMEM(table.shape, table.dtype) for table in tables]
        + [
            padded,
            padded,
            padded,
            planes,
            pltpu.VMEM((LEV, NX, NY), F32),
            pltpu.VMEM((NX, NY), jnp.int32),
            pltpu.VMEM((NX, NY), jnp.int32),
            planes,
            pltpu.VMEM((2 * LEV, NX, NY), F32),
            planes,
            planes,
            pltpu.VMEM((SLOTS * NX, 2 * NY), F32),
            pltpu.VMEM((NX, 128), F32),
            pltpu.VMEM((3, 2, GROUPS, SLOTS, 4, 128), F32),
            pltpu.VMEM((3, 2, GROUPS, SLOTS, 4, 128), F32),
            pltpu.VMEM((3, GROUPS, NX, 128), F32),
            pltpu.VMEM((3, 2, GROUPS, NX, 128), F32),
            pltpu.VMEM((BANDS, RY, 128), F32),
            pltpu.VMEM((BANDS, RY, 128), F32),
            pltpu.VMEM((TILES, 8, 128), F32),
            pltpu.VMEM((TILES, 8, 128), F32),
            pltpu.VMEM((TILES, 8, 128), F32),
            pltpu.VMEM((TILES, 8, 128), F32),
            pltpu.VMEM((BANDS, RY, 128), F32),
            pltpu.VMEM((BANDS, RY, 128), F32),
            pltpu.VMEM((BANDS, NY, 128), F32),
            pltpu.VMEM((GROUPS, NY, 128), F32),
            pltpu.VMEM((SLOTS * NX, 4 * NY), BF),
            dma((9, GROUPS)),
            dma((TABLES,)),
            dma((4, GROUPS)),
            dma((3, 2, GROUPS)),
            dma((3, 2, GROUPS)),
            dma((3, 2, GROUPS)),
            dma((3, 2, GROUPS)),
            dma((BANDS,)),
            dma((BANDS,)),
            dma((TILES,)),
            dma((TILES,)),
            dma((TILES,)),
            dma((TILES,)),
            dma((BANDS,)),
            dma((BANDS,)),
        ],
        compiler_params=pltpu.CompilerParams(
            collective_id=0, has_side_effects=True, vmem_limit_bytes=61 * 1024 * 1024
        ),
        cost_estimate=pl.CostEstimate(
            flops=10**9, bytes_accessed=6 * 2**20, transcendentals=LEV * NX * NY
        ),
        name="step",
    )(*arguments, *tables)
    return pl.pallas_call(
        deliver,
        out_shape=(field,) * 4,
        in_specs=[anywhere] * 4,
        out_specs=(anywhere,) * 4,
        scratch_shapes=[
            pltpu.VMEM((4, LEV, NX, NY), F32),
            dma((4, PARTS)),
            dma((4, PARTS)),
        ],
        compiler_params=pltpu.CompilerParams(vmem_limit_bytes=61 * 1024 * 1024),
        name="deliver",
    )(*outcome)


def solution(mesh):
    field = P(None, "tile", "band")
    column = P("tile", "band")
    in_specs = (field,) * 7 + (column,) * 2 + (P(),) * 3
    return jax.shard_map(
        shards, mesh=mesh, in_specs=in_specs, out_specs=(field,) * 4, check_vma=False
    )
```

```python
import functools

import jax
import jax.numpy as jnp
import ml_dtypes
import numpy as np
from jax import lax
from jax.experimental import pallas as pl
from jax.experimental.pallas import tpu as pltpu
from jax.sharding import PartitionSpec as P

KMAX = 64
MODES = 2 * KMAX
NTYPE = 8
LEV = 16
FIELDS = 3
BANDS = 8
TILES = 16
NX = 64
NY = 128
RX = 21
RY = 32
PLANES = 6
GROUPS = 4
GLEV = LEV // GROUPS
SLOTS = FIELDS * GLEV
PER = 6
PAD = 8
TABLES = 14
MESH = pl.DeviceIdType.MESH
BF = jnp.bfloat16
F32 = jnp.float32


def wavenumbers():
    index = np.arange(MODES)
    return np.where(index < KMAX, index, index - KMAX + 1)


def basis(extent, positions):
    number = wavenumbers()
    angle = 2 * np.pi * ((number[:, None] * positions[None, :]) % extent) / extent
    return np.where((np.arange(MODES) < KMAX)[:, None], np.cos(angle), np.sin(angle))


def window(length, extent, rank):
    index = np.arange(length)
    half = (KMAX + 0.5) / extent
    diagonal = ((length - 1 - 2 * index) / 2) ** 2 * np.cos(2 * np.pi * half)
    beside = index[1:] * (length - index[1:]) / 2
    _, vectors = np.linalg.eigh(np.diag(diagonal) + np.diag(beside, 1) + np.diag(beside, -1))
    vectors = vectors[:, ::-1][:, :rank]
    largest = vectors[np.argmax(np.abs(vectors) > 0.02, axis=0), np.arange(rank)]
    return vectors * np.sign(largest)


def halves(table):
    high = table.astype(np.float32).astype(ml_dtypes.bfloat16)
    low = (table - high.astype(np.float64)).astype(np.float32).astype(ml_dtypes.bfloat16)
    return high, low


def stencil_table():
    central = {1: 45.0, -1: -45.0, 2: -9.0, -2: 9.0, 3: 1.0, -3: -1.0}
    smooth = {3: 1.0, -3: 1.0, 2: -6.0, -2: -6.0, 1: 15.0, -1: 15.0, 0: -20.0}
    inner = np.zeros((NY, 2 * NY))
    outer = np.zeros((NY, 2 * NY))
    for column, taps in ((0, central), (NY, smooth)):
        for y in range(NY):
            for offset, tap in taps.items():
                at = y + offset
                if 0 <= at < NY:
                    inner[at, column + y] = tap
                elif at < 0:
                    outer[at + 3, column + y] = tap
                else:
                    outer[at - NY + 3, column + y] = tap
    return np.concatenate([inner, inner, outer, outer]).astype(ml_dtypes.bfloat16)


def make_tables():
    east_n, north_n = NX * TILES, NY * BANDS
    vx = window(NX, east_n, RX)
    vy = window(NY, north_n, RY)
    wx = window(NX + 6, east_n, RX)
    wy = window(NY + 6, north_n, RY)
    cells_x = np.arange(NX + 6) - 3
    cells_y = np.arange(NY + 6) - 3
    ux = [basis(east_n, NX * t + np.arange(NX)) @ vx for t in range(TILES)]
    uy = [basis(north_n, NY * b + np.arange(NY)) @ vy for b in range(BANDS)]

    block = np.zeros((PLANES * NX, 128))
    for p in range(PLANES):
        block[p * NX : (p + 1) * NX, p * RX : (p + 1) * RX] = vx
    high, low = halves(block.T)
    x_forward = np.concatenate([high, low], axis=0)
    rows = PLANES * NX
    block = np.zeros((rows + PLANES * 8, 128))
    for p in range(PLANES):
        columns = slice(p * RX, (p + 1) * RX)
        block[p * NX : (p + 1) * NX, columns] = 0.5 * wx[3 : NX + 3]
        block[rows + 8 * p : rows + 8 * p + 3, columns] = 0.5 * wx[:3]
        block[rows + 8 * p + 4 : rows + 8 * p + 7, columns] = 0.5 * wx[NX + 3 :]
    high, low = halves(block)
    x_back = np.concatenate([high, high, low], axis=1)
    shared = sum(block[p * NX : (p + 1) * NX] for p in range(PLANES))
    high, low = halves(shared)
    x_shared = np.concatenate([high, high, low], axis=1)

    high, low = halves(vy.T)
    y_forward = np.concatenate(
        [np.concatenate([high, high], axis=1), np.concatenate([low, 0 * low], axis=1)], axis=0
    )
    both_y = np.zeros((2 * NY, RY))
    both_y[:NY] = wy[3 : NY + 3]
    both_y[NY : NY + 6 * SLOTS] = np.tile(np.concatenate([wy[:3], wy[NY + 3 :]]), (SLOTS, 1))
    high, low = halves(both_y)
    y_back = np.concatenate([high, high, low, 0 * low], axis=1)
    own_slot = np.zeros((2, 128, 128), np.float32)
    for pair in range(2):
        for p in range(PLANES):
            slot = (p // 2) * GLEV + 2 * pair + p % 2
            own_slot[pair, 6 * slot : 6 * slot + 6, p * RX : (p + 1) * RX] = 1

    uy_all = np.concatenate(uy, axis=1)
    m_forward = np.concatenate(halves(uy_all), axis=0)
    uy = [basis(north_n, NY * b + cells_y) @ wy for b in range(BANDS)]
    m_back = np.concatenate(halves(np.concatenate(uy, axis=1).T), axis=0)

    ux_all = np.zeros((MODES, 384))
    for t in range(TILES):
        at = 128 * (t // PER) + RX * (t % PER)
        ux_all[:, at : at + RX] = ux[t]
    k_forward = np.concatenate(halves(ux_all.T), axis=1)
    for t in range(TILES):
        at = 128 * (t // PER) + RX * (t % PER)
        ux_all[:, at : at + RX] = basis(east_n, NX * t + cells_x) @ wx
    k_back = np.concatenate(halves(ux_all), axis=1)

    number = wavenumbers()
    weight_k = np.where(number == 0, 1.0, 2.0) / east_n
    weight_m = np.where(number == 0, 1.0, 2.0) / north_n
    weights = (weight_m[:, None] * weight_k[None, :]).astype(np.float32)
    number_k = np.broadcast_to(number[None, :], (8, MODES)).astype(np.int32)
    number_m = np.broadcast_to(number[:, None], (MODES, MODES)).astype(np.int32)
    return (
        x_forward,
        y_forward,
        m_forward,
        k_forward,
        k_back,
        m_back,
        y_back,
        x_back,
        x_shared,
        own_slot,
        stencil_table(),
        weights,
        number_k,
        number_m,
    )


def split(value):
    high = value.astype(BF)
    low = (value - high.astype(F32)).astype(BF)
    return high, low


def dot(a, b):
    return lax.dot_general(a, b, (((1,), (0,)), ((), ())), preferred_element_type=F32)


def quarters(product, rows, columns):
    return (product[:rows, :columns] + product[:rows, columns:]) + (
        product[rows:, :columns] + product[rows:, columns:]
    )


def kernel(
    wind_east,
    wind_north,
    theta_pert,
    tke_field,
    target_east,
    target_north,
    target_theta,
    turbine_count,
    turbine_type,
    drag_coeff,
    tke_coeff,
    cutoffs,
    *rest,
):
    table_sources, rest = rest[:TABLES], rest[TABLES:]
    tables, rest = rest[4 : 4 + TABLES], rest[:4] + rest[4 + TABLES :]
    step_body(
        wind_east,
        wind_north,
        theta_pert,
        tke_field,
        target_east,
        target_north,
        target_theta,
        turbine_count,
        turbine_type,
        drag_coeff,
        tke_coeff,
        cutoffs,
        table_sources,
        tables,
        *rest,
    )


def step_body(
    wind_east,
    wind_north,
    theta_pert,
    tke_field,
    target_east,
    target_north,
    target_theta,
    turbine_count,
    turbine_type,
    drag_coeff,
    tke_coeff,
    cutoffs,
    table_sources,
    tables,
    east_out,
    north_out,
    theta_out,
    tke_out,
    q0,
    q1,
    q2,
    target,
    tke,
    count,
    kind,
    partial,
    drag,
    force,
    result,
    diffs,
    y_halo,
    xs,
    xr,
    ys,
    yr,
    s1,
    r1,
    s2,
    r2,
    s3,
    r3,
    s4,
    r4,
    modes,
    outer_modes,
    operand,
    in_sem,
    table_sem,
    out_sem,
    xs_sem,
    xr_sem,
    ys_sem,
    yr_sem,
    s1_sem,
    r1_sem,
    s2_sem,
    r2_sem,
    s3_sem,
    r3_sem,
    s4_sem,
    r4_sem,
):
    (
        x_forward,
        y_forward,
        m_forward,
        k_forward,
        k_back,
        m_back,
        y_back,
        x_back,
        x_shared,
        own_slot,
        stencil,
        weights,
        number_k,
        number_m,
    ) = tables
    band = lax.axis_index("band")
    tile = lax.axis_index("tile")

    def field_copies(group):
        rows = pl.ds(group * GLEV, GLEV)
        copies = []
        for f, source in enumerate((wind_east, wind_north, theta_pert)):
            into = q0.at[pl.ds(f * LEV + group * GLEV, GLEV), pl.ds(PAD, NX), :]
            copies.append(pltpu.make_async_copy(source.at[rows], into, in_sem.at[f, group]))
        for f, source in enumerate((target_east, target_north, target_theta)):
            into = target.at[pl.ds(f * LEV + group * GLEV, GLEV)]
            copies.append(pltpu.make_async_copy(source.at[rows], into, in_sem.at[3 + f, group]))
        return copies

    others = [
        pltpu.make_async_copy(source, into, in_sem.at[6 + i, 0])
        for i, (source, into) in enumerate(
            ((tke_field, tke), (turbine_count, count), (turbine_type, kind))
        )
    ]
    table_copies = [
        pltpu.make_async_copy(source, into, table_sem.at[i])
        for i, (source, into) in enumerate(zip(table_sources, tables))
    ]
    for copy in table_copies[:2]:
        copy.start()

    for group in range(1):
        for copy in field_copies(group):
            copy.start()

    barrier = pltpu.get_barrier_semaphore()
    for step in range(1, TILES):
        pl.semaphore_signal(
            barrier, inc=1, device_id={"tile": lax.rem(tile + step, TILES)}, device_id_type=MESH
        )
    for step in range(1, BANDS):
        pl.semaphore_signal(
            barrier, inc=1, device_id={"band": lax.rem(band + step, BANDS)}, device_id_type=MESH
        )

    for group in range(1, GROUPS):
        for copy in field_copies(group):
            copy.start()
    for copy in others + table_copies[2:]:
        copy.start()

    @pl.when(tile == 0)
    def _():
        xr[:, 0] = jnp.zeros((3, GROUPS, SLOTS, 4, 128), F32)

    @pl.when(tile == TILES - 1)
    def _():
        xr[:, 1] = jnp.zeros((3, GROUPS, SLOTS, 4, 128), F32)

    @pl.when(band == 0)
    def _():
        yr[:, 0] = jnp.zeros((3, GROUPS, NX, 128), F32)

    @pl.when(band == BANDS - 1)
    def _():
        yr[:, 1] = jnp.zeros((3, GROUPS, NX, 128), F32)

    lane = lax.broadcasted_iota(jnp.int32, (NX, 128), 1)
    low_lane = lax.rem(lane, 6) < 3


    def pack_edges(turn, group, plane_of):
        packed = jnp.zeros((NX, 128), F32)
        for slot in range(SLOTS):
            plane = plane_of((slot // GLEV) * LEV + group * GLEV + slot % GLEV)
            xs[turn, 0, group, slot, 0:3, :] = plane[0:3]
            xs[turn, 1, group, slot, 0:3, :] = plane[NX - 3 : NX]
            mine = jnp.logical_and(lane >= slot * 6, lane < slot * 6 + 6)
            packed = jnp.where(mine, pltpu.roll(plane, slot * 6 + 3, 1), packed)
        ys[turn, group] = packed

    def interior(source):
        return lambda plane: source[plane, PAD : PAD + NX, :]

    def x_copy(turn, group, side):
        return pltpu.make_async_remote_copy(
            src_ref=xs.at[turn, side, group],
            dst_ref=xr.at[turn, 1 - side, group],
            send_sem=xs_sem.at[turn, side, group],
            recv_sem=xr_sem.at[turn, 1 - side, group],
            device_id={"tile": tile + (1 if side else -1)},
            device_id_type=MESH,
        )

    def y_copy(turn, group, side):
        return pltpu.make_async_remote_copy(
            src_ref=ys.at[turn, group],
            dst_ref=yr.at[turn, 1 - side, group],
            send_sem=ys_sem.at[turn, side, group],
            recv_sem=yr_sem.at[turn, 1 - side, group],
            device_id={"band": band + (1 if side else -1)},
            device_id_type=MESH,
        )

    has = (
        (tile > 0, band > 0),
        (tile < TILES - 1, band < BANDS - 1),
    )

    def send_edges(turn, group):
        for side in range(2):

            @pl.when(has[side][0])
            def _():
                x_copy(turn, group, side).start()

            @pl.when(has[side][1])
            def _():
                y_copy(turn, group, side).start()

    def await_edges(turn, group):
        for side in range(2):

            @pl.when(has[side][0])
            def _():
                x_copy(turn, group, 1 - side).wait_recv()

            @pl.when(has[side][1])
            def _():
                y_copy(turn, group, 1 - side).wait_recv()

    def merged_halo(turn, group):
        return jnp.where(low_lane, yr[turn, 0, group], yr[turn, 1, group])

    def fill_pads(turn, group, source):
        for f in range(FIELDS):
            for inner in range(GLEV):
                plane, slot = f * LEV + group * GLEV + inner, f * GLEV + inner
                source[plane, PAD - 3 : PAD, :] = xr[turn, 0, group, slot, 0:3, :]
                source[plane, PAD + NX : PAD + NX + 3, :] = xr[turn, 1, group, slot, 0:3, :]

    def edges_sent(turn, group):
        for side in range(2):

            @pl.when(has[side][0])
            def _():
                x_copy(turn, group, side).wait_send()

            @pl.when(has[side][1])
            def _():
                y_copy(turn, group, side).wait_send()


    def advance(group, source, finish):
        halo = y_halo[...]
        for slot in range(SLOTS):
            place = (slot % GLEV) * FIELDS + slot // GLEV
            plane = (slot // GLEV) * LEV + group * GLEV + slot % GLEV
            high, low = split(source[plane, PAD : PAD + NX, :])
            halo_high, halo_low = split(pltpu.roll(halo, 128 - slot * 6, 1) if slot else halo)
            operand[place * NX : (place + 1) * NX, :] = jnp.concatenate(
                [high, low, halo_high, halo_low], axis=1
            )


        for inner in range(GLEV):
            level = group * GLEV + inner
            chunk = 32
            own = pl.ds(inner * FIELDS * NX, FIELDS * NX)
            diffs[own, :] = dot(operand[own, :], stencil[...])
            for at in range(0, NX, chunk):
                east = source[level, PAD + at : PAD + at + chunk, :] * (1.0 / 60.0)
                north = source[LEV + level, PAD + at : PAD + at + chunk, :] * (1.0 / 60.0)
                east_size = jnp.abs(east)
                north_size = jnp.abs(north)
                for f in range(FIELDS):
                    plane = f * LEV + level

                    def cell(offset):
                        return source[plane, PAD + at + offset : PAD + at + offset + chunk, :]

                    up1, up2, up3 = cell(1), cell(2), cell(3)
                    down1, down2, down3 = cell(-1), cell(-2), cell(-3)
                    central = 45.0 * (up1 - down1) - 9.0 * (up2 - down2) + (up3 - down3)
                    smooth = (
                        (up3 + down3)
                        - 6.0 * (up2 + down2)
                        + 15.0 * (up1 + down1)
                        - 20.0 * cell(0)
                    )
                    first = (inner * FIELDS + f) * NX + at
                    central_y = diffs[pl.ds(first, chunk), 0:NY]
                    smooth_y = diffs[pl.ds(first, chunk), NY : 2 * NY]
                    value = (east_size * smooth - east * central) + (
                        north_size * smooth_y - north * central_y
                    )
                    finish(f, plane, at, chunk, value)


    def turbines(group):
        counts = count[...].astype(F32)
        kinds = kind[...]

        @pl.loop(0, GLEV)
        def _(inner):
            level = group * GLEV + inner
            rate = jnp.full((NX, NY), drag_coeff[0, level])
            growth = jnp.full((NX, NY), tke_coeff[0, level])
            for k in range(1, NTYPE):
                here = kinds == k
                rate = jnp.where(here, drag_coeff[k, level], rate)
                growth = jnp.where(here, tke_coeff[k, level], growth)
            east = q0[level, PAD : PAD + NX, :]
            north = q0[LEV + level, PAD : PAD + NX, :]
            speed = jnp.sqrt(east * east + north * north)
            rate = counts * rate * speed
            tke[level] = tke[level] + counts * growth * speed * speed * speed
            drag[level] = -(rate * east)
            drag[LEV + level] = -(rate * north)

    def tke_copy(group):
        rows = pl.ds(group * GLEV, GLEV)
        return pltpu.make_async_copy(tke.at[rows], tke_out.at[rows], out_sem.at[3, group])


    for copy in table_copies[:2]:
        copy.wait()

    def coefficients(to):
        rows = []
        for f in range(FIELDS):
            part = pl.ds(f * LEV + 2 * to, 2)
            gap = target[part] - q0[part, PAD : PAD + NX, :]
            rows.append(gap.reshape(2 * NX, NY))
        high, low = split(jnp.concatenate(rows, axis=0))
        along_x = quarters(dot(x_forward[...], jnp.concatenate([high, low], axis=1)), 128, NY)
        both = lax.dot_general(
            y_forward[...],
            jnp.concatenate(split(along_x), axis=1),
            (((1,), (1,)), ((), ())),
            preferred_element_type=F32,
        )
        s1[to] = both[:RY] + both[RY:]

    @pl.loop(0, GROUPS)
    def _(group):
        for copy in field_copies(group):
            copy.wait()
        for pair in range(2):
            coefficients(2 * group + pair)

    pl.semaphore_wait(barrier, BANDS - 1 + TILES - 1)

    def partners(axis):
        if axis == "band":
            return [lax.rem(band + step, BANDS) for step in (4, 3, 5, 2, 6, 1, 7)]
        apart = sorted(
            ((dx, dz) for dx in range(4) for dz in range(4) if dx or dz),
            key=lambda at: -(min(at[0], 4 - at[0]) + min(at[1], 4 - at[1])),
        )
        x, z = tile // 4, lax.rem(tile, 4)
        return [lax.rem(x + dx, 4) * 4 + lax.rem(z + dz, 4) for dx, dz in apart]

    def outgoing(axis, me, source, into, send_sem, recv_sem, other):
        return pltpu.make_async_remote_copy(
            src_ref=source.at[other],
            dst_ref=into.at[me],
            send_sem=send_sem.at[other],
            recv_sem=recv_sem.at[me],
            device_id={axis: other},
            device_id_type=MESH,
        )

    def send_all(axis, me, source, into, send_sem, recv_sem):
        for other in partners(axis):
            outgoing(axis, me, source, into, send_sem, recv_sem, other).start()
        into[me] = source[me]

    def receive_all(axis, me, source, into, send_sem, recv_sem):
        for other in partners(axis)[::-1]:
            pltpu.make_async_remote_copy(
                src_ref=source.at[other],
                dst_ref=into.at[other],
                send_sem=send_sem.at[other],
                recv_sem=recv_sem.at[other],
                device_id={axis: other},
                device_id_type=MESH,
            ).wait_recv()

    def sent_all(axis, me, source, into, send_sem, recv_sem):
        for other in partners(axis):
            outgoing(axis, me, source, into, send_sem, recv_sem, other).wait_send()

    phase1 = ("band", band, s1, r1, s1_sem, r1_sem)
    phase2 = ("tile", tile, s2, r2, s2_sem, r2_sem)
    phase3 = ("tile", tile, s3, r3, s3_sem, r3_sem)
    phase4 = ("band", band, s4, r4, s4_sem, r4_sem)

    send_all(*phase1)

    @pl.loop(0, GROUPS)
    def _(group):
        pack_edges(0, group, interior(q0))
        send_edges(0, group)

    for copy in others + table_copies[2:]:
        copy.wait()

    @pl.loop(0, GROUPS)
    def _(group):
        turbines(group)
        tke_copy(group).start()

    third = 1.0 / 3.0

    def first_finish(f, plane, at, chunk, value):
        if f < 2:
            value = value + drag[plane, at : at + chunk, :]
        partial[plane, at : at + chunk, :] = (
            q0[plane, PAD + at : PAD + at + chunk, :] + third * value
        )

    def first_stage(group):
        await_edges(0, group)
        fill_pads(0, group, q0)
        y_halo[...] = merged_halo(0, group)
        advance(group, q0, first_finish)
        pack_edges(1, group, lambda plane: partial[plane])
        send_edges(1, group)

    receive_all(*phase1)

    received = r1[...].reshape(BANDS * RY, 128)
    columns = jnp.concatenate(split(received), axis=1)
    s2[...] = quarters(dot(m_forward[...], columns), MODES, 128).reshape(TILES, 8, 128)
    send_all(*phase2)

    @pl.loop(0, GROUPS)
    def _(group):
        first_stage(group)

    receive_all(*phase2)

    lane8 = lax.broadcasted_iota(jnp.int32, (8, 128), 1)
    inside = [
        jnp.logical_and(lane8 >= RX * i, lane8 < RX * (i + 1)) for i in range(PER)
    ]
    blocks = [r2[t] for t in range(TILES)]
    rows = []
    for p in range(PLANES):
        parts = []
        for first in range(0, TILES, PER):
            value = jnp.zeros((8, 128), F32)
            for i, t in enumerate(range(first, min(first + PER, TILES))):
                moved = pltpu.roll(blocks[t], (RX * (i - p)) % 128, 1)
                value = jnp.where(inside[i], moved, value)
            parts.append(value)
        rows.append(jnp.concatenate(parts, axis=1))
    packed = jnp.concatenate(split(jnp.concatenate(rows, axis=0)), axis=0)
    spectra = quarters(dot(packed, k_forward[...]), 8 * PLANES, MODES)
    mine = pl.ds(pl.multiple_of(tile * 8, 8), 8)
    weight = weights[mine, :]
    east_number = number_k[...]
    north_number = number_m[mine, :]
    masks = []
    for inner in range(2):
        keep = jnp.logical_and(
            east_number <= cutoffs[0, 2 * band + inner],
            north_number <= cutoffs[1, 2 * band + inner],
        )
        masks.append(jnp.where(keep, weight, 0.0))
    spectra = spectra * jnp.concatenate(masks * FIELDS, axis=0)
    high, low = split(spectra)
    back = dot(jnp.concatenate([high, low], axis=0), k_back[...])
    back = quarters(back, 8 * PLANES, 384)
    for t in range(TILES):
        first = 128 * (t // PER)
        value = jnp.zeros((8, 128), F32)
        for p in range(PLANES):
            moved = pltpu.roll(
                back[8 * p : 8 * p + 8, first : first + 128], (RX * (p - t % PER)) % 128, 1
            )
            value = jnp.where(inside[p], moved, value)
        s3[t] = value
    send_all(*phase3)

    receive_all(*phase3)

    received = r3[...].reshape(MODES, 128)
    back = quarters(dot(m_back[...], jnp.concatenate(split(received), axis=1)), BANDS * RY, 128)
    s4[...] = back.reshape(BANDS, RY, 128)
    send_all(*phase4)
    for phase in (phase1, phase2, phase3):
        sent_all(*phase)

    @pl.loop(0, GROUPS)
    def _(group):
        edges_sent(0, group)
        edges_sent(1, group)
        tke_copy(group).wait()
        await_edges(1, group)

    receive_all(*phase4)

    columns = []
    for of in range(BANDS):
        high, low = split(r4[of])
        columns.append(jnp.concatenate([high, low, high, jnp.zeros((RY, 128), BF)], axis=0))
    wide = dot(y_back[...], jnp.concatenate(columns, axis=1))
    for of in range(BANDS):
        modes[of] = wide[:NY, of * 128 : (of + 1) * 128]
    for group in range(GROUPS):
        first = 2 * group * 128
        outer_modes[group] = (
            wide[NY:, first : first + 128] * own_slot[0]
            + wide[NY:, first + 128 : first + 256] * own_slot[1]
        )

    def across(table, value):
        high, low = split(value)
        return lax.dot_general(
            table,
            jnp.concatenate([high, low, high], axis=1),
            (((1,), (1,)), ((), ())),
            preferred_element_type=F32,
        )

    inside_x = [jnp.where(flag[0], third, 0.0) for flag in has]
    inside_y = jnp.where(
        low_lane, jnp.where(has[0][1], third, 0.0), jnp.where(has[1][1], third, 0.0)
    )

    def second_finish(f, plane, at, chunk, value):
        q2[plane, PAD + at : PAD + at + chunk, :] = q0[
            plane, PAD + at : PAD + at + chunk, :
        ] + 0.5 * (value + force[plane, at : at + chunk, :])

    @pl.loop(0, GROUPS)
    def _(group):
        outer = across(x_shared[...], outer_modes[group])
        pairs = modes[pl.ds(2 * group, 2)].reshape(2 * NY, 128)
        smooth_pairs = across(x_back[...], pairs)
        for pair in range(2):
            smooth_part = smooth_pairs[:, pair * NY : (pair + 1) * NY]
            for f in range(FIELDS):
                for inner in range(2):
                    plane = f * LEV + group * GLEV + 2 * pair + inner
                    slot = f * GLEV + 2 * pair + inner
                    p = 2 * f + inner
                    nudge = smooth_part[p * NX : (p + 1) * NX]
                    if f < 2:
                        force[plane] = nudge + drag[plane]
                    else:
                        force[plane] = nudge
                    q1[plane, PAD : PAD + NX, :] = partial[plane] + third * nudge
                    for side, into in ((0, PAD - 3), (1, PAD + NX)):
                        first = PLANES * NX + 8 * p + 4 * side
                        q1[plane, into : into + 3, :] = xr[
                            1, side, group, slot, 0:3, :
                        ] + smooth_part[first : first + 3] * inside_x[side]
        y_halo[...] = merged_halo(1, group) + outer * inside_y

        advance(group, q1, second_finish)
        pack_edges(2, group, interior(q2))
        send_edges(2, group)

    def third_finish(f, plane, at, chunk, value):
        result[plane, at : at + chunk, :] = q0[plane, PAD + at : PAD + at + chunk, :] + (
            value + force[plane, at : at + chunk, :]
        )

    def out_copy(f, group):
        rows = pl.ds(group * GLEV, GLEV)
        into = (east_out, north_out, theta_out)[f]
        return pltpu.make_async_copy(
            result.at[pl.ds(f * LEV + group * GLEV, GLEV)], into.at[rows], out_sem.at[f, group]
        )

    @pl.loop(0, GROUPS)
    def _(group):
        await_edges(2, group)
        fill_pads(2, group, q2)
        y_halo[...] = merged_halo(2, group)
        advance(group, q2, third_finish)
        for f in range(FIELDS):
            out_copy(f, group).start()

    sent_all(*phase4)

    @pl.loop(0, GROUPS)
    def _(group):
        edges_sent(2, group)
        for f in range(FIELDS):
            out_copy(f, group).wait()


PARTS = 2


def deliver(*refs):
    sources, results, held, in_sems, out_sems = refs[:4], refs[4:8], refs[8], refs[9], refs[10]
    inward, outward = [], []
    for j in range(PARTS):
        rows = pl.ds(j * (LEV // PARTS), LEV // PARTS)
        for i in range(4):
            inward.append(
                pltpu.make_async_copy(sources[i].at[rows], held.at[i, rows], in_sems.at[i, j])
            )
            outward.append(
                pltpu.make_async_copy(held.at[i, rows], results[i].at[rows], out_sems.at[i, j])
            )
    for copy in inward:
        copy.start()
    for first, second in zip(inward, outward):
        first.wait()
        second.start()
    for copy in outward:
        copy.wait()


def shards(*arguments):
    tables = [jnp.asarray(table) for table in make_tables()]
    field = jax.ShapeDtypeStruct((LEV, NX, NY), F32)
    anywhere = pl.BlockSpec(memory_space=pl.ANY)
    smem = pl.BlockSpec(memory_space=pltpu.SMEM)
    padded = pltpu.VMEM((FIELDS * LEV, NX + 2 * PAD, NY), F32)
    planes = pltpu.VMEM((FIELDS * LEV, NX, NY), F32)
    dma = pltpu.SemaphoreType.DMA
    outcome = pl.pallas_call(
        kernel,
        out_shape=(field,) * 4,
        in_specs=[anywhere] * 9 + [smem] * 3 + [anywhere] * TABLES,
        out_specs=(anywhere,) * 4,
        scratch_shapes=[pltpu.VMEM(table.shape, table.dtype) for table in tables]
        + [
            padded,
            padded,
            padded,
            planes,
            pltpu.VMEM((LEV, NX, NY), F32),
            pltpu.VMEM((NX, NY), jnp.int32),
            pltpu.VMEM((NX, NY), jnp.int32),
            planes,
            pltpu.VMEM((2 * LEV, NX, NY), F32),
            planes,
            planes,
            pltpu.VMEM((SLOTS * NX, 2 * NY), F32),
            pltpu.VMEM((NX, 128), F32),
            pltpu.VMEM((3, 2, GROUPS, SLOTS, 4, 128), F32),
            pltpu.VMEM((3, 2, GROUPS, SLOTS, 4, 128), F32),
            pltpu.VMEM((3, GROUPS, NX, 128), F32),
            pltpu.VMEM((3, 2, GROUPS, NX, 128), F32),
            pltpu.VMEM((BANDS, RY, 128), F32),
            pltpu.VMEM((BANDS, RY, 128), F32),
            pltpu.VMEM((TILES, 8, 128), F32),
            pltpu.VMEM((TILES, 8, 128), F32),
            pltpu.VMEM((TILES, 8, 128), F32),
            pltpu.VMEM((TILES, 8, 128), F32),
            pltpu.VMEM((BANDS, RY, 128), F32),
            pltpu.VMEM((BANDS, RY, 128), F32),
            pltpu.VMEM((BANDS, NY, 128), F32),
            pltpu.VMEM((GROUPS, NY, 128), F32),
            pltpu.VMEM((SLOTS * NX, 4 * NY), BF),
            dma((9, GROUPS)),
            dma((TABLES,)),
            dma((4, GROUPS)),
            dma((3, 2, GROUPS)),
            dma((3, 2, GROUPS)),
            dma((3, 2, GROUPS)),
            dma((3, 2, GROUPS)),
            dma((BANDS,)),
            dma((BANDS,)),
            dma((TILES,)),
            dma((TILES,)),
            dma((TILES,)),
            dma((TILES,)),
            dma((BANDS,)),
            dma((BANDS,)),
        ],
        compiler_params=pltpu.CompilerParams(
            collective_id=0, has_side_effects=True, vmem_limit_bytes=61 * 1024 * 1024
        ),
        cost_estimate=pl.CostEstimate(
            flops=10**9, bytes_accessed=6 * 2**20, transcendentals=LEV * NX * NY
        ),
        name="step",
    )(*arguments, *tables)
    return pl.pallas_call(
        deliver,
        out_shape=(field,) * 4,
        in_specs=[anywhere] * 4,
        out_specs=(anywhere,) * 4,
        scratch_shapes=[
            pltpu.VMEM((4, LEV, NX, NY), F32),
            dma((4, PARTS)),
            dma((4, PARTS)),
        ],
        compiler_params=pltpu.CompilerParams(vmem_limit_bytes=61 * 1024 * 1024),
        name="deliver",
    )(*outcome)


def solution(mesh):
    field = P(None, "tile", "band")
    column = P("tile", "band")
    in_specs = (field,) * 7 + (column,) * 2 + (P(),) * 3
    return jax.shard_map(
        shards, mesh=mesh, in_specs=in_specs, out_specs=(field,) * 4, check_vma=False
    )
```
